32 devices in a mesh: lon: 16 (over z, x, core), lat: 2 (over y).
Axes of the slice: x: 2, y: 2, z: 4, core: 2. Of those that a mesh axis runs over, the one named last changes fastest.
Arguments:
- fields: bfloat16 [32, 2880, 640], P('lat', 'lon'), may hold values from -6 to 6
- owner_slot: int32 [32], replicated, may hold values from 0 to 31, as said below
- widths: int32 [32], replicated, may hold values from 90 to 360, as said below
- tap_weights: bfloat16 [32, 2880], replicated, may hold values from -0.21875 to 0.21875
Outputs:
- filtered: bfloat16 [32, 2880, 640], P('lat', 'lon')
The draws below stay inside these ranges and needn't reach their ends.
Inputs may be any that keep to these rules, and one draw needn't show every extreme that they name: `owner_slot`: a permutation of the 32 rows; the 16 rows of each band of 16 rows are sent to every band of positions in equal numbers. `widths`: some row has the largest and some row the smallest value.
All inputs are finite; a program needn't handle non-finite values.
Results may differ from the reference program's by a relative error of at most 0.001.
Values may be sent and summed in bfloat16 or wider, within the bound.
No kernel may reach another device: no remote copies, remote signals or barrier semaphores. Data moves between devices by JAX's collectives and lax.ppermute only.
A program may use at most 128 MiB of HBM per device.

```python
import jax
import jax.numpy as jnp
from jax import lax

NLON = 2880
CH = 640
LAT_DEV = 16
NLAT = 32


def draw_owner_slot(key, part):
    key = jax.random.fold_in(key, 11)
    bands = NLAT // LAT_DEV
    share = LAT_DEV // bands
    key_a, key_b = jax.random.split(key)
    perms = jax.vmap(lambda k: jax.random.permutation(k, LAT_DEV))(jax.random.split(key_a, bands))
    mixes = jax.vmap(lambda k: jax.random.permutation(k, LAT_DEV))(jax.random.split(key_b, bands))
    target = perms // share
    before = jnp.arange(bands, dtype=jnp.int32)[:, None] * share + perms % share
    within = mixes[target, before]
    return (target * LAT_DEV + within).reshape(-1).astype(jnp.int32)


def draw_widths(key, part):
    key = jax.random.fold_in(key, 13)
    key_a, key_b, key_c = jax.random.split(key, 3)
    lowest = NLON // 32
    highest = NLON // 8
    result = jax.random.randint(key_a, (NLAT,), lowest, highest + 1)
    first = jax.random.randint(key_b, (), 0, NLAT)
    second = (first + 1 + jax.random.randint(key_c, (), 0, NLAT - 1)) % NLAT
    result = result.at[first].set(highest).at[second].set(lowest)
    return result.astype(jnp.int32)


def level_of(stream_key, dims, shards, low, high):
    def one(axis_at, shards_of):
        draws = jax.random.uniform(jax.random.fold_in(jax.random.fold_in(stream_key, 6), axis_at), (shards_of,), jnp.float32, low / len(shards), high / len(shards))
        return jnp.repeat(jnp.exp(draws), dims[axis_at] // shards_of).reshape((-1,) + (1,) * (len(dims) - axis_at - 1))

    gain = one(*shards[0])
    for cut in shards[1:]:
        gain = gain * one(*cut)
    return gain


def noise(key, extent, deviation, limit, cuts=(), held_as=jnp.bfloat16):
    level = level_of(key, extent, cuts, -0.22, 0.18) if cuts else 1.0
    drawn = jax.random.normal(key, extent, jnp.float32) * deviation * level
    return jnp.minimum(jnp.maximum(drawn, -limit), limit).astype(held_as)


def setup_inputs(seed: int = 0) -> dict:
    splits = jax.random.split(jax.random.key(seed), 5)
    fields = noise(splits[0], (NLAT, NLON, CH), 1.0, 6.0, ((0, 2), (1, 16)))
    owner_slot = draw_owner_slot(jax.random.fold_in(splits[4], 71), 0)
    widths = draw_widths(jax.random.fold_in(splits[4], 71), 0)
    tap_weights = noise(splits[3], (NLAT, NLON), (NLON // 4) ** -0.5, 0.21875)
    return dict(fields=fields, owner_slot=owner_slot, widths=widths, tap_weights=tap_weights)


def reference(fields, owner_slot, widths, tap_weights):
    circle = fields.shape[1]
    offset = jnp.arange(circle, dtype=jnp.int32)
    distance = jnp.minimum(offset, circle - offset)
    active = jnp.where(distance[None, :] <= widths[:, None], tap_weights.astype(jnp.float32), jnp.zeros((), jnp.float32))

    def filter_row(pair):
        panel, weights = pair
        values = panel.astype(jnp.float32)
        spectrum = jnp.fft.rfft(values, axis=0)
        transfer = jnp.conj(jnp.fft.rfft(weights))
        convolved = jnp.fft.irfft(transfer[:, None] * spectrum, n=circle, axis=0)
        return (values + convolved).astype(jnp.bfloat16)

    smoothed = lax.map(filter_row, (fields, active))
    inverse = jnp.argsort(owner_slot).astype(jnp.int32)
    return smoothed[inverse]
```

```python
import functools

import jax
import jax.numpy as jnp
from jax import lax
from jax.experimental import pallas as pl
from jax.experimental.pallas import tpu as pltpu
from jax.sharding import PartitionSpec as P

VMEM_LIMIT = 48 * 1024 * 1024


def up_to(value, multiple):
    return -(-value // multiple) * multiple


def shift_by(x, axis, by):
    count = lax.axis_size(axis)
    return lax.ppermute(x, axis, [(i, (i + by) % count) for i in range(count)])


def split_kernel(chunks, lat_dev, slot_ref, band_ref, fields_ref, rows_ref, slots_ref, *rest):
    outs, (home_ref, sems) = rest[:-2], rest[-2:]
    band = band_ref[0]
    half = lat_dev // 2
    stay, leave, come = jnp.int32(0), jnp.int32(half), jnp.int32(half)
    for j in range(lat_dev):
        here = band * lat_dev + j
        there = (1 - band) * lat_dev + j
        stays = slot_ref[here] // lat_dev == band
        home_ref[jnp.where(stays, stay, leave)] = j
        one = stays.astype(jnp.int32)

        @pl.when(stays)
        def _():
            rows_ref[stay] = here
            slots_ref[stay] = slot_ref[here] % lat_dev

        comes = slot_ref[there] // lat_dev == band

        @pl.when(comes)
        def _():
            rows_ref[come] = there
            slots_ref[come] = slot_ref[there] % lat_dev

        stay, leave, come = stay + one, leave + 1 - one, come + comes.astype(jnp.int32)
    copies = []
    at = 0
    for out, count in zip(outs, chunks):
        for i in range(count):
            copies.append(pltpu.make_async_copy(fields_ref.at[home_ref[at]], out.at[i], sems.at[at]))
            copies[-1].start()
            at += 1
    for copy in copies:
        copy.wait()


def split_rows(fields, owner_slot, band, chunks):
    lat_dev, lon_dev, channels = fields.shape
    smem = pl.BlockSpec(memory_space=pltpu.SMEM)
    anywhere = pl.BlockSpec(memory_space=pl.ANY)
    ints = jax.ShapeDtypeStruct((lat_dev,), jnp.int32)
    outs = [jax.ShapeDtypeStruct((n, lon_dev, channels), fields.dtype) for n in chunks]
    return pl.pallas_call(
        functools.partial(split_kernel, chunks, lat_dev),
        out_shape=[ints, ints] + outs,
        in_specs=[smem, smem, anywhere],
        out_specs=[smem, smem] + [anywhere] * len(outs),
        scratch_shapes=[pltpu.SMEM((lat_dev,), jnp.int32), pltpu.SemaphoreType.DMA((lat_dev,))],
        cost_estimate=pl.CostEstimate(flops=0, bytes_accessed=4 * fields.size, transcendentals=0),
        name="split_rows",
    )(owner_slot, jnp.reshape(band, (1,)).astype(jnp.int32), fields)


def tap_windows(widths, tap_weights, lon_dev, reach):
    circle = tap_weights.shape[1]
    offset = jnp.arange(circle, dtype=jnp.int32)
    distance = jnp.minimum(offset, circle - offset)
    active = jnp.where(
        distance[None, :] <= widths[:, None],
        tap_weights.astype(jnp.float32),
        jnp.zeros((), jnp.float32),
    )
    behind = (reach + 1) * lon_dev
    line = jnp.concatenate([active[:, circle - behind :], active[:, :behind]], axis=1)
    lanes = up_to(2 * lon_dev, 128)
    return jnp.stack(
        [
            jnp.pad(line[:, s * lon_dev : (s + 2) * lon_dev], ((0, 0), (0, lanes - 2 * lon_dev)))
            for s in range(2 * reach + 1)
        ],
        axis=1,
    )


def filter_kernel(groups, rows_ref, slots_ref, sector_ref, *refs):
    out_ref = refs[-1]
    win_ref, own_ref = refs[0], refs[1]
    lon_dev, channels = own_ref.shape[1:]
    lanes = win_ref.shape[2]
    step = min(up_to(lon_dev, 16), 96)
    tall = up_to(lon_dev, step)

    def term(group, ref):
        taps = win_ref[0, pl.ds(sector_ref[group], 1), :]
        bands = []
        for start in range(0, tall, step):
            band = jnp.broadcast_to(taps, (step, lanes))
            band = pltpu.roll(band, (lanes - lon_dev + start) % lanes, 1)
            band = pltpu.roll(band, 0, 1, stride=1, stride_axis=0)
            bands.append(band[:, :lon_dev].astype(jnp.bfloat16))
        taps = jnp.concatenate(bands, axis=0)
        return jnp.dot(taps, ref[0], preferred_element_type=jnp.float32)[:lon_dev]

    total = own_ref[0].astype(jnp.float32)
    at = 1
    for group, size in enumerate(groups):
        if size == 1:
            total += term(group, refs[at])
        else:
            first, second = refs[at], refs[at + 1]
            total += lax.cond(
                sector_ref[len(groups)] == 0,
                lambda: term(group, first),
                lambda: term(group, second),
            )
        at += size
    out_ref[0] = total.astype(out_ref.dtype)


def filter_rows(rows, slots, sectors, windows, groups, before, base, lat_dev):
    own = groups[0][0]
    count, lon_dev, channels = own.shape
    arrays = [a for group in groups for a in group]
    row_spec = pl.BlockSpec((1, lon_dev, channels), lambda i, rows, slots, sectors: (i, 0, 0))
    win_spec = pl.BlockSpec((1,) + windows.shape[1:], lambda i, rows, slots, sectors: (rows[base + i], 0, 0))
    out_spec = pl.BlockSpec((1, lon_dev, channels), lambda i, rows, slots, sectors: (slots[base + i], 0, 0))
    in_specs = [win_spec] + [row_spec] * len(arrays)
    operands = [windows] + arrays
    aliases = {}
    kernel = functools.partial(filter_kernel, tuple(len(g) for g in groups))
    if before is not None:
        in_specs = [pl.BlockSpec(memory_space=pl.ANY)] + in_specs
        operands = [before] + operands
        aliases = {3: 0}
        inner = kernel
        kernel = lambda rows_ref, slots_ref, sector_ref, before_ref, *refs: inner(
            rows_ref, slots_ref, sector_ref, *refs
        )
    return pl.pallas_call(
        kernel,
        out_shape=jax.ShapeDtypeStruct((lat_dev, lon_dev, channels), own.dtype),
        grid_spec=pltpu.PrefetchScalarGridSpec(
            num_scalar_prefetch=3,
            grid=(count,),
            in_specs=in_specs,
            out_specs=out_spec,
        ),
        input_output_aliases=aliases,
        compiler_params=pltpu.CompilerParams(vmem_limit_bytes=VMEM_LIMIT),
        cost_estimate=pl.CostEstimate(
            flops=2 * count * len(groups) * up_to(lon_dev, 256) ** 2 * up_to(channels, 256),
            bytes_accessed=2 * (len(arrays) + 1) * own.size,
            transcendentals=0,
        ),
        name="filter_rows",
    )(rows, slots, sectors, *operands)


def chip_aware(fields, owner_slot, widths, tap_weights):
    lat_dev, lon_dev, channels = fields.shape
    n_lon = lax.axis_size("lon")
    at = lax.axis_index("lon")
    band = lax.axis_index("lat")
    core, x = at % 2, at // 2 % 2
    half = lat_dev // 2
    stay_chunks = (4, 4)
    come_chunks = (4, 4)
    chunks = stay_chunks + come_chunks
    split = split_rows(fields, owner_slot, band, chunks)
    rows, slots, own = split[0], split[1], list(split[2:])
    for i in range(len(stay_chunks), len(chunks)):
        own[i] = lax.ppermute(own[i], "lat", [(0, 1), (1, 0)])
    windows = tap_windows(widths, tap_weights, lon_dev, 2)
    sectors = jnp.stack(
        [
            jnp.int32(2),
            jnp.where(core == 0, 3, 1),
            jnp.where(x == 0, 4, 0),
            jnp.where(x == 0, 0, 4),
            jnp.where(core == 0, 1, 3),
            (x == core).astype(jnp.int32),
        ]
    ).astype(jnp.int32)
    across_core = [(i, i ^ 1) for i in range(n_lon)]
    across_x = [(i, i ^ 2) for i in range(n_lon)]
    across_z = [(i, (i + (4 if i // 2 % 2 == 0 else -4)) % n_lon) for i in range(n_lon)]
    second_x = [(i, i ^ 1) for i in range(n_lon) if i // 2 % 2 == i % 2]
    second_z = [(i, i ^ 1) for i in range(n_lon) if i // 2 % 2 != i % 2]
    out = None
    base = 0
    for part in own:
        beside = lax.ppermute(part, "lon", across_core)
        by_x = lax.ppermute(part, "lon", across_x)
        by_z = lax.ppermute(by_x, "lon", across_z)
        from_x = lax.ppermute(by_x, "lon", second_x)
        from_z = lax.ppermute(by_z, "lon", second_z)
        groups = [(part,), (beside,), (by_x,), (by_z,), (from_x, from_z)]
        out = filter_rows(rows, slots, sectors, windows, groups, out, base, lat_dev)
        base += part.shape[0]
    return out


def any_mesh(fields, owner_slot, widths, tap_weights):
    lat_dev, lon_dev, channels = fields.shape
    n_lon = lax.axis_size("lon")
    n_lat = lax.axis_size("lat")
    reach = n_lon // 8
    band = lax.axis_index("lat")
    dest_band = owner_slot // lat_dev
    home_rows = band * lat_dev + jnp.arange(lat_dev, dtype=jnp.int32)
    ordering = jnp.argsort(dest_band[home_rows], stable=True)
    rows = jnp.argsort((dest_band != band).astype(jnp.int32), stable=True)[:lat_dev].astype(jnp.int32)
    slots = (owner_slot[rows] % lat_dev).astype(jnp.int32)
    outgoing = fields[ordering].reshape(n_lat, lat_dev // n_lat, lon_dev, channels)
    incoming = lax.all_to_all(outgoing, "lat", split_axis=0, concat_axis=0, tiled=True)
    own = incoming.reshape(lat_dev, lon_dev, channels)
    windows = tap_windows(widths, tap_weights, lon_dev, reach)
    groups, order = [(own,)], [reach]
    ahead = behind = own
    for step in range(1, reach + 1):
        ahead = shift_by(ahead, "lon", -1)
        behind = shift_by(behind, "lon", 1)
        groups += [(ahead,), (behind,)]
        order += [reach + step, reach - step]
    sectors = jnp.array(order + [0], jnp.int32)
    return filter_rows(rows, slots, sectors, windows, groups, None, 0, lat_dev)


def solution(mesh):
    in_specs = (P("lat", "lon", None), P(), P(), P())
    out_specs = P("lat", "lon", None)
    body = chip_aware if (mesh.shape["lon"], mesh.shape["lat"]) == (16, 2) else any_mesh
    return jax.shard_map(body, mesh=mesh, in_specs=in_specs, out_specs=out_specs, check_vma=False)
```

```python
import functools

import jax
import jax.numpy as jnp
from jax import lax
from jax.experimental import pallas as pl
from jax.experimental.pallas import tpu as pltpu
from jax.sharding import PartitionSpec as P

VMEM_LIMIT = 48 * 1024 * 1024
SMEM_SPEC = pl.BlockSpec(memory_space=pltpu.SMEM)
STAY = (2, 2)
COME = (2, 2)


def up_to(value, multiple):
    return -(-value // multiple) * multiple


def shift_by(x, axis, by):
    count = lax.axis_size(axis)
    return lax.ppermute(x, axis, [(i, (i + by) % count) for i in range(count)])


def tap_windows(widths, tap_weights, lon_dev, reach):
    circle = tap_weights.shape[1]
    offset = jnp.arange(circle, dtype=jnp.int32)
    distance = jnp.minimum(offset, circle - offset)
    active = jnp.where(
        distance[None, :] <= widths[:, None],
        tap_weights.astype(jnp.float32),
        jnp.zeros((), jnp.float32),
    )
    behind = (reach + 1) * lon_dev
    line = jnp.concatenate([active[:, circle - behind :], active[:, :behind]], axis=1)
    lanes = up_to(2 * lon_dev, 128)
    return jnp.stack(
        [
            jnp.pad(line[:, s * lon_dev : (s + 2) * lon_dev], ((0, 0), (0, lanes - 2 * lon_dev)))
            for s in range(2 * reach + 1)
        ],
        axis=1,
    )


def toeplitz(taps, lon_dev, width):
    lanes = taps.shape[1]
    step = min(up_to(lon_dev, 16), 96)
    bands = []
    for start in range(0, up_to(lon_dev, step), step):
        band = jnp.broadcast_to(taps, (step, lanes))
        band = pltpu.roll(band, (lanes - lon_dev + start) % lanes, 1)
        band = pltpu.roll(band, 0, 1, stride=1, stride_axis=0)
        bands.append(band[:, :width].astype(jnp.bfloat16))
    return jnp.concatenate(bands, axis=0)


def take_kernel(chunks, lat_dev, lon_dev, block, slot_ref, place_ref, fields_ref, *refs):
    outs = refs[: len(chunks)]
    rows_ref, slots_ref, home_ref, take_ref = refs[len(chunks) :]
    half, quarter = lat_dev // 2, lat_dev // 4

    @pl.when(pl.program_id(0) == 0)
    def _():
        band, core = place_ref[0], place_ref[1]

        def at(n):
            mine = n // quarter == core
            return n % quarter + jnp.where(mine, 0, quarter)

        stay, leave, come = jnp.int32(0), jnp.int32(0), jnp.int32(0)
        for j in range(lat_dev):
            here = band * lat_dev + j
            there = (1 - band) * lat_dev + j
            stays = slot_ref[here] // lat_dev == band
            comes = slot_ref[there] // lat_dev == band
            home_ref[jnp.where(stays, at(stay), half + at(leave))] = jnp.int32(j)

            @pl.when(stays)
            def _():
                spot = at(stay)
                spot = spot + jnp.where(spot >= quarter, quarter, 0)
                rows_ref[spot] = here
                slots_ref[spot] = slot_ref[here] % lat_dev

            @pl.when(comes)
            def _():
                spot = at(come)
                spot = spot + jnp.where(spot >= quarter, half, quarter)
                rows_ref[spot] = there
                slots_ref[spot] = slot_ref[there] % lat_dev

            stay = stay + stays.astype(jnp.int32)
            leave = leave + 1 - stays.astype(jnp.int32)
            come = come + comes.astype(jnp.int32)
        lon_out = lax.broadcasted_iota(jnp.int32, (block, block * lat_dev), 0)
        column = lax.broadcasted_iota(jnp.int32, (block, block * lat_dev), 1)
        for place in range(lat_dev):
            wanted = lon_out * lat_dev + home_ref[place]
            take_ref[pl.ds(place * block, block), :] = jnp.where(column == wanted, 1.0, 0.0).astype(jnp.bfloat16)

    channels = fields_ref.shape[2]
    lon = pl.program_id(0) * block + lax.broadcasted_iota(jnp.int32, (block * lat_dev, channels), 0) // lat_dev
    panel = fields_ref[...].reshape(block * lat_dev, channels)
    panel = jnp.where(lon < lon_dev, panel.astype(jnp.float32), 0.0).astype(jnp.bfloat16)
    taken = jnp.dot(take_ref[...], panel, preferred_element_type=jnp.float32).astype(jnp.bfloat16)
    place = 0
    for out, count in zip(outs, chunks):
        out[...] = taken[place * block : (place + count) * block].reshape(count, block, channels)
        place += count


def take_rows(fields, owner_slot, place, chunks):
    lon_dev, lat_dev, channels = fields.shape
    block = 16
    padded = up_to(lon_dev, 8)
    ints = jax.ShapeDtypeStruct((lat_dev,), jnp.int32)
    result = pl.pallas_call(
        functools.partial(take_kernel, chunks, lat_dev, lon_dev, block),
        out_shape=[jax.ShapeDtypeStruct((n, padded, channels), fields.dtype) for n in chunks] + [ints, ints],
        grid=(pl.cdiv(lon_dev, block),),
        in_specs=[SMEM_SPEC, SMEM_SPEC, pl.BlockSpec((block, lat_dev, channels), lambda i: (i, 0, 0))],
        out_specs=[pl.BlockSpec((n, block, channels), lambda i: (0, i, 0)) for n in chunks] + [SMEM_SPEC, SMEM_SPEC],
        scratch_shapes=[
            pltpu.SMEM((lat_dev,), jnp.int32),
            pltpu.VMEM((block * lat_dev, block * lat_dev), jnp.bfloat16),
        ],
        compiler_params=pltpu.CompilerParams(vmem_limit_bytes=VMEM_LIMIT),
        cost_estimate=pl.CostEstimate(
            flops=2 * fields.size * block * lat_dev, bytes_accessed=4 * fields.size, transcendentals=0
        ),
        name="take_rows",
    )(owner_slot, place, fields)
    return result[:-2], result[-2], result[-1]


def put_kernel(counts, lat_dev, padded, block, slots_ref, *refs):
    ins, (out_ref, put_ref) = refs[:-2], refs[-2:]

    @pl.when(pl.program_id(0) == 0)
    def _():
        row = lax.broadcasted_iota(jnp.int32, (block * lat_dev, block), 0)
        lon_in = lax.broadcasted_iota(jnp.int32, (block * lat_dev, block), 1)
        strips = []
        for place in range(lat_dev):
            wanted = lon_in * lat_dev + slots_ref[place]
            strips.append(jnp.where(row == wanted, 1.0, 0.0))
        put_ref[...] = jnp.concatenate(strips, axis=1).astype(jnp.bfloat16)

    channels = out_ref.shape[2]
    panel = jnp.concatenate([r[...].reshape(n * block, channels) for r, n in zip(ins, counts)], axis=0)
    lon = lax.broadcasted_iota(jnp.int32, (block * lat_dev, channels), 0) % block + pl.program_id(0) * block
    panel = jnp.where(lon < padded, panel.astype(jnp.float32), 0.0).astype(jnp.bfloat16)
    spread = jnp.dot(put_ref[...], panel, preferred_element_type=jnp.float32).astype(jnp.bfloat16)
    out_ref[...] = spread.reshape(block, lat_dev, channels)


def put_rows(panels, slots, lon_dev, lat_dev):
    padded, channels = panels[0].shape[1:]
    block = 16
    counts = tuple(p.shape[0] for p in panels)
    return pl.pallas_call(
        functools.partial(put_kernel, counts, lat_dev, padded, block),
        out_shape=jax.ShapeDtypeStruct((lon_dev, lat_dev, channels), panels[0].dtype),
        grid=(pl.cdiv(lon_dev, block),),
        in_specs=[SMEM_SPEC] + [pl.BlockSpec((n, block, channels), lambda i: (0, i, 0)) for n in counts],
        out_specs=pl.BlockSpec((block, lat_dev, channels), lambda i: (i, 0, 0)),
        scratch_shapes=[pltpu.VMEM((block * lat_dev, block * lat_dev), jnp.bfloat16)],
        compiler_params=pltpu.CompilerParams(vmem_limit_bytes=VMEM_LIMIT),
        cost_estimate=pl.CostEstimate(
            flops=2 * lon_dev * lat_dev * channels * block * lat_dev,
            bytes_accessed=4 * lon_dev * lat_dev * channels,
            transcendentals=0,
        ),
        name="put_rows",
    )(slots, *panels)


def pair_kernel(lon_dev, rows_ref, sign_ref, win_ref, own, other, x_own, x_other, z_own, z_other,
                out_own, out_other, block_ref, total_ref):
    padded, channels = own.shape[1:]
    for s in range(5):
        block_ref[s] = toeplitz(win_ref[0, s : s + 1, :], lon_dev, padded)
    side, along = sign_ref[0], sign_ref[1]

    def times(offset, panel):
        return jnp.dot(block_ref[2 + offset], panel, preferred_element_type=jnp.float32)[:padded]

    def both(first, second):
        return jnp.concatenate([first[0], second[0]], axis=1)

    here = both(own, other)
    total = here.astype(jnp.float32) + times(0, here)
    total += times(2 * along, both(x_own, x_other))
    total += times(-2 * along, both(z_own, z_other))
    total += jnp.concatenate([times(side, other[0]), times(-side, own[0])], axis=1)
    total_ref[...] = total

    @pl.when(side == along)
    def _():
        total_ref[...] += jnp.concatenate([times(-along, z_other[0]), times(along, x_own[0])], axis=1)

    @pl.when(side != along)
    def _():
        total_ref[...] += jnp.concatenate([times(along, x_other[0]), times(-along, z_own[0])], axis=1)

    out_own[0] = total_ref[:, :channels].astype(out_own.dtype)
    out_other[0] = total_ref[:, channels:].astype(out_other.dtype)


def filter_pair(rows, signs, windows, panels, base, lon_dev):
    count, padded, channels = panels[0].shape
    row_spec = pl.BlockSpec((1, padded, channels), lambda i, rows, signs: (i, 0, 0))
    win_spec = pl.BlockSpec((1,) + windows.shape[1:], lambda i, rows, signs: (rows[base + i], 0, 0))
    out = jax.ShapeDtypeStruct((count, padded, channels), panels[0].dtype)
    tall = up_to(lon_dev, 96)
    return pl.pallas_call(
        functools.partial(pair_kernel, lon_dev),
        out_shape=[out, out],
        grid_spec=pltpu.PrefetchScalarGridSpec(
            num_scalar_prefetch=2,
            grid=(count,),
            in_specs=[win_spec] + [row_spec] * len(panels),
            out_specs=[row_spec, row_spec],
            scratch_shapes=[
                pltpu.VMEM((5, tall, padded), jnp.bfloat16),
                pltpu.VMEM((padded, 2 * channels), jnp.float32),
            ],
        ),
        compiler_params=pltpu.CompilerParams(vmem_limit_bytes=VMEM_LIMIT),
        cost_estimate=pl.CostEstimate(
            flops=2 * count * 10 * 256 * 256 * 768,
            bytes_accessed=2 * 8 * panels[0].size,
            transcendentals=0,
        ),
        name="filter_pair",
    )(rows, signs, windows, *panels)


def chip_aware(fields, owner_slot, widths, tap_weights):
    lat_dev, lon_dev, channels = fields.shape
    n_lon = lax.axis_size("lon")
    at = lax.axis_index("lon")
    band = lax.axis_index("lat")
    core, x = at % 2, at // 2 % 2
    place = jnp.stack([band, core]).astype(jnp.int32)
    signs = jnp.stack([1 - 2 * core, 1 - 2 * x]).astype(jnp.int32)
    chunks = STAY + STAY + COME + COME
    taken, rows, slots = take_rows(jnp.transpose(fields, (1, 0, 2)), owner_slot, place, chunks)
    n_stay, n_come = len(STAY), len(COME)
    keep, give = taken[:n_stay], taken[n_stay : 2 * n_stay]
    straight, cross = taken[2 * n_stay : 2 * n_stay + n_come], taken[2 * n_stay + n_come :]

    across_core = [(i, i ^ 1) for i in range(n_lon)]
    across_x = [(i, i ^ 2) for i in range(n_lon)]
    across_z = [(i, (i + (4 if i // 2 % 2 == 0 else -4)) % n_lon) for i in range(n_lon)]
    across_y = [(i, i ^ 1) for i in range(2 * n_lon)]
    across_both = [(i, i ^ 3) for i in range(2 * n_lon)]

    own = list(keep)
    other = [lax.ppermute(g, "lon", across_core) for g in give]
    own += [lax.ppermute(s, ("lon", "lat"), across_y) for s in straight]
    other += [lax.ppermute(s, ("lon", "lat"), across_both) for s in cross]
    windows = tap_windows(widths, tap_weights, lon_dev, 2)
    mine, theirs = [], []
    base = 0
    for part in zip(own, other):
        by_x = [lax.ppermute(p, "lon", across_x) for p in part]
        by_z = [lax.ppermute(p, "lon", across_z) for p in by_x]
        out_own, out_other = filter_pair(rows, signs, windows, list(part) + by_x + by_z, base, lon_dev)
        mine.append(out_own)
        theirs.append(lax.ppermute(out_other, "lon", across_core))
        base += part[0].shape[0]
    out = put_rows(mine + theirs, slots, lon_dev, lat_dev)
    return jnp.transpose(out, (1, 0, 2))


def filter_kernel(rows_ref, slots_ref, sector_ref, win_ref, *refs):
    ins, out_ref = refs[:-1], refs[-1]
    lon_dev, channels = out_ref.shape[1:]
    total = ins[0][0].astype(jnp.float32)
    for group, ref in enumerate(ins):
        block = toeplitz(win_ref[0, pl.ds(sector_ref[group], 1), :], lon_dev, lon_dev)
        total += jnp.dot(block, ref[0], preferred_element_type=jnp.float32)[:lon_dev]
    out_ref[0] = total.astype(out_ref.dtype)


def filter_rows(rows, slots, sectors, windows, arrays):
    lat_dev, lon_dev, channels = arrays[0].shape
    row_spec = pl.BlockSpec((1, lon_dev, channels), lambda i, rows, slots, sectors: (i, 0, 0))
    win_spec = pl.BlockSpec((1,) + windows.shape[1:], lambda i, rows, slots, sectors: (rows[i], 0, 0))
    out_spec = pl.BlockSpec((1, lon_dev, channels), lambda i, rows, slots, sectors: (slots[i], 0, 0))
    return pl.pallas_call(
        filter_kernel,
        out_shape=jax.ShapeDtypeStruct(arrays[0].shape, arrays[0].dtype),
        grid_spec=pltpu.PrefetchScalarGridSpec(
            num_scalar_prefetch=3,
            grid=(lat_dev,),
            in_specs=[win_spec] + [row_spec] * len(arrays),
            out_specs=out_spec,
        ),
        compiler_params=pltpu.CompilerParams(vmem_limit_bytes=VMEM_LIMIT),
        name="filter_rows",
    )(rows, slots, sectors, windows, *arrays)


def any_mesh(fields, owner_slot, widths, tap_weights):
    lat_dev, lon_dev, channels = fields.shape
    n_lon = lax.axis_size("lon")
    n_lat = lax.axis_size("lat")
    reach = n_lon // 8
    band = lax.axis_index("lat")
    dest_band = owner_slot // lat_dev
    home_rows = band * lat_dev + jnp.arange(lat_dev, dtype=jnp.int32)
    ordering = jnp.argsort(dest_band[home_rows], stable=True)
    rows = jnp.argsort((dest_band != band).astype(jnp.int32), stable=True)[:lat_dev].astype(jnp.int32)
    slots = (owner_slot[rows] % lat_dev).astype(jnp.int32)
    outgoing = fields[ordering].reshape(n_lat, lat_dev // n_lat, lon_dev, channels)
    incoming = lax.all_to_all(outgoing, "lat", split_axis=0, concat_axis=0, tiled=True)
    own = incoming.reshape(lat_dev, lon_dev, channels)
    windows = tap_windows(widths, tap_weights, lon_dev, reach)
    arrays, order = [own], [reach]
    ahead = behind = own
    for step in range(1, reach + 1):
        ahead = shift_by(ahead, "lon", -1)
        behind = shift_by(behind, "lon", 1)
        arrays += [ahead, behind]
        order += [reach + step, reach - step]
    sectors = jnp.array(order, jnp.int32)
    return filter_rows(rows, slots, sectors, windows, arrays)


def solution(mesh):
    in_specs = (P("lat", "lon", None), P(), P(), P())
    out_specs = P("lat", "lon", None)
    body = chip_aware if (mesh.shape["lon"], mesh.shape["lat"]) == (16, 2) else any_mesh
    return jax.shard_map(body, mesh=mesh, in_specs=in_specs, out_specs=out_specs, check_vma=False)
```

```python
import functools

import jax
import jax.numpy as jnp
from jax import lax
from jax.experimental import pallas as pl
from jax.experimental.pallas import tpu as pltpu
from jax.sharding import PartitionSpec as P

VMEM_LIMIT = 48 * 1024 * 1024
SMEM_SPEC = pl.BlockSpec(memory_space=pltpu.SMEM)
VMEM_SPEC = pl.BlockSpec(memory_space=pltpu.VMEM)
ANY_SPEC = pl.BlockSpec(memory_space=pl.ANY)
STAY = (2, 2)
COME = (2, 2)


def up_to(value, multiple):
    return -(-value // multiple) * multiple


def shift_by(x, axis, by):
    count = lax.axis_size(axis)
    return lax.ppermute(x, axis, [(i, (i + by) % count) for i in range(count)])


def tap_windows(widths, tap_weights, lon_dev, reach):
    circle = tap_weights.shape[1]
    offset = jnp.arange(circle, dtype=jnp.int32)
    distance = jnp.minimum(offset, circle - offset)
    active = jnp.where(
        distance[None, :] <= widths[:, None],
        tap_weights.astype(jnp.float32),
        jnp.zeros((), jnp.float32),
    )
    behind = (reach + 1) * lon_dev
    line = jnp.concatenate([active[:, circle - behind :], active[:, :behind]], axis=1)
    lanes = up_to(2 * lon_dev, 128)
    return jnp.stack(
        [
            jnp.pad(line[:, s * lon_dev : (s + 2) * lon_dev], ((0, 0), (0, lanes - 2 * lon_dev)))
            for s in range(2 * reach + 1)
        ],
        axis=1,
    )


def toeplitz(taps, lon_dev, width):
    lanes = taps.shape[1]
    step = min(up_to(lon_dev, 16), 96)
    bands = []
    for start in range(0, up_to(lon_dev, step), step):
        band = jnp.broadcast_to(taps, (step, lanes))
        band = pltpu.roll(band, (lanes - lon_dev + start) % lanes, 1)
        band = pltpu.roll(band, 0, 1, stride=1, stride_axis=0)
        bands.append(band[:, :width].astype(jnp.bfloat16))
    return jnp.concatenate(bands, axis=0)


def take_kernel(chunks, lat_dev, block, slot_ref, place_ref, fields_ref, *refs):
    outs = refs[: len(chunks)]
    rows_ref, slots_ref, home_ref, take_ref, panel_ref, sems = refs[len(chunks) :]
    lon_dev, _, channels = fields_ref.shape
    half, quarter = lat_dev // 2, lat_dev // 4
    starts = list(range(0, lon_dev, block))
    copies = []
    for n, start in enumerate(starts):
        window = pl.ds(start, min(block, lon_dev - start))
        copies.append(pltpu.make_async_copy(fields_ref.at[window], panel_ref.at[window], sems.at[n]))
        copies[-1].start()

    band, core = place_ref[0], place_ref[1]

    def at(n):
        return n % quarter + jnp.where(n // quarter == core, 0, quarter)

    stay, leave, come = jnp.int32(0), jnp.int32(0), jnp.int32(0)
    for j in range(lat_dev):
        here = band * lat_dev + j
        there = (1 - band) * lat_dev + j
        stays = slot_ref[here] // lat_dev == band
        comes = slot_ref[there] // lat_dev == band
        home_ref[jnp.where(stays, at(stay), half + at(leave))] = jnp.int32(j)

        @pl.when(stays)
        def _():
            spot = at(stay)
            spot = spot + jnp.where(spot >= quarter, quarter, 0)
            rows_ref[spot] = here
            slots_ref[spot] = slot_ref[here] % lat_dev

        @pl.when(comes)
        def _():
            spot = at(come)
            spot = spot + jnp.where(spot >= quarter, half, quarter)
            rows_ref[spot] = there
            slots_ref[spot] = slot_ref[there] % lat_dev

        stay = stay + stays.astype(jnp.int32)
        leave = leave + 1 - stays.astype(jnp.int32)
        come = come + comes.astype(jnp.int32)

    def selector(lon_in, lon_out):
        lon = lax.broadcasted_iota(jnp.int32, (lon_out, lon_in * lat_dev), 0)
        column = lax.broadcasted_iota(jnp.int32, (lon_out, lon_in * lat_dev), 1)
        strips = [jnp.where(column == lon * lat_dev + home_ref[p], 1.0, 0.0) for p in range(lat_dev)]
        return jnp.concatenate(strips, axis=0).astype(jnp.bfloat16)

    take_ref[...] = selector(block, block)
    for n, start in enumerate(starts):
        copies[n].wait()
        lon_in = min(block, lon_dev - start)
        lon_out = min(block, outs[0].shape[1] - start)
        panel = panel_ref[start : start + lon_in].reshape(lon_in * lat_dev, channels)
        take = take_ref[...] if (lon_in, lon_out) == (block, block) else selector(lon_in, lon_out)
        taken = jnp.dot(take, panel, preferred_element_type=jnp.float32).astype(jnp.bfloat16)
        place = 0
        for out, count in zip(outs, chunks):
            for i in range(count):
                out[i, start : start + lon_out, :] = taken[place * lon_out : (place + 1) * lon_out]
                place += 1


def take_rows(fields, owner_slot, place, chunks):
    lon_dev, lat_dev, channels = fields.shape
    block = 16
    padded = up_to(lon_dev, 8)
    ints = jax.ShapeDtypeStruct((lat_dev,), jnp.int32)
    result = pl.pallas_call(
        functools.partial(take_kernel, chunks, lat_dev, block),
        out_shape=[jax.ShapeDtypeStruct((n, padded, channels), fields.dtype) for n in chunks] + [ints, ints],
        in_specs=[SMEM_SPEC, SMEM_SPEC, ANY_SPEC],
        out_specs=[VMEM_SPEC] * len(chunks) + [SMEM_SPEC, SMEM_SPEC],
        scratch_shapes=[
            pltpu.SMEM((lat_dev,), jnp.int32),
            pltpu.VMEM((block * lat_dev, block * lat_dev), jnp.bfloat16),
            pltpu.VMEM(fields.shape, fields.dtype),
            pltpu.SemaphoreType.DMA((pl.cdiv(lon_dev, block),)),
        ],
        compiler_params=pltpu.CompilerParams(vmem_limit_bytes=VMEM_LIMIT),
        cost_estimate=pl.CostEstimate(
            flops=2 * fields.size * block * lat_dev, bytes_accessed=4 * fields.size, transcendentals=0
        ),
        name="take_rows",
    )(owner_slot, place, fields)
    return result[:-2], result[-2], result[-1]


def put_kernel(counts, lat_dev, block, slots_ref, *refs):
    ins, (out_ref, panel_ref, sems) = refs[:-3], refs[-3:]
    lon_dev, _, channels = out_ref.shape

    def selector(lon_in, lon_out):
        shape = (lon_out * lat_dev, lat_dev * lon_in)
        row = lax.broadcasted_iota(jnp.int32, shape, 0)
        column = lax.broadcasted_iota(jnp.int32, (8, lat_dev * lon_in), 1)
        wanted = column % lon_in * lat_dev
        for p in range(lat_dev):
            wanted += jnp.where(column // lon_in == p, slots_ref[p], 0)
        return jnp.where(row == wanted[:1], 1.0, 0.0).astype(jnp.bfloat16)

    whole = selector(block, block)
    copies = []
    for n, start in enumerate(range(0, lon_dev, block)):
        lon_out = min(block, lon_dev - start)
        lon_in = min(block, ins[0].shape[1] - start)
        pieces = [r[i, start : start + lon_in, :] for r, count in zip(ins, counts) for i in range(count)]
        put = whole if (lon_in, lon_out) == (block, block) else selector(lon_in, lon_out)
        spread = jnp.dot(put, jnp.concatenate(pieces, axis=0), preferred_element_type=jnp.float32)
        window = pl.ds(start, lon_out)
        panel_ref[window] = spread.astype(jnp.bfloat16).reshape(lon_out, lat_dev, channels)
        copies.append(pltpu.make_async_copy(panel_ref.at[window], out_ref.at[window], sems.at[n]))
        copies[-1].start()
    for copy in copies:
        copy.wait()


def put_rows(panels, slots, lon_dev, lat_dev):
    padded, channels = panels[0].shape[1:]
    block = 16
    counts = tuple(p.shape[0] for p in panels)
    shape = (lon_dev, lat_dev, channels)
    return pl.pallas_call(
        functools.partial(put_kernel, counts, lat_dev, block),
        out_shape=jax.ShapeDtypeStruct(shape, panels[0].dtype),
        in_specs=[SMEM_SPEC] + [VMEM_SPEC] * len(panels),
        out_specs=ANY_SPEC,
        scratch_shapes=[
            pltpu.VMEM(shape, panels[0].dtype),
            pltpu.SemaphoreType.DMA((pl.cdiv(lon_dev, block),)),
        ],
        compiler_params=pltpu.CompilerParams(vmem_limit_bytes=VMEM_LIMIT),
        cost_estimate=pl.CostEstimate(
            flops=2 * lon_dev * lat_dev * channels * block * lat_dev,
            bytes_accessed=4 * lon_dev * lat_dev * channels,
            transcendentals=0,
        ),
        name="put_rows",
    )(slots, *panels)


def pair_kernel(lon_dev, rows_ref, sign_ref, win_ref, own, other, x_own, x_other, z_own, z_other,
                out_own, out_other, block_ref, total_ref):
    padded, channels = own.shape[1:]
    for s in range(5):
        block_ref[s] = toeplitz(win_ref[0, s : s + 1, :], lon_dev, padded)
    side, along = sign_ref[0], sign_ref[1]

    def times(offset, panel):
        return jnp.dot(block_ref[2 + offset], panel, preferred_element_type=jnp.float32)[:padded]

    def both(first, second):
        return jnp.concatenate([first[0], second[0]], axis=1)

    here = both(own, other)
    total = here.astype(jnp.float32) + times(0, here)
    total += times(2 * along, both(x_own, x_other))
    total += times(-2 * along, both(z_own, z_other))
    total += jnp.concatenate([times(side, other[0]), times(-side, own[0])], axis=1)
    total_ref[...] = total

    @pl.when(side == along)
    def _():
        total_ref[...] += jnp.concatenate([times(-along, z_other[0]), times(along, x_own[0])], axis=1)

    @pl.when(side != along)
    def _():
        total_ref[...] += jnp.concatenate([times(along, x_other[0]), times(-along, z_own[0])], axis=1)

    out_own[0] = total_ref[:, :channels].astype(out_own.dtype)
    out_other[0] = total_ref[:, channels:].astype(out_other.dtype)


def filter_pair(rows, signs, windows, panels, base, lon_dev):
    count, padded, channels = panels[0].shape
    row_spec = pl.BlockSpec((1, padded, channels), lambda i, rows, signs: (i, 0, 0))
    win_spec = pl.BlockSpec((1,) + windows.shape[1:], lambda i, rows, signs: (rows[base + i], 0, 0))
    out = jax.ShapeDtypeStruct((count, padded, channels), panels[0].dtype)
    tall = up_to(lon_dev, 96)
    return pl.pallas_call(
        functools.partial(pair_kernel, lon_dev),
        out_shape=[out, out],
        grid_spec=pltpu.PrefetchScalarGridSpec(
            num_scalar_prefetch=2,
            grid=(count,),
            in_specs=[win_spec] + [row_spec] * len(panels),
            out_specs=[row_spec, row_spec],
            scratch_shapes=[
                pltpu.VMEM((5, tall, padded), jnp.bfloat16),
                pltpu.VMEM((padded, 2 * channels), jnp.float32),
            ],
        ),
        compiler_params=pltpu.CompilerParams(vmem_limit_bytes=VMEM_LIMIT),
        cost_estimate=pl.CostEstimate(
            flops=2 * count * 10 * 256 * 256 * 768,
            bytes_accessed=2 * 8 * panels[0].size,
            transcendentals=0,
        ),
        name="filter_pair",
    )(rows, signs, windows, *panels)


def chip_aware(fields, owner_slot, widths, tap_weights):
    lat_dev, lon_dev, channels = fields.shape
    n_lon = lax.axis_size("lon")
    at = lax.axis_index("lon")
    band = lax.axis_index("lat")
    core, x = at % 2, at // 2 % 2
    place = jnp.stack([band, core]).astype(jnp.int32)
    signs = jnp.stack([1 - 2 * core, 1 - 2 * x]).astype(jnp.int32)
    chunks = STAY + STAY + COME + COME
    taken, rows, slots = take_rows(jnp.transpose(fields, (1, 0, 2)), owner_slot, place, chunks)
    n_stay, n_come = len(STAY), len(COME)
    keep, give = taken[:n_stay], taken[n_stay : 2 * n_stay]
    straight, cross = taken[2 * n_stay : 2 * n_stay + n_come], taken[2 * n_stay + n_come :]

    across_core = [(i, i ^ 1) for i in range(n_lon)]
    across_x = [(i, i ^ 2) for i in range(n_lon)]
    across_z = [(i, (i + (4 if i // 2 % 2 == 0 else -4)) % n_lon) for i in range(n_lon)]
    across_y = [(i, i ^ 1) for i in range(2 * n_lon)]
    across_both = [(i, i ^ 3) for i in range(2 * n_lon)]

    def over_core(p):
        return lax.ppermute(p, "lon", across_core)

    def after(operand, *done):
        return lax.optimization_barrier((operand,) + done)[0]

    own = list(keep)
    other = [over_core(g) for g in give]
    for i in range(n_come):
        s, c = straight[i], cross[i]
        if i > 0:
            s, c = after(s, own[-1]), after(c, other[-1])
        own.append(lax.ppermute(s, ("lon", "lat"), across_y))
        other.append(lax.ppermute(c, ("lon", "lat"), across_both))
    windows = tap_windows(widths, tap_weights, lon_dev, 2)
    parts = [p for pair in zip(own, other) for p in pair]
    by_x, by_z = [], []
    for i, part in enumerate(parts):
        if i >= 2:
            part = after(part, by_x[i - 2], *by_z[max(i - 3, 0) : i - 2])
        by_x.append(lax.ppermute(part, "lon", across_x))
        by_z.append(lax.ppermute(by_x[i], "lon", across_z))
    mine, theirs = [], []
    base = 0
    for i in range(0, len(parts), 2):
        panels = parts[i : i + 2] + by_x[i : i + 2] + by_z[i : i + 2]
        out_own, out_other = filter_pair(rows, signs, windows, panels, base, lon_dev)
        mine.append(out_own)
        theirs.append(over_core(out_other))
        base += out_own.shape[0]
    out = put_rows(mine + theirs, slots, lon_dev, lat_dev)
    return jnp.transpose(out, (1, 0, 2))


def filter_kernel(rows_ref, slots_ref, sector_ref, win_ref, *refs):
    ins, out_ref = refs[:-1], refs[-1]
    lon_dev, channels = out_ref.shape[1:]
    total = ins[0][0].astype(jnp.float32)
    for group, ref in enumerate(ins):
        block = toeplitz(win_ref[0, pl.ds(sector_ref[group], 1), :], lon_dev, lon_dev)
        total += jnp.dot(block, ref[0], preferred_element_type=jnp.float32)[:lon_dev]
    out_ref[0] = total.astype(out_ref.dtype)


def filter_rows(rows, slots, sectors, windows, arrays):
    lat_dev, lon_dev, channels = arrays[0].shape
    row_spec = pl.BlockSpec((1, lon_dev, channels), lambda i, rows, slots, sectors: (i, 0, 0))
    win_spec = pl.BlockSpec((1,) + windows.shape[1:], lambda i, rows, slots, sectors: (rows[i], 0, 0))
    out_spec = pl.BlockSpec((1, lon_dev, channels), lambda i, rows, slots, sectors: (slots[i], 0, 0))
    return pl.pallas_call(
        filter_kernel,
        out_shape=jax.ShapeDtypeStruct(arrays[0].shape, arrays[0].dtype),
        grid_spec=pltpu.PrefetchScalarGridSpec(
            num_scalar_prefetch=3,
            grid=(lat_dev,),
            in_specs=[win_spec] + [row_spec] * len(arrays),
            out_specs=out_spec,
        ),
        compiler_params=pltpu.CompilerParams(vmem_limit_bytes=VMEM_LIMIT),
        name="filter_rows",
    )(rows, slots, sectors, windows, *arrays)


def any_mesh(fields, owner_slot, widths, tap_weights):
    lat_dev, lon_dev, channels = fields.shape
    n_lon = lax.axis_size("lon")
    n_lat = lax.axis_size("lat")
    reach = n_lon // 8
    band = lax.axis_index("lat")
    dest_band = owner_slot // lat_dev
    home_rows = band * lat_dev + jnp.arange(lat_dev, dtype=jnp.int32)
    ordering = jnp.argsort(dest_band[home_rows], stable=True)
    rows = jnp.argsort((dest_band != band).astype(jnp.int32), stable=True)[:lat_dev].astype(jnp.int32)
    slots = (owner_slot[rows] % lat_dev).astype(jnp.int32)
    outgoing = fields[ordering].reshape(n_lat, lat_dev // n_lat, lon_dev, channels)
    incoming = lax.all_to_all(outgoing, "lat", split_axis=0, concat_axis=0, tiled=True)
    own = incoming.reshape(lat_dev, lon_dev, channels)
    windows = tap_windows(widths, tap_weights, lon_dev, reach)
    arrays, order = [own], [reach]
    ahead = behind = own
    for step in range(1, reach + 1):
        ahead = shift_by(ahead, "lon", -1)
        behind = shift_by(behind, "lon", 1)
        arrays += [ahead, behind]
        order += [reach + step, reach - step]
    sectors = jnp.array(order, jnp.int32)
    return filter_rows(rows, slots, sectors, windows, arrays)


def solution(mesh):
    in_specs = (P("lat", "lon", None), P(), P(), P())
    out_specs = P("lat", "lon", None)
    body = chip_aware if (mesh.shape["lon"], mesh.shape["lat"]) == (16, 2) else any_mesh
    return jax.shard_map(body, mesh=mesh, in_specs=in_specs, out_specs=out_specs, check_vma=False)
```

```python
import functools

import jax
import jax.numpy as jnp
from jax import lax
from jax.experimental import pallas as pl
from jax.experimental.pallas import tpu as pltpu
from jax.sharding import PartitionSpec as P

VMEM_LIMIT = 16 * 1024 * 1024
SMEM_SPEC = pl.BlockSpec(memory_space=pltpu.SMEM)
VMEM_SPEC = pl.BlockSpec(memory_space=pltpu.VMEM)
HBM_SPEC = pl.BlockSpec(memory_space=pltpu.HBM)
STAY = (2, 2)
COME = (2, 2)


def up_to(value, multiple):
    return -(-value // multiple) * multiple


def shift_by(x, axis, by):
    count = lax.axis_size(axis)
    return lax.ppermute(x, axis, [(i, (i + by) % count) for i in range(count)])


def tap_windows(widths, tap_weights, lon_dev, reach):
    circle = tap_weights.shape[1]
    offset = jnp.arange(circle, dtype=jnp.int32)
    distance = jnp.minimum(offset, circle - offset)
    active = jnp.where(
        distance[None, :] <= widths[:, None],
        tap_weights.astype(jnp.float32),
        jnp.zeros((), jnp.float32),
    )
    behind = (reach + 1) * lon_dev
    line = jnp.concatenate([active[:, circle - behind :], active[:, :behind]], axis=1)
    lanes = up_to(2 * lon_dev, 128)
    return jnp.stack(
        [
            jnp.pad(line[:, s * lon_dev : (s + 2) * lon_dev], ((0, 0), (0, lanes - 2 * lon_dev)))
            for s in range(2 * reach + 1)
        ],
        axis=1,
    )


def toeplitz(taps, lon_dev, width):
    lanes = taps.shape[1]
    step = min(up_to(lon_dev, 16), 96)
    bands = []
    for start in range(0, up_to(lon_dev, step), step):
        band = jnp.broadcast_to(taps, (step, lanes))
        band = pltpu.roll(band, (lanes - lon_dev + start) % lanes, 1)
        band = pltpu.roll(band, 0, 1, stride=1, stride_axis=0)
        bands.append(band[:, :width].astype(jnp.bfloat16))
    return jnp.concatenate(bands, axis=0)


def take_kernel(chunks, lat_dev, block, slot_ref, place_ref, fields_ref, *refs):
    outs = refs[: len(chunks)]
    rows_ref, slots_ref, home_ref, take_ref = refs[len(chunks) :]
    lon_dev, _, channels = fields_ref.shape
    half, quarter = lat_dev // 2, lat_dev // 4
    starts = list(range(0, lon_dev, block))
    band, core = place_ref[0], place_ref[1]

    def at(n):
        return n % quarter + jnp.where(n // quarter == core, 0, quarter)

    stay, leave, come = jnp.int32(0), jnp.int32(0), jnp.int32(0)
    for j in range(lat_dev):
        here = band * lat_dev + j
        there = (1 - band) * lat_dev + j
        stays = slot_ref[here] // lat_dev == band
        comes = slot_ref[there] // lat_dev == band
        home_ref[jnp.where(stays, at(stay), half + at(leave))] = jnp.int32(j)

        @pl.when(stays)
        def _():
            spot = at(stay)
            spot = spot + jnp.where(spot >= quarter, quarter, 0)
            rows_ref[spot] = here
            slots_ref[spot] = slot_ref[here] % lat_dev

        @pl.when(comes)
        def _():
            spot = at(come)
            spot = spot + jnp.where(spot >= quarter, half, quarter)
            rows_ref[spot] = there
            slots_ref[spot] = slot_ref[there] % lat_dev

        stay = stay + stays.astype(jnp.int32)
        leave = leave + 1 - stays.astype(jnp.int32)
        come = come + comes.astype(jnp.int32)

    def selector(lon_in, lon_out):
        lon = lax.broadcasted_iota(jnp.int32, (lon_out, lon_in * lat_dev), 0)
        column = lax.broadcasted_iota(jnp.int32, (lon_out, lon_in * lat_dev), 1)
        strips = [jnp.where(column == lon * lat_dev + home_ref[p], 1.0, 0.0) for p in range(lat_dev)]
        return jnp.concatenate(strips, axis=0).astype(jnp.bfloat16)

    take_ref[...] = selector(block, block)
    for start in starts:
        lon_in = min(block, lon_dev - start)
        lon_out = min(block, outs[0].shape[1] - start)
        panel = fields_ref[start : start + lon_in].reshape(lon_in * lat_dev, channels)
        take = take_ref[...] if (lon_in, lon_out) == (block, block) else selector(lon_in, lon_out)
        taken = jnp.dot(take, panel, preferred_element_type=jnp.float32).astype(jnp.bfloat16)
        place = 0
        for out, count in zip(outs, chunks):
            for i in range(count):
                out[i, start : start + lon_out, :] = taken[place * lon_out : (place + 1) * lon_out]
                place += 1


def take_rows(fields, owner_slot, place, chunks):
    lon_dev, lat_dev, channels = fields.shape
    block = 16
    padded = up_to(lon_dev, 8)
    ints = jax.ShapeDtypeStruct((lat_dev,), jnp.int32)
    result = pl.pallas_call(
        functools.partial(take_kernel, chunks, lat_dev, block),
        out_shape=[jax.ShapeDtypeStruct((n, padded, channels), fields.dtype) for n in chunks] + [ints, ints],
        in_specs=[SMEM_SPEC, SMEM_SPEC, VMEM_SPEC],
        out_specs=[VMEM_SPEC] * len(chunks) + [SMEM_SPEC, SMEM_SPEC],
        scratch_shapes=[
            pltpu.SMEM((lat_dev,), jnp.int32),
            pltpu.VMEM((block * lat_dev, block * lat_dev), jnp.bfloat16),
        ],
        compiler_params=pltpu.CompilerParams(vmem_limit_bytes=VMEM_LIMIT),
        cost_estimate=pl.CostEstimate(
            flops=2 * fields.size * block * lat_dev, bytes_accessed=4 * fields.size, transcendentals=0
        ),
        name="take_rows",
    )(owner_slot, place, fields)
    return result[:-2], result[-2], result[-1]


def put_kernel(counts, lat_dev, block, slots_ref, *refs):
    ins, (out_ref, panel_ref, sems) = refs[:-3], refs[-3:]
    lon_dev, _, channels = out_ref.shape

    def selector(lon_in, lon_out):
        shape = (lon_out * lat_dev, lat_dev * lon_in)
        row = lax.broadcasted_iota(jnp.int32, shape, 0)
        column = lax.broadcasted_iota(jnp.int32, (8, lat_dev * lon_in), 1)
        wanted = column % lon_in * lat_dev
        for p in range(lat_dev):
            wanted += jnp.where(column // lon_in == p, slots_ref[p], 0)
        return jnp.where(row == wanted[:1], 1.0, 0.0).astype(jnp.bfloat16)

    whole = selector(block, block)
    copies = []
    for n, start in enumerate(range(0, lon_dev, block)):
        lon_out = min(block, lon_dev - start)
        lon_in = min(block, ins[0].shape[1] - start)
        pieces = [r[i, start : start + lon_in, :] for r, count in zip(ins, counts) for i in range(count)]
        put = whole if (lon_in, lon_out) == (block, block) else selector(lon_in, lon_out)
        spread = jnp.dot(put, jnp.concatenate(pieces, axis=0), preferred_element_type=jnp.float32)
        window = pl.ds(start, lon_out)
        panel_ref[window] = spread.astype(jnp.bfloat16).reshape(lon_out, lat_dev, channels)
        copies.append(pltpu.make_async_copy(panel_ref.at[window], out_ref.at[window], sems.at[n]))
        copies[-1].start()
    for copy in copies:
        copy.wait()


def put_rows(panels, slots, lon_dev, lat_dev):
    padded, channels = panels[0].shape[1:]
    block = 16
    counts = tuple(p.shape[0] for p in panels)
    shape = (lon_dev, lat_dev, channels)
    return pl.pallas_call(
        functools.partial(put_kernel, counts, lat_dev, block),
        out_shape=jax.ShapeDtypeStruct(shape, panels[0].dtype),
        in_specs=[SMEM_SPEC] + [VMEM_SPEC] * len(panels),
        out_specs=HBM_SPEC,
        scratch_shapes=[
            pltpu.VMEM(shape, panels[0].dtype),
            pltpu.SemaphoreType.DMA((pl.cdiv(lon_dev, block),)),
        ],
        compiler_params=pltpu.CompilerParams(vmem_limit_bytes=VMEM_LIMIT),
        cost_estimate=pl.CostEstimate(
            flops=2 * lon_dev * lat_dev * channels * block * lat_dev,
            bytes_accessed=4 * lon_dev * lat_dev * channels,
            transcendentals=0,
        ),
        name="put_rows",
    )(slots, *panels)


def pair_kernel(lon_dev, rows_ref, sign_ref, win_ref, own, other, x_own, x_other, z_own, z_other,
                out_own, out_other, block_ref, total_ref):
    padded, channels = own.shape[1:]
    for s in range(5):
        block_ref[s] = toeplitz(win_ref[0, s : s + 1, :], lon_dev, padded)
    side, along = sign_ref[0], sign_ref[1]

    def times(offset, panel):
        return jnp.dot(block_ref[2 + offset], panel, preferred_element_type=jnp.float32)[:padded]

    def both(first, second):
        return jnp.concatenate([first[0], second[0]], axis=1)

    here = both(own, other)
    total = here.astype(jnp.float32) + times(0, here)
    total += times(2 * along, both(x_own, x_other))
    total += times(-2 * along, both(z_own, z_other))
    total += jnp.concatenate([times(side, other[0]), times(-side, own[0])], axis=1)
    total_ref[...] = total

    @pl.when(side == along)
    def _():
        total_ref[...] += jnp.concatenate([times(-along, z_other[0]), times(along, x_own[0])], axis=1)

    @pl.when(side != along)
    def _():
        total_ref[...] += jnp.concatenate([times(along, x_other[0]), times(-along, z_own[0])], axis=1)

    out_own[0] = total_ref[:, :channels].astype(out_own.dtype)
    out_other[0] = total_ref[:, channels:].astype(out_other.dtype)


def filter_pair(rows, signs, windows, panels, base, lon_dev):
    count, padded, channels = panels[0].shape
    row_spec = pl.BlockSpec((1, padded, channels), lambda i, rows, signs: (i, 0, 0))
    win_spec = pl.BlockSpec((1,) + windows.shape[1:], lambda i, rows, signs: (rows[base + i], 0, 0))
    out = jax.ShapeDtypeStruct((count, padded, channels), panels[0].dtype)
    tall = up_to(lon_dev, 96)
    return pl.pallas_call(
        functools.partial(pair_kernel, lon_dev),
        out_shape=[out, out],
        grid_spec=pltpu.PrefetchScalarGridSpec(
            num_scalar_prefetch=2,
            grid=(count,),
            in_specs=[win_spec] + [row_spec] * len(panels),
            out_specs=[row_spec, row_spec],
            scratch_shapes=[
                pltpu.VMEM((5, tall, padded), jnp.bfloat16),
                pltpu.VMEM((padded, 2 * channels), jnp.float32),
            ],
        ),
        compiler_params=pltpu.CompilerParams(vmem_limit_bytes=VMEM_LIMIT),
        cost_estimate=pl.CostEstimate(
            flops=2 * count * 10 * 256 * 256 * 768,
            bytes_accessed=2 * 8 * panels[0].size,
            transcendentals=0,
        ),
        name="filter_pair",
    )(rows, signs, windows, *panels)


def chip_aware(fields, owner_slot, widths, tap_weights):
    lat_dev, lon_dev, channels = fields.shape
    n_lon = lax.axis_size("lon")
    at = lax.axis_index("lon")
    band = lax.axis_index("lat")
    core, x = at % 2, at // 2 % 2
    place = jnp.stack([band, core]).astype(jnp.int32)
    signs = jnp.stack([1 - 2 * core, 1 - 2 * x]).astype(jnp.int32)
    chunks = STAY + STAY + COME + COME
    taken, rows, slots = take_rows(jnp.transpose(fields, (1, 0, 2)), owner_slot, place, chunks)
    n_stay, n_come = len(STAY), len(COME)
    keep, give = taken[:n_stay], taken[n_stay : 2 * n_stay]
    straight, cross = taken[2 * n_stay : 2 * n_stay + n_come], taken[2 * n_stay + n_come :]

    across_core = [(i, i ^ 1) for i in range(n_lon)]
    across_x = [(i, i ^ 2) for i in range(n_lon)]
    across_z = [(i, (i + (4 if i // 2 % 2 == 0 else -4)) % n_lon) for i in range(n_lon)]
    across_y = [(i, i ^ 1) for i in range(2 * n_lon)]
    across_both = [(i, i ^ 3) for i in range(2 * n_lon)]

    def over_core(p):
        return lax.ppermute(p, "lon", across_core)

    def after(operand, *done):
        return lax.optimization_barrier((operand,) + done)[0]

    own = list(keep)
    other = [over_core(g) for g in give]
    over_y = []
    for i in range(n_come):
        for operand, pairs in ((straight[i], across_y), (cross[i], across_both)):
            operand = after(operand, *over_y[-2:-1])
            over_y.append(lax.ppermute(operand, ("lon", "lat"), pairs))
    own += over_y[0::2]
    other += over_y[1::2]
    windows = tap_windows(widths, tap_weights, lon_dev, 2)
    parts = [p for pair in zip(own, other) for p in pair]
    by_x, by_z = [], []
    for i, part in enumerate(parts):
        if i >= 2:
            part = after(part, by_x[i - 2], *over_y[i - 2 : i - 1])
        by_x.append(lax.ppermute(part, "lon", across_x))
        by_z.append(lax.ppermute(after(by_x[i], *by_z[max(i - 2, 0) : max(i - 1, 0)]), "lon", across_z))
    mine, theirs = [], []
    base = 0
    for i in range(0, len(parts), 2):
        panels = parts[i : i + 2] + by_x[i : i + 2] + by_z[i : i + 2]
        out_own, out_other = filter_pair(rows, signs, windows, panels, base, lon_dev)
        mine.append(out_own)
        theirs.append(over_core(out_other))
        base += out_own.shape[0]
    out = put_rows(mine + theirs, slots, lon_dev, lat_dev)
    return jnp.transpose(out, (1, 0, 2))


def filter_kernel(rows_ref, slots_ref, sector_ref, win_ref, *refs):
    ins, out_ref = refs[:-1], refs[-1]
    lon_dev, channels = out_ref.shape[1:]
    total = ins[0][0].astype(jnp.float32)
    for group, ref in enumerate(ins):
        block = toeplitz(win_ref[0, pl.ds(sector_ref[group], 1), :], lon_dev, lon_dev)
        total += jnp.dot(block, ref[0], preferred_element_type=jnp.float32)[:lon_dev]
    out_ref[0] = total.astype(out_ref.dtype)


def filter_rows(rows, slots, sectors, windows, arrays):
    lat_dev, lon_dev, channels = arrays[0].shape
    row_spec = pl.BlockSpec((1, lon_dev, channels), lambda i, rows, slots, sectors: (i, 0, 0))
    win_spec = pl.BlockSpec((1,) + windows.shape[1:], lambda i, rows, slots, sectors: (rows[i], 0, 0))
    out_spec = pl.BlockSpec((1, lon_dev, channels), lambda i, rows, slots, sectors: (slots[i], 0, 0))
    return pl.pallas_call(
        filter_kernel,
        out_shape=jax.ShapeDtypeStruct(arrays[0].shape, arrays[0].dtype),
        grid_spec=pltpu.PrefetchScalarGridSpec(
            num_scalar_prefetch=3,
            grid=(lat_dev,),
            in_specs=[win_spec] + [row_spec] * len(arrays),
            out_specs=out_spec,
        ),
        compiler_params=pltpu.CompilerParams(vmem_limit_bytes=VMEM_LIMIT),
        name="filter_rows",
    )(rows, slots, sectors, windows, *arrays)


def any_mesh(fields, owner_slot, widths, tap_weights):
    lat_dev, lon_dev, channels = fields.shape
    n_lon = lax.axis_size("lon")
    n_lat = lax.axis_size("lat")
    reach = n_lon // 8
    band = lax.axis_index("lat")
    dest_band = owner_slot // lat_dev
    home_rows = band * lat_dev + jnp.arange(lat_dev, dtype=jnp.int32)
    ordering = jnp.argsort(dest_band[home_rows], stable=True)
    rows = jnp.argsort((dest_band != band).astype(jnp.int32), stable=True)[:lat_dev].astype(jnp.int32)
    slots = (owner_slot[rows] % lat_dev).astype(jnp.int32)
    outgoing = fields[ordering].reshape(n_lat, lat_dev // n_lat, lon_dev, channels)
    incoming = lax.all_to_all(outgoing, "lat", split_axis=0, concat_axis=0, tiled=True)
    own = incoming.reshape(lat_dev, lon_dev, channels)
    windows = tap_windows(widths, tap_weights, lon_dev, reach)
    arrays, order = [own], [reach]
    ahead = behind = own
    for step in range(1, reach + 1):
        ahead = shift_by(ahead, "lon", -1)
        behind = shift_by(behind, "lon", 1)
        arrays += [ahead, behind]
        order += [reach + step, reach - step]
    sectors = jnp.array(order, jnp.int32)
    return filter_rows(rows, slots, sectors, windows, arrays)


def solution(mesh):
    in_specs = (P("lat", "lon", None), P(), P(), P())
    out_specs = P("lat", "lon", None)
    body = chip_aware if (mesh.shape["lon"], mesh.shape["lat"]) == (16, 2) else any_mesh
    return jax.shard_map(body, mesh=mesh, in_specs=in_specs, out_specs=out_specs, check_vma=False)
```

```python
import functools

import jax
import jax.numpy as jnp
from jax import lax
from jax.experimental import pallas as pl
from jax.experimental.pallas import tpu as pltpu
from jax.sharding import PartitionSpec as P

VMEM_LIMIT = 16 * 1024 * 1024
SMEM_SPEC = pl.BlockSpec(memory_space=pltpu.SMEM)
VMEM_SPEC = pl.BlockSpec(memory_space=pltpu.VMEM)
HBM_SPEC = pl.BlockSpec(memory_space=pltpu.HBM)
STAY = (1, 1, 2)
COME = (2, 2)
PARTS = [("k", 2), ("c", 2), ("y", 0), ("y", 1), ("y", 2), ("y", 3)]
FILTERS = ((2, 3), (4, 5), (6, 7))
WAITS = {
    ("x", 1): [("p", 1), ("q", 0)],
    ("x", 2): [("x", 0), ("q", 1), ("q", 0)],
    ("x", 3): [("x", 1), ("q", 2)],
    ("x", 4): [("x", 2), ("q", 3), ("q", 2)],
    ("x", 5): [("x", 3), ("z", 0), ("f", 0)],
    ("q", 3): [("q", 1)],
    ("z", 0): [("q", 2)],
    ("z", 1): [("q", 3)],
    ("z", 2): [("z", 0)],
    ("z", 3): [("z", 1)],
    ("z", 4): [("z", 2)],
    ("z", 5): [("z", 3)],
    ("y", 2): [("y", 0)],
    ("y", 3): [("y", 1)],
}
FLOPS = 6


def up_to(value, multiple):
    return -(-value // multiple) * multiple


def shift_by(x, axis, by):
    count = lax.axis_size(axis)
    return lax.ppermute(x, axis, [(i, (i + by) % count) for i in range(count)])


def tap_windows(widths, tap_weights, lon_dev, reach):
    circle = tap_weights.shape[1]
    offset = jnp.arange(circle, dtype=jnp.int32)
    distance = jnp.minimum(offset, circle - offset)
    active = jnp.where(
        distance[None, :] <= widths[:, None],
        tap_weights.astype(jnp.float32),
        jnp.zeros((), jnp.float32),
    )
    behind = (reach + 1) * lon_dev
    line = jnp.concatenate([active[:, circle - behind :], active[:, :behind]], axis=1)
    lanes = up_to(2 * lon_dev, 128)
    return jnp.stack(
        [
            jnp.pad(line[:, s * lon_dev : (s + 2) * lon_dev], ((0, 0), (0, lanes - 2 * lon_dev)))
            for s in range(2 * reach + 1)
        ],
        axis=1,
    )


def toeplitz(taps, lon_dev, width):
    lanes = taps.shape[1]
    step = min(up_to(lon_dev, 16), 96)
    bands = []
    for start in range(0, up_to(lon_dev, step), step):
        band = jnp.broadcast_to(taps, (step, lanes))
        band = pltpu.roll(band, (lanes - lon_dev + start) % lanes, 1)
        band = pltpu.roll(band, 0, 1, stride=1, stride_axis=0)
        bands.append(band[:, :width].astype(jnp.bfloat16))
    return jnp.concatenate(bands, axis=0)


def take_kernel(chunks, lat_dev, block, slot_ref, place_ref, fields_ref, *refs):
    outs = refs[: len(chunks)]
    rows_ref, slots_ref, home_ref, take_ref = refs[len(chunks) :]
    lon_dev, _, channels = fields_ref.shape
    half, quarter = lat_dev // 2, lat_dev // 4
    starts = list(range(0, lon_dev, block))
    band, core, x = place_ref[0], place_ref[1], place_ref[2]

    def at(n):
        within = n % quarter
        return within + jnp.where(n // quarter == core, 0, quarter)

    def traded(n):
        within = n % quarter
        return n + jnp.where(within < 2, (within + x) % 2 - within, 0)

    stay, leave, come = jnp.int32(0), jnp.int32(0), jnp.int32(0)
    for j in range(lat_dev):
        here = band * lat_dev + j
        there = (1 - band) * lat_dev + j
        stays = slot_ref[here] // lat_dev == band
        comes = slot_ref[there] // lat_dev == band
        home_ref[jnp.where(stays, traded(at(stay)), half + at(leave))] = jnp.int32(j)

        @pl.when(stays)
        def _():
            spot = traded(at(stay))
            spot = spot + jnp.where(spot >= quarter, quarter, 0)
            rows_ref[spot] = here
            slots_ref[spot] = slot_ref[here] % lat_dev

        @pl.when(comes)
        def _():
            spot = at(come)
            spot = spot + jnp.where(spot >= quarter, half, quarter)
            rows_ref[spot] = there
            slots_ref[spot] = slot_ref[there] % lat_dev

        stay = stay + stays.astype(jnp.int32)
        leave = leave + 1 - stays.astype(jnp.int32)
        come = come + comes.astype(jnp.int32)

    def selector(lon_in, lon_out):
        lon = lax.broadcasted_iota(jnp.int32, (lon_out, lon_in * lat_dev), 0)
        column = lax.broadcasted_iota(jnp.int32, (lon_out, lon_in * lat_dev), 1)
        strips = [jnp.where(column == lon * lat_dev + home_ref[p], 1.0, 0.0) for p in range(lat_dev)]
        return jnp.concatenate(strips, axis=0).astype(jnp.bfloat16)

    take_ref[...] = selector(block, block)
    for start in starts:
        lon_in = min(block, lon_dev - start)
        lon_out = min(block, outs[0].shape[1] - start)
        panel = fields_ref[start : start + lon_in].reshape(lon_in * lat_dev, channels)
        take = take_ref[...] if (lon_in, lon_out) == (block, block) else selector(lon_in, lon_out)
        taken = jnp.dot(take, panel, preferred_element_type=jnp.float32).astype(jnp.bfloat16)
        place = 0
        for out, count in zip(outs, chunks):
            for i in range(count):
                out[i, start : start + lon_out, :] = taken[place * lon_out : (place + 1) * lon_out]
                place += 1


def take_rows(fields, owner_slot, place, chunks):
    lon_dev, lat_dev, channels = fields.shape
    block = 16
    padded = up_to(lon_dev, 8)
    ints = jax.ShapeDtypeStruct((lat_dev,), jnp.int32)
    result = pl.pallas_call(
        functools.partial(take_kernel, chunks, lat_dev, block),
        out_shape=[jax.ShapeDtypeStruct((n, padded, channels), fields.dtype) for n in chunks] + [ints, ints],
        in_specs=[SMEM_SPEC, SMEM_SPEC, VMEM_SPEC],
        out_specs=[VMEM_SPEC] * len(chunks) + [SMEM_SPEC, SMEM_SPEC],
        scratch_shapes=[
            pltpu.SMEM((lat_dev,), jnp.int32),
            pltpu.VMEM((block * lat_dev, block * lat_dev), jnp.bfloat16),
        ],
        compiler_params=pltpu.CompilerParams(vmem_limit_bytes=VMEM_LIMIT),
        cost_estimate=pl.CostEstimate(
            flops=2 * fields.size * block * lat_dev, bytes_accessed=4 * fields.size, transcendentals=0
        ),
        name="take_rows",
    )(owner_slot, place, fields)
    return result[:-2], result[-2], result[-1]


def put_kernel(counts, lat_dev, block, slots_ref, *refs):
    ins, (out_ref, panel_ref, sems) = refs[:-3], refs[-3:]
    lon_dev, _, channels = out_ref.shape

    def selector(lon_in, lon_out):
        shape = (lon_out * lat_dev, lat_dev * lon_in)
        row = lax.broadcasted_iota(jnp.int32, shape, 0)
        column = lax.broadcasted_iota(jnp.int32, (8, lat_dev * lon_in), 1)
        wanted = column % lon_in * lat_dev
        for p in range(lat_dev):
            wanted += jnp.where(column // lon_in == p, slots_ref[p], 0)
        return jnp.where(row == wanted[:1], 1.0, 0.0).astype(jnp.bfloat16)

    whole = selector(block, block)
    copies = []
    for n, start in enumerate(range(0, lon_dev, block)):
        lon_out = min(block, lon_dev - start)
        lon_in = min(block, ins[0].shape[1] - start)
        pieces = [r[i, start : start + lon_in, :] for r, count in zip(ins, counts) for i in range(count)]
        put = whole if (lon_in, lon_out) == (block, block) else selector(lon_in, lon_out)
        spread = jnp.dot(put, jnp.concatenate(pieces, axis=0), preferred_element_type=jnp.float32)
        window = pl.ds(start, lon_out)
        panel_ref[window] = spread.astype(jnp.bfloat16).reshape(lon_out, lat_dev, channels)
        copies.append(pltpu.make_async_copy(panel_ref.at[window], out_ref.at[window], sems.at[n]))
        copies[-1].start()
    for copy in copies:
        copy.wait()


def put_rows(panels, slots, lon_dev, lat_dev):
    padded, channels = panels[0].shape[1:]
    block = 16
    counts = tuple(p.shape[0] for p in panels)
    shape = (lon_dev, lat_dev, channels)
    return pl.pallas_call(
        functools.partial(put_kernel, counts, lat_dev, block),
        out_shape=jax.ShapeDtypeStruct(shape, panels[0].dtype),
        in_specs=[SMEM_SPEC] + [VMEM_SPEC] * len(panels),
        out_specs=HBM_SPEC,
        scratch_shapes=[
            pltpu.VMEM(shape, panels[0].dtype),
            pltpu.SemaphoreType.DMA((pl.cdiv(lon_dev, block),)),
        ],
        compiler_params=pltpu.CompilerParams(vmem_limit_bytes=VMEM_LIMIT),
        cost_estimate=pl.CostEstimate(
            flops=2 * lon_dev * lat_dev * channels * block * lat_dev,
            bytes_accessed=4 * lon_dev * lat_dev * channels,
            transcendentals=0,
        ),
        name="put_rows",
    )(slots, *panels)


def pair_kernel(lon_dev, base, plan, rows_ref, sign_ref, win_ref, *refs):
    ins, (out_own, out_other, block_ref, total_ref) = refs[:-4], refs[-4:]
    padded, channels = out_own.shape[1:]
    side, along = sign_ref[0], sign_ref[1]
    for n, places in enumerate(plan):
        taps = win_ref[rows_ref[base + n]]
        for s in range(5):
            block_ref[n, s] = toeplitz(taps[s : s + 1], lon_dev, padded)
        own, other, x_own, x_other, z_own, z_other = [ins[array].at[i] for array, i in places]

        def times(offset, panel):
            return jnp.dot(block_ref[n, 2 + offset], panel, preferred_element_type=jnp.float32)[:padded]

        def both(first, second):
            return jnp.concatenate([first[...], second[...]], axis=1)

        here = both(own, other)
        total = here.astype(jnp.float32) + times(0, here)
        total += times(2 * along, both(x_own, x_other))
        total += times(-2 * along, both(z_own, z_other))
        total += jnp.concatenate([times(side, other[...]), times(-side, own[...])], axis=1)
        total_ref[n] = total

        @pl.when(side == along)
        def _():
            total_ref[n] += jnp.concatenate([times(-along, z_other[...]), times(along, x_own[...])], axis=1)

        @pl.when(side != along)
        def _():
            total_ref[n] += jnp.concatenate([times(along, x_other[...]), times(-along, z_own[...])], axis=1)

        out_own[n] = total_ref[n, :, :channels].astype(out_own.dtype)
        out_other[n] = total_ref[n, :, channels:].astype(out_other.dtype)


def filter_pair(rows, signs, windows, places, base, lon_dev):
    arrays = []
    plan = []
    for row in places:
        found = []
        for array, i in row:
            at = next((n for n, a in enumerate(arrays) if a is array), len(arrays))
            if at == len(arrays):
                arrays.append(array)
            found.append((at, i))
        plan.append(tuple(found))
    count = len(plan)
    padded, channels = arrays[0].shape[1:]
    out = jax.ShapeDtypeStruct((count, padded, channels), arrays[0].dtype)
    return pl.pallas_call(
        functools.partial(pair_kernel, lon_dev, base, tuple(plan)),
        out_shape=[out, out],
        in_specs=[SMEM_SPEC, SMEM_SPEC] + [VMEM_SPEC] * (1 + len(arrays)),
        out_specs=[VMEM_SPEC, VMEM_SPEC],
        scratch_shapes=[
            pltpu.VMEM((count, 5, up_to(lon_dev, 96), padded), jnp.bfloat16),
            pltpu.VMEM((count, padded, 2 * channels), jnp.float32),
        ],
        compiler_params=pltpu.CompilerParams(vmem_limit_bytes=VMEM_LIMIT),
        cost_estimate=pl.CostEstimate(
            flops=FLOPS * count * 10 * 256 * 256 * 768,
            bytes_accessed=16 * count * padded * channels,
            transcendentals=0,
        ),
        name="filter_pair",
    )(rows, signs, windows, *arrays)


def chip_aware(fields, owner_slot, widths, tap_weights):
    lat_dev, lon_dev, channels = fields.shape
    n_lon = lax.axis_size("lon")
    at = lax.axis_index("lon")
    band = lax.axis_index("lat")
    core, x = at % 2, at // 2 % 2
    place = jnp.stack([band, core, x]).astype(jnp.int32)
    signs = jnp.stack([1 - 2 * core, 1 - 2 * x]).astype(jnp.int32)
    chunks = STAY + STAY + COME + COME
    taken, rows, slots = take_rows(jnp.transpose(fields, (1, 0, 2)), owner_slot, place, chunks)
    n_stay, n_come = len(STAY), len(COME)
    keep, give = taken[:n_stay], taken[n_stay : 2 * n_stay]
    straight, cross = taken[2 * n_stay : 2 * n_stay + n_come], taken[2 * n_stay + n_come :]

    across_core = [(i, i ^ 1) for i in range(n_lon)]
    across_x = [(i, i ^ 2) for i in range(n_lon)]
    across_x_core = [(i, i ^ 3) for i in range(n_lon)]
    across_z = [(i, (i + (4 if i // 2 % 2 == 0 else -4)) % n_lon) for i in range(n_lon)]
    back_z = [(i, (i + (-4 if i // 2 % 2 == 0 else 4)) % n_lon) for i in range(n_lon)]
    across_y = [(i, i ^ 1) for i in range(2 * n_lon)]
    across_both = [(i, i ^ 3) for i in range(2 * n_lon)]

    windows = tap_windows(widths, tap_weights, lon_dev, 2)
    sizes = STAY + COME
    starts = [sum(sizes[:c]) for c in range(len(sizes))]
    done = {}

    def get(kind, i):
        if (kind, i) in done:
            return done[kind, i]

        def moved(operand, axes, pairs):
            first = [get(*g)[0] if g[0] in "ft" else get(*g) for g in WAITS.get((kind, i), ())]
            if first:
                operand = lax.optimization_barrier((operand, *first))[0]
            return lax.ppermute(operand, axes, pairs)

        if kind == "k":
            result = keep[i]
        elif kind == "c":
            result = moved(give[i], "lon", across_core)
        elif kind == "y":
            operand, pairs = ((straight, across_y), (cross, across_both))[i % 2]
            result = moved(operand[i // 2], ("lon", "lat"), pairs)
        elif kind == "x":
            result = moved(get(*PARTS[i]), "lon", across_x)
        elif kind == "z":
            result = moved(get("x", i), "lon", across_z)
        elif kind == "p":
            operand, pairs = ((keep[1], across_x), (give[1], across_x_core))[i]
            result = moved(operand, "lon", pairs)
        elif kind == "q":
            operand = get(*(("k", 0), ("c", 0), ("p", 0), ("p", 1))[i])
            result = moved(operand, "lon", back_z if i < 2 else across_z)
        elif kind == "t":
            here = [get("k", 0), get("c", 0)]
            beside = [get("p", 0), get("p", 1)]
            if i == 0:
                panels = here + beside + [get("q", 2), get("q", 3)]
            else:
                panels = beside + [get("q", 0), get("q", 1)] + here
            result = filter_pair(rows, signs, windows, [[(p, 0) for p in panels]], 0, lon_dev)
        elif kind == "b":
            operand, pairs = ((get("t", 0)[1], across_core), (get("t", 1)[0], across_x), (get("t", 1)[1], across_x_core))[i]
            result = moved(operand, "lon", pairs)
        elif kind == "f":
            places = []
            for row in FILTERS[i]:
                chunk, index = next((c, row - at) for c, at in enumerate(starts) if at <= row < at + sizes[c])
                if chunk < n_stay:
                    pair = ("k", chunk), ("c", chunk)
                else:
                    pair = ("y", 2 * (chunk - n_stay)), ("y", 2 * (chunk - n_stay) + 1)
                parts = [get(*p) for p in pair]
                parts += [get(axis, PARTS.index(p)) for axis in "xz" for p in pair]
                places.append([(p, index) for p in parts])
            result = filter_pair(rows, signs, windows, places, FILTERS[i][0], lon_dev)
        else:
            result = moved(get("f", i)[1], "lon", across_core)
        done[kind, i] = result
        return result

    mine = [get("t", 0)[0], get("b", 1)] + [get("f", i)[0] for i in range(len(FILTERS))]
    theirs = [get("b", 0), get("b", 2)] + [get("o", i) for i in range(len(FILTERS))]
    out = put_rows(mine + theirs, slots, lon_dev, lat_dev)
    return jnp.transpose(out, (1, 0, 2))


def filter_kernel(rows_ref, slots_ref, sector_ref, win_ref, *refs):
    ins, out_ref = refs[:-1], refs[-1]
    lon_dev, channels = out_ref.shape[1:]
    total = ins[0][0].astype(jnp.float32)
    for group, ref in enumerate(ins):
        block = toeplitz(win_ref[0, pl.ds(sector_ref[group], 1), :], lon_dev, lon_dev)
        total += jnp.dot(block, ref[0], preferred_element_type=jnp.float32)[:lon_dev]
    out_ref[0] = total.astype(out_ref.dtype)


def filter_rows(rows, slots, sectors, windows, arrays):
    lat_dev, lon_dev, channels = arrays[0].shape
    row_spec = pl.BlockSpec((1, lon_dev, channels), lambda i, rows, slots, sectors: (i, 0, 0))
    win_spec = pl.BlockSpec((1,) + windows.shape[1:], lambda i, rows, slots, sectors: (rows[i], 0, 0))
    out_spec = pl.BlockSpec((1, lon_dev, channels), lambda i, rows, slots, sectors: (slots[i], 0, 0))
    return pl.pallas_call(
        filter_kernel,
        out_shape=jax.ShapeDtypeStruct(arrays[0].shape, arrays[0].dtype),
        grid_spec=pltpu.PrefetchScalarGridSpec(
            num_scalar_prefetch=3,
            grid=(lat_dev,),
            in_specs=[win_spec] + [row_spec] * len(arrays),
            out_specs=out_spec,
        ),
        compiler_params=pltpu.CompilerParams(vmem_limit_bytes=VMEM_LIMIT),
        name="filter_rows",
    )(rows, slots, sectors, windows, *arrays)


def any_mesh(fields, owner_slot, widths, tap_weights):
    lat_dev, lon_dev, channels = fields.shape
    n_lon = lax.axis_size("lon")
    n_lat = lax.axis_size("lat")
    reach = n_lon // 8
    band = lax.axis_index("lat")
    dest_band = owner_slot // lat_dev
    home_rows = band * lat_dev + jnp.arange(lat_dev, dtype=jnp.int32)
    ordering = jnp.argsort(dest_band[home_rows], stable=True)
    rows = jnp.argsort((dest_band != band).astype(jnp.int32), stable=True)[:lat_dev].astype(jnp.int32)
    slots = (owner_slot[rows] % lat_dev).astype(jnp.int32)
    outgoing = fields[ordering].reshape(n_lat, lat_dev // n_lat, lon_dev, channels)
    incoming = lax.all_to_all(outgoing, "lat", split_axis=0, concat_axis=0, tiled=True)
    own = incoming.reshape(lat_dev, lon_dev, channels)
    windows = tap_windows(widths, tap_weights, lon_dev, reach)
    arrays, order = [own], [reach]
    ahead = behind = own
    for step in range(1, reach + 1):
        ahead = shift_by(ahead, "lon", -1)
        behind = shift_by(behind, "lon", 1)
        arrays += [ahead, behind]
        order += [reach + step, reach - step]
    sectors = jnp.array(order, jnp.int32)
    return filter_rows(rows, slots, sectors, windows, arrays)


def solution(mesh):
    in_specs = (P("lat", "lon", None), P(), P(), P())
    out_specs = P("lat", "lon", None)
    chips = (mesh.shape["lon"], mesh.shape["lat"]) == (16, 2)

    def body(fields, owner_slot, widths, tap_weights):
        fits = chips and fields.shape[0] == 4 * sum(STAY)
        form = chip_aware if fits else any_mesh
        return form(fields, owner_slot, widths, tap_weights)

    return jax.shard_map(body, mesh=mesh, in_specs=in_specs, out_specs=out_specs, check_vma=False)
```

```python
import functools

import jax
import jax.numpy as jnp
from jax import lax
from jax.experimental import pallas as pl
from jax.experimental.pallas import tpu as pltpu
from jax.sharding import PartitionSpec as P

VMEM_LIMIT = 16 * 1024 * 1024
TAKE_VMEM_LIMIT = 50 * 1024 * 1024
AHEAD = 4
SMEM_SPEC = pl.BlockSpec(memory_space=pltpu.SMEM)
VMEM_SPEC = pl.BlockSpec(memory_space=pltpu.VMEM)
HBM_SPEC = pl.BlockSpec(memory_space=pltpu.HBM)
STAY = (1, 1, 2)
COME = (2, 2)
PARTS = [("k", 2), ("c", 2), ("y", 0), ("y", 1), ("y", 2), ("y", 3)]
FILTERS = ((2, 3), (4, 5), (6, 7))
WAITS = {
    ("x", 1): [("p", 1), ("q", 0)],
    ("x", 2): [("x", 0), ("q", 1), ("q", 0)],
    ("x", 3): [("x", 1), ("q", 2)],
    ("x", 4): [("x", 2), ("q", 3), ("q", 2)],
    ("x", 5): [("x", 3), ("z", 0), ("f", 0)],
    ("q", 3): [("q", 1)],
    ("z", 0): [("q", 2)],
    ("z", 1): [("q", 3)],
    ("z", 2): [("z", 0)],
    ("z", 3): [("z", 1)],
    ("z", 4): [("z", 2)],
    ("z", 5): [("z", 3)],
    ("y", 2): [("y", 0)],
    ("y", 3): [("y", 1)],
}
FLOPS = 6


def up_to(value, multiple):
    return -(-value // multiple) * multiple


def shift_by(x, axis, by):
    count = lax.axis_size(axis)
    return lax.ppermute(x, axis, [(i, (i + by) % count) for i in range(count)])


def tap_lines(widths, tap_weights, lon_dev, reach):
    circle = tap_weights.shape[1]
    behind = (reach + 1) * lon_dev
    line = jnp.concatenate([tap_weights[:, circle - behind :], tap_weights[:, :behind]], axis=1)
    offset = jnp.arange(circle - behind, circle + behind, dtype=jnp.int32) % circle
    distance = jnp.minimum(offset, circle - offset)
    line = jnp.where(distance[None, :] <= widths[:, None], line.astype(jnp.float32), jnp.zeros((), jnp.float32))
    return jnp.pad(line, ((0, 0), (0, up_to(2 * behind, 128) - 2 * behind)))


def toeplitz(line, at, lon_dev, width):
    lanes = up_to(width, 128) + 128
    step = min(up_to(lon_dev, 16), 96)
    bands = []
    for start in range(0, up_to(lon_dev, step), step):
        taps = pltpu.roll(line, line.shape[1] + start - at, 1)
        taps = jnp.concatenate([taps[:, : lanes - 128], taps[:, -128:]], axis=1)[:1]
        band = pltpu.roll(jnp.broadcast_to(taps, (step, lanes)), 0, 1, stride=1, stride_axis=0)
        bands.append(band[:, :width].astype(jnp.bfloat16))
    return jnp.concatenate(bands, axis=0)


def take_kernel(chunks, lat_dev, block, slot_ref, place_ref, fields_ref, *refs):
    outs = refs[: len(chunks)]
    rows_ref, slots_ref, home_ref, take_ref, panel_ref, sems = refs[len(chunks) :]
    lon_dev, _, channels = fields_ref.shape
    half, quarter = lat_dev // 2, lat_dev // 4
    starts = list(range(0, lon_dev, block))
    copies = []
    for n, start in enumerate(starts):
        window = pl.ds(start, min(block, lon_dev - start))
        copies.append(pltpu.make_async_copy(fields_ref.at[window], panel_ref.at[window], sems.at[n]))
    for copy in copies[:AHEAD]:
        copy.start()
    band, core, x = place_ref[0], place_ref[1], place_ref[2]

    def at(n):
        within = n % quarter
        return within + jnp.where(n // quarter == core, 0, quarter)

    def traded(n):
        within = n % quarter
        return n + jnp.where(within < 2, (within + x) % 2 - within, 0)

    stay, leave, come = jnp.int32(0), jnp.int32(0), jnp.int32(0)
    for j in range(lat_dev):
        here = band * lat_dev + j
        there = (1 - band) * lat_dev + j
        stays = slot_ref[here] // lat_dev == band
        comes = slot_ref[there] // lat_dev == band
        home_ref[jnp.where(stays, traded(at(stay)), half + at(leave))] = jnp.int32(j)

        @pl.when(stays)
        def _():
            spot = traded(at(stay))
            spot = spot + jnp.where(spot >= quarter, quarter, 0)
            rows_ref[spot] = here
            slots_ref[spot] = slot_ref[here] % lat_dev

        @pl.when(comes)
        def _():
            spot = at(come)
            spot = spot + jnp.where(spot >= quarter, half, quarter)
            rows_ref[spot] = there
            slots_ref[spot] = slot_ref[there] % lat_dev

        stay = stay + stays.astype(jnp.int32)
        leave = leave + 1 - stays.astype(jnp.int32)
        come = come + comes.astype(jnp.int32)

    def selector(lon_in, lon_out):
        lon = lax.broadcasted_iota(jnp.int32, (lon_out, lon_in * lat_dev), 0)
        column = lax.broadcasted_iota(jnp.int32, (lon_out, lon_in * lat_dev), 1)
        strips = [jnp.where(column == lon * lat_dev + home_ref[p], 1.0, 0.0) for p in range(lat_dev)]
        return jnp.concatenate(strips, axis=0).astype(jnp.bfloat16)

    take_ref[...] = selector(block, block)
    for n, start in enumerate(starts):
        copies[n].wait()
        if n + AHEAD < len(copies):
            copies[n + AHEAD].start()
        lon_in = min(block, lon_dev - start)
        lon_out = min(block, outs[0].shape[1] - start)
        panel = panel_ref[start : start + lon_in].reshape(lon_in * lat_dev, channels)
        take = take_ref[...] if (lon_in, lon_out) == (block, block) else selector(lon_in, lon_out)
        taken = jnp.dot(take, panel, preferred_element_type=jnp.float32).astype(jnp.bfloat16)
        place = 0
        for out, count in zip(outs, chunks):
            for i in range(count):
                out[i, start : start + lon_out, :] = taken[place * lon_out : (place + 1) * lon_out]
                place += 1


def take_rows(fields, owner_slot, place, chunks):
    lon_dev, lat_dev, channels = fields.shape
    block = 16
    padded = up_to(lon_dev, 8)
    ints = jax.ShapeDtypeStruct((lat_dev,), jnp.int32)
    result = pl.pallas_call(
        functools.partial(take_kernel, chunks, lat_dev, block),
        out_shape=[jax.ShapeDtypeStruct((n, padded, channels), fields.dtype) for n in chunks] + [ints, ints],
        in_specs=[SMEM_SPEC, SMEM_SPEC, HBM_SPEC],
        out_specs=[VMEM_SPEC] * len(chunks) + [SMEM_SPEC, SMEM_SPEC],
        scratch_shapes=[
            pltpu.SMEM((lat_dev,), jnp.int32),
            pltpu.VMEM((block * lat_dev, block * lat_dev), jnp.bfloat16),
            pltpu.VMEM(fields.shape, fields.dtype),
            pltpu.SemaphoreType.DMA((pl.cdiv(lon_dev, block),)),
        ],
        compiler_params=pltpu.CompilerParams(vmem_limit_bytes=TAKE_VMEM_LIMIT),
        cost_estimate=pl.CostEstimate(
            flops=2 * fields.size * block * lat_dev, bytes_accessed=4 * fields.size, transcendentals=0
        ),
        name="take_rows",
    )(owner_slot, place, fields)
    return result[:-2], result[-2], result[-1]


def put_kernel(counts, lat_dev, block, slots_ref, *refs):
    ins, (out_ref, panel_ref, sems) = refs[:-3], refs[-3:]
    lon_dev, _, channels = out_ref.shape

    def selector(lon_in, lon_out):
        shape = (lon_out * lat_dev, lat_dev * lon_in)
        row = lax.broadcasted_iota(jnp.int32, shape, 0)
        column = lax.broadcasted_iota(jnp.int32, (8, lat_dev * lon_in), 1)
        wanted = column % lon_in * lat_dev
        for p in range(lat_dev):
            wanted += jnp.where(column // lon_in == p, slots_ref[p], 0)
        return jnp.where(row == wanted[:1], 1.0, 0.0).astype(jnp.bfloat16)

    whole = selector(block, block)
    copies = []
    for n, start in enumerate(range(0, lon_dev, block)):
        lon_out = min(block, lon_dev - start)
        lon_in = min(block, ins[0].shape[1] - start)
        pieces = [r[i, start : start + lon_in, :] for r, count in zip(ins, counts) for i in range(count)]
        put = whole if (lon_in, lon_out) == (block, block) else selector(lon_in, lon_out)
        spread = jnp.dot(put, jnp.concatenate(pieces, axis=0), preferred_element_type=jnp.float32)
        window = pl.ds(start, lon_out)
        panel_ref[window] = spread.astype(jnp.bfloat16).reshape(lon_out, lat_dev, channels)
        copies.append(pltpu.make_async_copy(panel_ref.at[window], out_ref.at[window], sems.at[n]))
        copies[-1].start()
    for copy in copies:
        copy.wait()


def put_rows(panels, slots, lon_dev, lat_dev):
    padded, channels = panels[0].shape[1:]
    block = 16
    counts = tuple(p.shape[0] for p in panels)
    shape = (lon_dev, lat_dev, channels)
    return pl.pallas_call(
        functools.partial(put_kernel, counts, lat_dev, block),
        out_shape=jax.ShapeDtypeStruct(shape, panels[0].dtype),
        in_specs=[SMEM_SPEC] + [VMEM_SPEC] * len(panels),
        out_specs=HBM_SPEC,
        scratch_shapes=[
            pltpu.VMEM(shape, panels[0].dtype),
            pltpu.SemaphoreType.DMA((pl.cdiv(lon_dev, block),)),
        ],
        compiler_params=pltpu.CompilerParams(vmem_limit_bytes=VMEM_LIMIT),
        cost_estimate=pl.CostEstimate(
            flops=2 * lon_dev * lat_dev * channels * block * lat_dev,
            bytes_accessed=4 * lon_dev * lat_dev * channels,
            transcendentals=0,
        ),
        name="put_rows",
    )(slots, *panels)


def pair_kernel(lon_dev, base, plan, phase, rows_ref, sign_ref, *refs):
    count = len(plan)
    side, along = sign_ref[0], sign_ref[1]
    if phase == "late":
        (total_in, block_ref), refs = refs[:2], refs[2:]
    else:
        line_ref, refs = refs[0], refs[1:]
    if phase == "early":
        ins, (total_ref, block_ref) = refs[:-2], refs[-2:]
    elif phase == "late":
        ins, (out_own, out_other, total_ref) = refs[:-3], refs[-3:]
    else:
        ins, (out_own, out_other, total_ref, block_ref) = refs[:-4], refs[-4:]
    padded, channels = ins[0].shape[1:]

    def both(first, second):
        return jnp.concatenate([first[...], second[...]], axis=1)

    for n, places in enumerate(plan):
        panels = [ins[array].at[i] for array, i in places]

        def times(offset, panel):
            return jnp.dot(block_ref[n, 2 + offset], panel, preferred_element_type=jnp.float32)[:padded]

        def add(which, offset, panel):
            lanes = pl.ds(which * channels, channels)
            total_ref[n, :, lanes] += times(offset, panel[...])

        if phase != "late":
            own, other, x_own, x_other = panels[:4]
            line = jnp.broadcast_to(line_ref[pl.ds(rows_ref[base + n], 1), :], (8, line_ref.shape[1]))
            for s in range(5):
                block_ref[n, s] = toeplitz(line, (s + 1) * lon_dev, lon_dev, padded)
            here = both(own, other)
            total = here.astype(jnp.float32) + times(0, here)
            total += times(2 * along, both(x_own, x_other))
            total += jnp.concatenate([times(side, other[...]), times(-side, own[...])], axis=1)
            total_ref[n] = total
            pl.when(side == along)(functools.partial(add, 1, along, x_own))
            pl.when(side != along)(functools.partial(add, 0, along, x_other))
        if phase != "early":
            z_own, z_other = panels[-2:]
            before = total_in[n] if phase == "late" else total_ref[n]
            total_ref[n] = before + times(-2 * along, both(z_own, z_other))
            pl.when(side == along)(functools.partial(add, 0, -along, z_other))
            pl.when(side != along)(functools.partial(add, 1, -along, z_own))
            out_own[n] = total_ref[n, :, :channels].astype(out_own.dtype)
            out_other[n] = total_ref[n, :, channels:].astype(out_other.dtype)


def filter_pair(rows, signs, lines, places, base, lon_dev, phase="whole", early=()):
    arrays = []
    plan = []
    for row in places:
        found = []
        for array, i in row:
            at = next((n for n, a in enumerate(arrays) if a is array), len(arrays))
            if at == len(arrays):
                arrays.append(array)
            found.append((at, i))
        plan.append(tuple(found))
    count = len(plan)
    padded, channels = arrays[0].shape[1:]
    total = (count, padded, 2 * channels), jnp.float32
    block = (count, 5, up_to(lon_dev, 96), padded), jnp.bfloat16
    out = jax.ShapeDtypeStruct((count, padded, channels), arrays[0].dtype)
    first = [lines] if phase != "late" else list(early)
    if phase == "early":
        outs, scratch = [jax.ShapeDtypeStruct(*total), jax.ShapeDtypeStruct(*block)], []
    elif phase == "late":
        outs, scratch = [out, out], [pltpu.VMEM(*total)]
    else:
        outs, scratch = [out, out], [pltpu.VMEM(*total), pltpu.VMEM(*block)]
    weight = {"whole": 10, "early": 7, "late": 3}[phase]
    return pl.pallas_call(
        functools.partial(pair_kernel, lon_dev, base, tuple(plan), phase),
        out_shape=outs,
        in_specs=[SMEM_SPEC, SMEM_SPEC] + [VMEM_SPEC] * (len(first) + len(arrays)),
        out_specs=[VMEM_SPEC] * len(outs),
        scratch_shapes=scratch,
        compiler_params=pltpu.CompilerParams(vmem_limit_bytes=VMEM_LIMIT),
        cost_estimate=pl.CostEstimate(
            flops=FLOPS * count * weight * 256 * 256 * 768,
            bytes_accessed=16 * count * padded * channels,
            transcendentals=0,
        ),
        name="filter_" + phase,
    )(rows, signs, *first, *arrays)


def chip_aware(fields, owner_slot, widths, tap_weights):
    lat_dev, lon_dev, channels = fields.shape
    n_lon = lax.axis_size("lon")
    at = lax.axis_index("lon")
    band = lax.axis_index("lat")
    core, x = at % 2, at // 2 % 2
    place = jnp.stack([band, core, x]).astype(jnp.int32)
    signs = jnp.stack([1 - 2 * core, 1 - 2 * x]).astype(jnp.int32)
    chunks = STAY + STAY + COME + COME
    taken, rows, slots = take_rows(jnp.transpose(fields, (1, 0, 2)), owner_slot, place, chunks)
    n_stay, n_come = len(STAY), len(COME)
    keep, give = taken[:n_stay], taken[n_stay : 2 * n_stay]
    straight, cross = taken[2 * n_stay : 2 * n_stay + n_come], taken[2 * n_stay + n_come :]

    across_core = [(i, i ^ 1) for i in range(n_lon)]
    across_x = [(i, i ^ 2) for i in range(n_lon)]
    across_x_core = [(i, i ^ 3) for i in range(n_lon)]
    across_z = [(i, (i + (4 if i // 2 % 2 == 0 else -4)) % n_lon) for i in range(n_lon)]
    back_z = [(i, (i + (-4 if i // 2 % 2 == 0 else 4)) % n_lon) for i in range(n_lon)]
    across_y = [(i, i ^ 1) for i in range(2 * n_lon)]
    across_both = [(i, i ^ 3) for i in range(2 * n_lon)]

    lines = tap_lines(widths, tap_weights, lon_dev, 2)
    sizes = STAY + COME
    starts = [sum(sizes[:c]) for c in range(len(sizes))]
    done = {}

    def get(kind, i):
        if (kind, i) in done:
            return done[kind, i]

        def moved(operand, axes, pairs):
            first = [get(*g)[0] if g[0] in "ft" else get(*g) for g in WAITS.get((kind, i), ())]
            if first:
                operand = lax.optimization_barrier((operand, *first))[0]
            return lax.ppermute(operand, axes, pairs)

        if kind == "k":
            result = keep[i]
        elif kind == "c":
            result = moved(give[i], "lon", across_core)
        elif kind == "y":
            operand, pairs = ((straight, across_y), (cross, across_both))[i % 2]
            result = moved(operand[i // 2], ("lon", "lat"), pairs)
        elif kind == "x":
            result = moved(get(*PARTS[i]), "lon", across_x)
        elif kind == "z":
            result = moved(get("x", i), "lon", across_z)
        elif kind == "p":
            operand, pairs = ((keep[1], across_x), (give[1], across_x_core))[i]
            result = moved(operand, "lon", pairs)
        elif kind == "q":
            operand = get(*(("k", 0), ("c", 0), ("p", 0), ("p", 1))[i])
            result = moved(operand, "lon", back_z if i < 2 else across_z)
        elif kind == "t":
            here = [get("k", 0), get("c", 0)]
            beside = [get("p", 0), get("p", 1)]
            if i == 0:
                panels = here + beside + [get("q", 2), get("q", 3)]
            else:
                panels = beside + [get("q", 0), get("q", 1)] + here
            result = filter_pair(rows, signs, lines, [[(p, 0) for p in panels]], 0, lon_dev)
        elif kind == "b":
            operand, pairs = ((get("t", 0)[1], across_core), (get("t", 1)[0], across_x), (get("t", 1)[1], across_x_core))[i]
            result = moved(operand, "lon", pairs)
        elif kind == "f":
            places = []
            for row in FILTERS[i]:
                chunk, index = next((c, row - at) for c, at in enumerate(starts) if at <= row < at + sizes[c])
                if chunk < n_stay:
                    pair = ("k", chunk), ("c", chunk)
                else:
                    pair = ("y", 2 * (chunk - n_stay)), ("y", 2 * (chunk - n_stay) + 1)
                parts = [get(*p) for p in pair]
                parts += [get(axis, PARTS.index(p)) for axis in "xz" for p in pair]
                places.append([(p, index) for p in parts])
            base = FILTERS[i][0]
            if i < len(FILTERS) - 1:
                result = filter_pair(rows, signs, lines, places, base, lon_dev)
            else:
                early = filter_pair(rows, signs, lines, [p[:4] for p in places], base, lon_dev, "early")
                result = filter_pair(rows, signs, lines, [p[4:] for p in places], base, lon_dev, "late", early)
        else:
            result = moved(get("f", i)[1], "lon", across_core)
        done[kind, i] = result
        return result

    mine = [get("t", 0)[0], get("b", 1)] + [get("f", i)[0] for i in range(len(FILTERS))]
    theirs = [get("b", 0), get("b", 2)] + [get("o", i) for i in range(len(FILTERS))]
    out = put_rows(mine + theirs, slots, lon_dev, lat_dev)
    return jnp.transpose(out, (1, 0, 2))


def filter_kernel(rows_ref, slots_ref, sector_ref, line_ref, *refs):
    ins, out_ref = refs[:-1], refs[-1]
    lon_dev, channels = out_ref.shape[1:]
    row = rows_ref[pl.program_id(0)]
    line = jnp.broadcast_to(line_ref[pl.ds(row, 1), :], (8, line_ref.shape[1]))
    total = ins[0][0].astype(jnp.float32)
    for group, ref in enumerate(ins):
        block = toeplitz(line, (sector_ref[group] + 1) * lon_dev, lon_dev, lon_dev)
        total += jnp.dot(block, ref[0], preferred_element_type=jnp.float32)[:lon_dev]
    out_ref[0] = total.astype(out_ref.dtype)


def filter_rows(rows, slots, sectors, lines, arrays):
    lat_dev, lon_dev, channels = arrays[0].shape
    row_spec = pl.BlockSpec((1, lon_dev, channels), lambda i, rows, slots, sectors: (i, 0, 0))
    line_spec = pl.BlockSpec(lines.shape, lambda i, rows, slots, sectors: (0, 0))
    out_spec = pl.BlockSpec((1, lon_dev, channels), lambda i, rows, slots, sectors: (slots[i], 0, 0))
    return pl.pallas_call(
        filter_kernel,
        out_shape=jax.ShapeDtypeStruct(arrays[0].shape, arrays[0].dtype),
        grid_spec=pltpu.PrefetchScalarGridSpec(
            num_scalar_prefetch=3,
            grid=(lat_dev,),
            in_specs=[line_spec] + [row_spec] * len(arrays),
            out_specs=out_spec,
        ),
        compiler_params=pltpu.CompilerParams(vmem_limit_bytes=VMEM_LIMIT),
        name="filter_rows",
    )(rows, slots, sectors, lines, *arrays)


def any_mesh(fields, owner_slot, widths, tap_weights):
    lat_dev, lon_dev, channels = fields.shape
    n_lon = lax.axis_size("lon")
    n_lat = lax.axis_size("lat")
    reach = n_lon // 8
    band = lax.axis_index("lat")
    dest_band = owner_slot // lat_dev
    home_rows = band * lat_dev + jnp.arange(lat_dev, dtype=jnp.int32)
    ordering = jnp.argsort(dest_band[home_rows], stable=True)
    rows = jnp.argsort((dest_band != band).astype(jnp.int32), stable=True)[:lat_dev].astype(jnp.int32)
    slots = (owner_slot[rows] % lat_dev).astype(jnp.int32)
    outgoing = fields[ordering].reshape(n_lat, lat_dev // n_lat, lon_dev, channels)
    incoming = lax.all_to_all(outgoing, "lat", split_axis=0, concat_axis=0, tiled=True)
    own = incoming.reshape(lat_dev, lon_dev, channels)
    lines = tap_lines(widths, tap_weights, lon_dev, reach)
    arrays, order = [own], [reach]
    ahead = behind = own
    for step in range(1, reach + 1):
        ahead = shift_by(ahead, "lon", -1)
        behind = shift_by(behind, "lon", 1)
        arrays += [ahead, behind]
        order += [reach + step, reach - step]
    sectors = jnp.array(order, jnp.int32)
    return filter_rows(rows, slots, sectors, lines, arrays)


def solution(mesh):
    in_specs = (P("lat", "lon", None), P(), P(), P())
    out_specs = P("lat", "lon", None)
    chips = (mesh.shape["lon"], mesh.shape["lat"]) == (16, 2)

    def body(fields, owner_slot, widths, tap_weights):
        fits = chips and fields.shape[0] == 4 * sum(STAY)
        form = chip_aware if fits else any_mesh
        return form(fields, owner_slot, widths, tap_weights)

    return jax.shard_map(body, mesh=mesh, in_specs=in_specs, out_specs=out_specs, check_vma=False)
```

```python
import functools

import jax
import jax.numpy as jnp
from jax import lax
from jax.experimental import pallas as pl
from jax.experimental.pallas import tpu as pltpu
from jax.sharding import PartitionSpec as P

VMEM_LIMIT = 16 * 1024 * 1024
SMEM_SPEC = pl.BlockSpec(memory_space=pltpu.SMEM)
VMEM_SPEC = pl.BlockSpec(memory_space=pltpu.VMEM)
HBM_SPEC = pl.BlockSpec(memory_space=pltpu.HBM)
STAY = (1, 1, 2)
COME = (2, 2)
PARTS = [("k", 2), ("c", 2), ("y", 0), ("y", 1), ("y", 2), ("y", 3)]
FILTERS = ((2, 3), (4, 5), (6, 7))
WAITS = {
    ("x", 1): [("q", 0)],
    ("x", 2): [("x", 0), ("q", 1)],
    ("x", 3): [("x", 1), ("q", 2)],
    ("x", 4): [("x", 2), ("q", 3), ("x", 1), ("t", 1)],
    ("x", 5): [("x", 3), ("z", 0), ("f", 0)],
    ("q", 3): [("q", 1)],
    ("z", 0): [("q", 2)],
    ("z", 1): [("q", 3)],
    ("z", 2): [("z", 0)],
    ("z", 3): [("z", 1)],
    ("z", 4): [("z", 2)],
    ("y", 2): [("y", 0)],
    ("y", 3): [("y", 1)],
}
FLOPS = 6


def up_to(value, multiple):
    return -(-value // multiple) * multiple


def shift_by(x, axis, by):
    count = lax.axis_size(axis)
    return lax.ppermute(x, axis, [(i, (i + by) % count) for i in range(count)])


def tap_lines(widths, tap_weights, lon_dev, reach):
    circle = tap_weights.shape[1]
    behind = (reach + 1) * lon_dev
    line = jnp.concatenate([tap_weights[:, circle - behind :], tap_weights[:, :behind]], axis=1)
    offset = jnp.arange(circle - behind, circle + behind, dtype=jnp.int32) % circle
    distance = jnp.minimum(offset, circle - offset)
    line = jnp.where(distance[None, :] <= widths[:, None], line.astype(jnp.float32), jnp.zeros((), jnp.float32))
    return jnp.pad(line, ((0, 0), (0, up_to(2 * behind, 128) - 2 * behind)))


def toeplitz(line, at, lon_dev, width):
    lanes = up_to(width, 128) + 128
    step = min(up_to(lon_dev, 16), 96)
    bands = []
    for start in range(0, up_to(lon_dev, step), step):
        taps = pltpu.roll(line, line.shape[1] + start - at, 1)
        taps = jnp.concatenate([taps[:, : lanes - 128], taps[:, -128:]], axis=1)
        band = pltpu.roll(jnp.concatenate([taps] * (step // 8), axis=0), 0, 1, stride=1, stride_axis=0)
        bands.append(band[:, :width].astype(jnp.bfloat16))
    return jnp.concatenate(bands, axis=0)


def take_kernel(chunks, lat_dev, block, slot_ref, place_ref, fields_ref, *refs):
    outs = refs[: len(chunks)]
    rows_ref, slots_ref, home_ref, take_ref = refs[len(chunks) :]
    lon_dev, _, channels = fields_ref.shape
    half, quarter = lat_dev // 2, lat_dev // 4
    starts = list(range(0, lon_dev, block))
    band, core, x = place_ref[0], place_ref[1], place_ref[2]

    def at(n):
        within = n % quarter
        return within + jnp.where(n // quarter == core, 0, quarter)

    def traded(n):
        within = n % quarter
        return n + jnp.where(within < 2, (within + x) % 2 - within, 0)

    stay, leave, come = jnp.int32(0), jnp.int32(0), jnp.int32(0)
    for j in range(lat_dev):
        here = band * lat_dev + j
        there = (1 - band) * lat_dev + j
        stays = slot_ref[here] // lat_dev == band
        comes = slot_ref[there] // lat_dev == band
        home_ref[jnp.where(stays, traded(at(stay)), half + at(leave))] = jnp.int32(j)

        @pl.when(stays)
        def _():
            spot = traded(at(stay))
            spot = spot + jnp.where(spot >= quarter, quarter, 0)
            rows_ref[spot] = here
            slots_ref[spot] = slot_ref[here] % lat_dev

        @pl.when(comes)
        def _():
            spot = at(come)
            spot = spot + jnp.where(spot >= quarter, half, quarter)
            rows_ref[spot] = there
            slots_ref[spot] = slot_ref[there] % lat_dev

        stay = stay + stays.astype(jnp.int32)
        leave = leave + 1 - stays.astype(jnp.int32)
        come = come + comes.astype(jnp.int32)

    def selector(lon_in, lon_out):
        lon = lax.broadcasted_iota(jnp.int32, (lon_out, lon_in * lat_dev), 0)
        column = lax.broadcasted_iota(jnp.int32, (lon_out, lon_in * lat_dev), 1)
        strips = [jnp.where(column == lon * lat_dev + home_ref[p], 1.0, 0.0) for p in range(lat_dev)]
        return jnp.concatenate(strips, axis=0).astype(jnp.bfloat16)

    take_ref[...] = selector(block, block)
    for start in starts:
        lon_in = min(block, lon_dev - start)
        lon_out = min(block, outs[0].shape[1] - start)
        panel = fields_ref[start : start + lon_in].reshape(lon_in * lat_dev, channels)
        take = take_ref[...] if (lon_in, lon_out) == (block, block) else selector(lon_in, lon_out)
        taken = jnp.dot(take, panel, preferred_element_type=jnp.float32).astype(jnp.bfloat16)
        place = 0
        for out, count in zip(outs, chunks):
            for i in range(count):
                out[i, start : start + lon_out, :] = taken[place * lon_out : (place + 1) * lon_out]
                place += 1


def take_rows(fields, owner_slot, place, chunks):
    lon_dev, lat_dev, channels = fields.shape
    block = 16
    padded = up_to(lon_dev, 8)
    ints = jax.ShapeDtypeStruct((lat_dev,), jnp.int32)
    result = pl.pallas_call(
        functools.partial(take_kernel, chunks, lat_dev, block),
        out_shape=[jax.ShapeDtypeStruct((n, padded, channels), fields.dtype) for n in chunks] + [ints, ints],
        in_specs=[SMEM_SPEC, SMEM_SPEC, VMEM_SPEC],
        out_specs=[VMEM_SPEC] * len(chunks) + [SMEM_SPEC, SMEM_SPEC],
        scratch_shapes=[
            pltpu.SMEM((lat_dev,), jnp.int32),
            pltpu.VMEM((block * lat_dev, block * lat_dev), jnp.bfloat16),
        ],
        compiler_params=pltpu.CompilerParams(vmem_limit_bytes=VMEM_LIMIT),
        cost_estimate=pl.CostEstimate(
            flops=2 * fields.size * block * lat_dev, bytes_accessed=4 * fields.size, transcendentals=0
        ),
        name="take_rows",
    )(owner_slot, place, fields)
    return result[:-2], result[-2], result[-1]


def put_kernel(counts, lat_dev, block, slots_ref, *refs):
    ins, (out_ref, panel_ref, sems) = refs[:-3], refs[-3:]
    lon_dev, _, channels = out_ref.shape

    def selector(lon_in, lon_out):
        shape = (lon_out * lat_dev, lat_dev * lon_in)
        row = lax.broadcasted_iota(jnp.int32, shape, 0)
        column = lax.broadcasted_iota(jnp.int32, (8, lat_dev * lon_in), 1)
        wanted = column % lon_in * lat_dev
        for p in range(lat_dev):
            wanted += jnp.where(column // lon_in == p, slots_ref[p], 0)
        return jnp.where(row == wanted[:1], 1.0, 0.0).astype(jnp.bfloat16)

    whole = selector(block, block)
    copies = []
    for n, start in enumerate(range(0, lon_dev, block)):
        lon_out = min(block, lon_dev - start)
        lon_in = min(block, ins[0].shape[1] - start)
        pieces = [r[i, start : start + lon_in, :] for r, count in zip(ins, counts) for i in range(count)]
        put = whole if (lon_in, lon_out) == (block, block) else selector(lon_in, lon_out)
        spread = jnp.dot(put, jnp.concatenate(pieces, axis=0), preferred_element_type=jnp.float32)
        window = pl.ds(start, lon_out)
        panel_ref[window] = spread.astype(jnp.bfloat16).reshape(lon_out, lat_dev, channels)
        copies.append(pltpu.make_async_copy(panel_ref.at[window], out_ref.at[window], sems.at[n]))
        copies[-1].start()
    for copy in copies:
        copy.wait()


def put_rows(panels, slots, lon_dev, lat_dev):
    padded, channels = panels[0].shape[1:]
    block = 16
    counts = tuple(p.shape[0] for p in panels)
    shape = (lon_dev, lat_dev, channels)
    return pl.pallas_call(
        functools.partial(put_kernel, counts, lat_dev, block),
        out_shape=jax.ShapeDtypeStruct(shape, panels[0].dtype),
        in_specs=[SMEM_SPEC] + [VMEM_SPEC] * len(panels),
        out_specs=HBM_SPEC,
        scratch_shapes=[
            pltpu.VMEM(shape, panels[0].dtype),
            pltpu.SemaphoreType.DMA((pl.cdiv(lon_dev, block),)),
        ],
        compiler_params=pltpu.CompilerParams(vmem_limit_bytes=VMEM_LIMIT),
        cost_estimate=pl.CostEstimate(
            flops=2 * lon_dev * lat_dev * channels * block * lat_dev,
            bytes_accessed=4 * lon_dev * lat_dev * channels,
            transcendentals=0,
        ),
        name="put_rows",
    )(slots, *panels)


def pair_kernel(lon_dev, base, plan, phase, rows_ref, sign_ref, *refs):
    count = len(plan)
    side, along = sign_ref[0], sign_ref[1]
    if phase == "late":
        (total_in, block_ref), refs = refs[:2], refs[2:]
    else:
        line_ref, refs = refs[0], refs[1:]
    if phase == "early":
        ins, (total_ref, block_ref) = refs[:-2], refs[-2:]
    elif phase == "late":
        ins, (out_own, out_other) = refs[:-2], refs[-2:]
    else:
        ins, (out_own, out_other, block_ref) = refs[:-3], refs[-3:]
    padded, channels = ins[0].shape[1:]

    def both(first, second):
        return jnp.concatenate([first[...], second[...]], axis=1)

    for n, places in enumerate(plan):
        panels = [ins[array].at[i] for array, i in places]

        def times(offset, panel):
            return jnp.dot(block_ref[n, 2 + offset], panel, preferred_element_type=jnp.float32)[:padded]

        def halves(first, second):
            return jnp.concatenate([first, second], axis=1)

        nothing = jnp.zeros((padded, channels), jnp.float32)
        same = side == along
        if phase != "late":
            own, other, x_own, x_other = panels[:4]
            line = jnp.broadcast_to(line_ref[pl.ds(rows_ref[base + n], 1), :], (8, line_ref.shape[1]))
            for s in range(5):
                block_ref[n, s] = toeplitz(line, (s + 1) * lon_dev, lon_dev, padded)
            here = both(own, other)
            total = here.astype(jnp.float32) + times(0, here)
            total += times(2 * along, both(x_own, x_other))
            total += jnp.concatenate([times(side, other[...]), times(-side, own[...])], axis=1)
            more = times(along, jnp.where(same, x_own[...], x_other[...]))
            total += halves(jnp.where(same, nothing, more), jnp.where(same, more, nothing))
            if phase == "early":
                total_ref[n] = total
        if phase != "early":
            z_own, z_other = panels[-2:]
            if phase == "late":
                total = total_in[n]
            total += times(-2 * along, both(z_own, z_other))
            more = times(-along, jnp.where(same, z_other[...], z_own[...]))
            total += halves(jnp.where(same, more, nothing), jnp.where(same, nothing, more))
            out_own[n] = total[:, :channels].astype(out_own.dtype)
            out_other[n] = total[:, channels:].astype(out_other.dtype)


def filter_pair(rows, signs, lines, places, base, lon_dev, phase="whole", early=()):
    arrays = []
    plan = []
    for row in places:
        found = []
        for array, i in row:
            at = next((n for n, a in enumerate(arrays) if a is array), len(arrays))
            if at == len(arrays):
                arrays.append(array)
            found.append((at, i))
        plan.append(tuple(found))
    count = len(plan)
    padded, channels = arrays[0].shape[1:]
    total = (count, padded, 2 * channels), jnp.float32
    block = (count, 5, up_to(lon_dev, 96), padded), jnp.bfloat16
    out = jax.ShapeDtypeStruct((count, padded, channels), arrays[0].dtype)
    first = [lines] if phase != "late" else list(early)
    if phase == "early":
        outs, scratch = [jax.ShapeDtypeStruct(*total), jax.ShapeDtypeStruct(*block)], []
    elif phase == "late":
        outs, scratch = [out, out], []
    else:
        outs, scratch = [out, out], [pltpu.VMEM(*block)]
    weight = {"whole": 10, "early": 7, "late": 3}[phase]
    return pl.pallas_call(
        functools.partial(pair_kernel, lon_dev, base, tuple(plan), phase),
        out_shape=outs,
        in_specs=[SMEM_SPEC, SMEM_SPEC] + [VMEM_SPEC] * (len(first) + len(arrays)),
        out_specs=[VMEM_SPEC] * len(outs),
        scratch_shapes=scratch,
        compiler_params=pltpu.CompilerParams(vmem_limit_bytes=VMEM_LIMIT),
        cost_estimate=pl.CostEstimate(
            flops=FLOPS * count * weight * 256 * 256 * 768,
            bytes_accessed=16 * count * padded * channels,
            transcendentals=0,
        ),
        name="filter_" + phase,
    )(rows, signs, *first, *arrays)


def chip_aware(fields, owner_slot, widths, tap_weights):
    lat_dev, lon_dev, channels = fields.shape
    n_lon = lax.axis_size("lon")
    at = lax.axis_index("lon")
    band = lax.axis_index("lat")
    core, x = at % 2, at // 2 % 2
    place = jnp.stack([band, core, x]).astype(jnp.int32)
    signs = jnp.stack([1 - 2 * core, 1 - 2 * x]).astype(jnp.int32)
    chunks = STAY + STAY + COME + COME
    taken, rows, slots = take_rows(jnp.transpose(fields, (1, 0, 2)), owner_slot, place, chunks)
    n_stay, n_come = len(STAY), len(COME)
    keep, give = taken[:n_stay], taken[n_stay : 2 * n_stay]
    straight, cross = taken[2 * n_stay : 2 * n_stay + n_come], taken[2 * n_stay + n_come :]

    across_core = [(i, i ^ 1) for i in range(n_lon)]
    across_x = [(i, i ^ 2) for i in range(n_lon)]
    across_x_core = [(i, i ^ 3) for i in range(n_lon)]
    across_z = [(i, (i + (4 if i // 2 % 2 == 0 else -4)) % n_lon) for i in range(n_lon)]
    back_z = [(i, (i + (-4 if i // 2 % 2 == 0 else 4)) % n_lon) for i in range(n_lon)]
    across_y = [(i, i ^ 1) for i in range(2 * n_lon)]
    across_both = [(i, i ^ 3) for i in range(2 * n_lon)]

    lines = tap_lines(widths, tap_weights, lon_dev, 2)
    sizes = STAY + COME
    starts = [sum(sizes[:c]) for c in range(len(sizes))]
    done = {}

    def get(kind, i):
        if (kind, i) in done:
            return done[kind, i]

        def moved(operand, axes, pairs):
            first = [get(*g)[0] if g[0] in "ft" else get(*g) for g in WAITS.get((kind, i), ())]
            if first:
                operand = lax.optimization_barrier((operand, *first))[0]
            return lax.ppermute(operand, axes, pairs)

        if kind == "k":
            result = keep[i]
        elif kind == "c":
            result = moved(give[i], "lon", across_core)
        elif kind == "y":
            operand, pairs = ((straight, across_y), (cross, across_both))[i % 2]
            result = moved(operand[i // 2], ("lon", "lat"), pairs)
        elif kind == "x":
            result = moved(get(*PARTS[i]), "lon", across_x)
        elif kind == "z":
            result = moved(get("x", i), "lon", across_z)
        elif kind == "p":
            operand, pairs = ((keep[1], across_x), (give[1], across_x_core))[i]
            result = moved(operand, "lon", pairs)
        elif kind == "q":
            operand = get(*(("k", 0), ("c", 0), ("p", 0), ("p", 1))[i])
            result = moved(operand, "lon", back_z if i < 2 else across_z)
        elif kind == "t":
            here = [get("k", 0), get("c", 0)]
            beside = [get("p", 0), get("p", 1)]
            if i == 0:
                panels = here + beside + [get("q", 2), get("q", 3)]
            else:
                panels = beside + [get("q", 0), get("q", 1)] + here
            result = filter_pair(rows, signs, lines, [[(p, 0) for p in panels]], 0, lon_dev)
        elif kind == "b":
            operand, pairs = ((get("t", 0)[1], across_core), (get("t", 1)[0], across_x), (get("t", 1)[1], across_x_core))[i]
            result = moved(operand, "lon", pairs)
        elif kind == "f":
            places = []
            for row in FILTERS[i]:
                chunk, index = next((c, row - at) for c, at in enumerate(starts) if at <= row < at + sizes[c])
                if chunk < n_stay:
                    pair = ("k", chunk), ("c", chunk)
                else:
                    pair = ("y", 2 * (chunk - n_stay)), ("y", 2 * (chunk - n_stay) + 1)
                parts = [get(*p) for p in pair]
                parts += [get(axis, PARTS.index(p)) for axis in "xz" for p in pair]
                places.append([(p, index) for p in parts])
            base = FILTERS[i][0]
            if i < len(FILTERS) - 1:
                result = filter_pair(rows, signs, lines, places, base, lon_dev)
            else:
                early = filter_pair(rows, signs, lines, [p[:4] for p in places], base, lon_dev, "early")
                result = filter_pair(rows, signs, lines, [p[4:] for p in places], base, lon_dev, "late", early)
        else:
            result = moved(get("f", i)[1], "lon", across_core)
        done[kind, i] = result
        return result

    mine = [get("t", 0)[0], get("b", 1)] + [get("f", i)[0] for i in range(len(FILTERS))]
    theirs = [get("b", 0), get("b", 2)] + [get("o", i) for i in range(len(FILTERS))]
    out = put_rows(mine + theirs, slots, lon_dev, lat_dev)
    return jnp.transpose(out, (1, 0, 2))


def filter_kernel(rows_ref, slots_ref, sector_ref, line_ref, *refs):
    ins, out_ref = refs[:-1], refs[-1]
    lon_dev, channels = out_ref.shape[1:]
    row = rows_ref[pl.program_id(0)]
    line = jnp.broadcast_to(line_ref[pl.ds(row, 1), :], (8, line_ref.shape[1]))
    total = ins[0][0].astype(jnp.float32)
    for group, ref in enumerate(ins):
        block = toeplitz(line, (sector_ref[group] + 1) * lon_dev, lon_dev, lon_dev)
        total += jnp.dot(block, ref[0], preferred_element_type=jnp.float32)[:lon_dev]
    out_ref[0] = total.astype(out_ref.dtype)


def filter_rows(rows, slots, sectors, lines, arrays):
    lat_dev, lon_dev, channels = arrays[0].shape
    row_spec = pl.BlockSpec((1, lon_dev, channels), lambda i, rows, slots, sectors: (i, 0, 0))
    line_spec = pl.BlockSpec(lines.shape, lambda i, rows, slots, sectors: (0, 0))
    out_spec = pl.BlockSpec((1, lon_dev, channels), lambda i, rows, slots, sectors: (slots[i], 0, 0))
    return pl.pallas_call(
        filter_kernel,
        out_shape=jax.ShapeDtypeStruct(arrays[0].shape, arrays[0].dtype),
        grid_spec=pltpu.PrefetchScalarGridSpec(
            num_scalar_prefetch=3,
            grid=(lat_dev,),
            in_specs=[line_spec] + [row_spec] * len(arrays),
            out_specs=out_spec,
        ),
        compiler_params=pltpu.CompilerParams(vmem_limit_bytes=VMEM_LIMIT),
        name="filter_rows",
    )(rows, slots, sectors, lines, *arrays)


def any_mesh(fields, owner_slot, widths, tap_weights):
    lat_dev, lon_dev, channels = fields.shape
    n_lon = lax.axis_size("lon")
    n_lat = lax.axis_size("lat")
    reach = n_lon // 8
    band = lax.axis_index("lat")
    dest_band = owner_slot // lat_dev
    home_rows = band * lat_dev + jnp.arange(lat_dev, dtype=jnp.int32)
    ordering = jnp.argsort(dest_band[home_rows], stable=True)
    rows = jnp.argsort((dest_band != band).astype(jnp.int32), stable=True)[:lat_dev].astype(jnp.int32)
    slots = (owner_slot[rows] % lat_dev).astype(jnp.int32)
    outgoing = fields[ordering].reshape(n_lat, lat_dev // n_lat, lon_dev, channels)
    incoming = lax.all_to_all(outgoing, "lat", split_axis=0, concat_axis=0, tiled=True)
    own = incoming.reshape(lat_dev, lon_dev, channels)
    lines = tap_lines(widths, tap_weights, lon_dev, reach)
    arrays, order = [own], [reach]
    ahead = behind = own
    for step in range(1, reach + 1):
        ahead = shift_by(ahead, "lon", -1)
        behind = shift_by(behind, "lon", 1)
        arrays += [ahead, behind]
        order += [reach + step, reach - step]
    sectors = jnp.array(order, jnp.int32)
    return filter_rows(rows, slots, sectors, lines, arrays)


def solution(mesh):
    in_specs = (P("lat", "lon", None), P(), P(), P())
    out_specs = P("lat", "lon", None)
    chips = (mesh.shape["lon"], mesh.shape["lat"]) == (16, 2)

    def body(fields, owner_slot, widths, tap_weights):
        fits = chips and fields.shape[0] == 4 * sum(STAY)
        form = chip_aware if fits else any_mesh
        return form(fields, owner_slot, widths, tap_weights)

    return jax.shard_map(body, mesh=mesh, in_specs=in_specs, out_specs=out_specs, check_vma=False)
```

```python
import functools

import jax
import jax.numpy as jnp
from jax import lax
from jax.experimental import pallas as pl
from jax.experimental.pallas import tpu as pltpu
from jax.sharding import PartitionSpec as P

VMEM_LIMIT = 12 * 1024 * 1024
SMEM_SPEC = pl.BlockSpec(memory_space=pltpu.SMEM)
VMEM_SPEC = pl.BlockSpec(memory_space=pltpu.VMEM)
HBM_SPEC = pl.BlockSpec(memory_space=pltpu.HBM)
STAY = (1, 1, 2)
COME = (2, 2)
PARTS = [("k", 2), ("c", 2), ("y", 0), ("y", 1), ("y", 2), ("y", 3)]
FILTERS = ((2, 3), (4, 5), (6, 7))
WAITS = {
    ("x", 1): [("q", 0)],
    ("x", 2): [("x", 0), ("q", 1)],
    ("x", 3): [("x", 1), ("q", 2)],
    ("x", 4): [("x", 2), ("q", 3), ("x", 1), ("t", 1)],
    ("x", 5): [("x", 3), ("z", 0), ("f", 0)],
    ("q", 3): [("q", 1)],
    ("z", 0): [("q", 2)],
    ("z", 1): [("q", 3)],
    ("z", 2): [("z", 0)],
    ("z", 3): [("z", 1)],
    ("z", 4): [("z", 2)],
    ("y", 2): [("y", 0)],
    ("y", 3): [("y", 1)],
}
FLOPS = 6


def up_to(value, multiple):
    return -(-value // multiple) * multiple


def shift_by(x, axis, by):
    count = lax.axis_size(axis)
    return lax.ppermute(x, axis, [(i, (i + by) % count) for i in range(count)])


def line_kernel(behind, taps_ref, line_ref):
    circle = taps_ref.shape[1]
    rows, lanes = line_ref.shape
    taps = taps_ref[...].astype(jnp.float32)
    pieces = [taps[:, circle - behind :], taps[:, :behind]]
    if lanes > 2 * behind:
        pieces.append(jnp.zeros((rows, lanes - 2 * behind), jnp.float32))
    line_ref[...] = jnp.concatenate(pieces, axis=1)


def tap_lines(tap_weights, behind):
    rows = tap_weights.shape[0]
    lanes = up_to(2 * behind, 128)
    return pl.pallas_call(
        functools.partial(line_kernel, behind),
        out_shape=jax.ShapeDtypeStruct((rows, lanes), jnp.float32),
        in_specs=[VMEM_SPEC],
        out_specs=VMEM_SPEC,
        compiler_params=pltpu.CompilerParams(vmem_limit_bytes=VMEM_LIMIT),
        cost_estimate=pl.CostEstimate(flops=0, bytes_accessed=2 * tap_weights.size, transcendentals=0),
        name="tap_lines",
    )(tap_weights)


def active_line(line_ref, row, width, behind):
    line = jnp.broadcast_to(line_ref[pl.ds(row, 1), :], (8, line_ref.shape[1]))
    distance = jnp.abs(lax.broadcasted_iota(jnp.int32, line.shape, 1) - behind)
    return jnp.where(distance <= width, line, 0.0)


def toeplitz(line, at, lon_dev, width):
    lanes = up_to(width, 128) + 128
    step = min(up_to(lon_dev, 16), 96)
    bands = []
    for start in range(0, up_to(lon_dev, step), step):
        taps = pltpu.roll(line, line.shape[1] + start - at, 1)
        taps = jnp.concatenate([taps[:, : lanes - 128], taps[:, -128:]], axis=1)
        band = pltpu.roll(jnp.concatenate([taps] * (step // 8), axis=0), 0, 1, stride=1, stride_axis=0)
        bands.append(band[:, :width].astype(jnp.bfloat16))
    return jnp.concatenate(bands, axis=0)


def take_kernel(chunks, lat_dev, block, slot_ref, place_ref, fields_ref, *refs):
    outs = refs[: len(chunks)]
    rows_ref, slots_ref, home_ref, take_ref = refs[len(chunks) :]
    lon_dev, _, channels = fields_ref.shape
    half, quarter = lat_dev // 2, lat_dev // 4
    starts = list(range(0, lon_dev, block))
    band, core, x = place_ref[0], place_ref[1], place_ref[2]

    def at(n):
        within = n % quarter
        return within + jnp.where(n // quarter == core, 0, quarter)

    def traded(n):
        within = n % quarter
        return n + jnp.where(within < 2, (within + x) % 2 - within, 0)

    stay, leave, come = jnp.int32(0), jnp.int32(0), jnp.int32(0)
    for j in range(lat_dev):
        here = band * lat_dev + j
        there = (1 - band) * lat_dev + j
        stays = slot_ref[here] // lat_dev == band
        comes = slot_ref[there] // lat_dev == band
        home_ref[jnp.where(stays, traded(at(stay)), half + at(leave))] = jnp.int32(j)

        @pl.when(stays)
        def _():
            spot = traded(at(stay))
            spot = spot + jnp.where(spot >= quarter, quarter, 0)
            rows_ref[spot] = here
            slots_ref[spot] = slot_ref[here] % lat_dev

        @pl.when(comes)
        def _():
            spot = at(come)
            spot = spot + jnp.where(spot >= quarter, half, quarter)
            rows_ref[spot] = there
            slots_ref[spot] = slot_ref[there] % lat_dev

        stay = stay + stays.astype(jnp.int32)
        leave = leave + 1 - stays.astype(jnp.int32)
        come = come + comes.astype(jnp.int32)

    def selector(lon_in, lon_out):
        lon = lax.broadcasted_iota(jnp.int32, (lon_out, lon_in * lat_dev), 0)
        column = lax.broadcasted_iota(jnp.int32, (lon_out, lon_in * lat_dev), 1)
        strips = [jnp.where(column == lon * lat_dev + home_ref[p], 1.0, 0.0) for p in range(lat_dev)]
        return jnp.concatenate(strips, axis=0).astype(jnp.bfloat16)

    take_ref[...] = selector(block, block)
    for start in starts:
        lon_in = min(block, lon_dev - start)
        lon_out = min(block, outs[0].shape[1] - start)
        panel = fields_ref[start : start + lon_in].reshape(lon_in * lat_dev, channels)
        take = take_ref[...] if (lon_in, lon_out) == (block, block) else selector(lon_in, lon_out)
        taken = jnp.dot(take, panel, preferred_element_type=jnp.float32).astype(jnp.bfloat16)
        place = 0
        for out, count in zip(outs, chunks):
            for i in range(count):
                out[i, start : start + lon_out, :] = taken[place * lon_out : (place + 1) * lon_out]
                place += 1


def take_rows(fields, owner_slot, place, chunks):
    lon_dev, lat_dev, channels = fields.shape
    block = 16
    padded = up_to(lon_dev, 8)
    ints = jax.ShapeDtypeStruct((lat_dev,), jnp.int32)
    result = pl.pallas_call(
        functools.partial(take_kernel, chunks, lat_dev, block),
        out_shape=[jax.ShapeDtypeStruct((n, padded, channels), fields.dtype) for n in chunks] + [ints, ints],
        in_specs=[SMEM_SPEC, SMEM_SPEC, VMEM_SPEC],
        out_specs=[VMEM_SPEC] * len(chunks) + [SMEM_SPEC, SMEM_SPEC],
        scratch_shapes=[
            pltpu.SMEM((lat_dev,), jnp.int32),
            pltpu.VMEM((block * lat_dev, block * lat_dev), jnp.bfloat16),
        ],
        compiler_params=pltpu.CompilerParams(vmem_limit_bytes=VMEM_LIMIT),
        cost_estimate=pl.CostEstimate(
            flops=2 * fields.size * block * lat_dev, bytes_accessed=4 * fields.size, transcendentals=0
        ),
        name="take_rows",
    )(owner_slot, place, fields)
    return result[:-2], result[-2], result[-1]


def put_kernel(counts, lat_dev, block, slots_ref, *refs):
    ins, (out_ref, panel_ref, sems) = refs[:-3], refs[-3:]
    lon_dev, _, channels = out_ref.shape

    def selector(lon_in, lon_out):
        shape = (lon_out * lat_dev, lat_dev * lon_in)
        row = lax.broadcasted_iota(jnp.int32, shape, 0)
        column = lax.broadcasted_iota(jnp.int32, (8, lat_dev * lon_in), 1)
        wanted = column % lon_in * lat_dev
        for p in range(lat_dev):
            wanted += jnp.where(column // lon_in == p, slots_ref[p], 0)
        return jnp.where(row == wanted[:1], 1.0, 0.0).astype(jnp.bfloat16)

    whole = selector(block, block)
    copies = []
    for n, start in enumerate(range(0, lon_dev, block)):
        lon_out = min(block, lon_dev - start)
        lon_in = min(block, ins[0].shape[1] - start)
        pieces = [r[i, start : start + lon_in, :] for r, count in zip(ins, counts) for i in range(count)]
        put = whole if (lon_in, lon_out) == (block, block) else selector(lon_in, lon_out)
        spread = jnp.dot(put, jnp.concatenate(pieces, axis=0), preferred_element_type=jnp.float32)
        window = pl.ds(start, lon_out)
        panel_ref[window] = spread.astype(jnp.bfloat16).reshape(lon_out, lat_dev, channels)
        copies.append(pltpu.make_async_copy(panel_ref.at[window], out_ref.at[window], sems.at[n]))
        copies[-1].start()
    for copy in copies:
        copy.wait()


def put_rows(panels, slots, lon_dev, lat_dev):
    padded, channels = panels[0].shape[1:]
    block = 16
    counts = tuple(p.shape[0] for p in panels)
    shape = (lon_dev, lat_dev, channels)
    return pl.pallas_call(
        functools.partial(put_kernel, counts, lat_dev, block),
        out_shape=jax.ShapeDtypeStruct(shape, panels[0].dtype),
        in_specs=[SMEM_SPEC] + [VMEM_SPEC] * len(panels),
        out_specs=HBM_SPEC,
        scratch_shapes=[
            pltpu.VMEM(shape, panels[0].dtype),
            pltpu.SemaphoreType.DMA((pl.cdiv(lon_dev, block),)),
        ],
        compiler_params=pltpu.CompilerParams(vmem_limit_bytes=VMEM_LIMIT),
        cost_estimate=pl.CostEstimate(
            flops=2 * lon_dev * lat_dev * channels * block * lat_dev,
            bytes_accessed=4 * lon_dev * lat_dev * channels,
            transcendentals=0,
        ),
        name="put_rows",
    )(slots, *panels)


def pair_kernel(lon_dev, base, plan, phase, rows_ref, place_ref, widths_ref, *refs):
    count = len(plan)
    side, along = 1 - 2 * place_ref[1], 1 - 2 * place_ref[2]
    if phase == "late":
        (total_in, block_ref), refs = refs[:2], refs[2:]
    else:
        line_ref, refs = refs[0], refs[1:]
    if phase == "early":
        ins, (total_ref, block_ref) = refs[:-2], refs[-2:]
    elif phase == "late":
        ins, (out_own, out_other) = refs[:-2], refs[-2:]
    else:
        ins, (out_own, out_other, block_ref) = refs[:-3], refs[-3:]
    padded, channels = ins[0].shape[1:]

    def both(first, second):
        return jnp.concatenate([first[...], second[...]], axis=1)

    for n, places in enumerate(plan):
        panels = [ins[array].at[i] for array, i in places]

        def times(offset, panel):
            return jnp.dot(block_ref[n, 2 + offset], panel, preferred_element_type=jnp.float32)[:padded]

        def halves(first, second):
            return jnp.concatenate([first, second], axis=1)

        nothing = jnp.zeros((padded, channels), jnp.float32)
        same = side == along
        if phase != "late":
            own, other, x_own, x_other = panels[:4]
            row = rows_ref[base + n]
            line = active_line(line_ref, row, widths_ref[row], 3 * lon_dev)
            for s in range(5):
                block_ref[n, s] = toeplitz(line, (s + 1) * lon_dev, lon_dev, padded)
            here = both(own, other)
            total = here.astype(jnp.float32) + times(0, here)
            total += times(2 * along, both(x_own, x_other))
            total += jnp.concatenate([times(side, other[...]), times(-side, own[...])], axis=1)
            more = times(along, jnp.where(same, x_own[...], x_other[...]))
            total += halves(jnp.where(same, nothing, more), jnp.where(same, more, nothing))
            if phase == "early":
                total_ref[n] = total
        if phase != "early":
            z_own, z_other = panels[-2:]
            if phase == "late":
                total = total_in[n]
            total += times(-2 * along, both(z_own, z_other))
            more = times(-along, jnp.where(same, z_other[...], z_own[...]))
            total += halves(jnp.where(same, more, nothing), jnp.where(same, nothing, more))
            out_own[n] = total[:, :channels].astype(out_own.dtype)
            out_other[n] = total[:, channels:].astype(out_other.dtype)


def filter_pair(scalars, lines, places, base, lon_dev, phase="whole", early=()):
    arrays = []
    plan = []
    for row in places:
        found = []
        for array, i in row:
            at = next((n for n, a in enumerate(arrays) if a is array), len(arrays))
            if at == len(arrays):
                arrays.append(array)
            found.append((at, i))
        plan.append(tuple(found))
    count = len(plan)
    padded, channels = arrays[0].shape[1:]
    total = (count, padded, 2 * channels), jnp.float32
    block = (count, 5, up_to(lon_dev, 96), padded), jnp.bfloat16
    out = jax.ShapeDtypeStruct((count, padded, channels), arrays[0].dtype)
    first = [lines] if phase != "late" else list(early)
    if phase == "early":
        outs, scratch = [jax.ShapeDtypeStruct(*total), jax.ShapeDtypeStruct(*block)], []
    elif phase == "late":
        outs, scratch = [out, out], []
    else:
        outs, scratch = [out, out], [pltpu.VMEM(*block)]
    weight = {"whole": 10, "early": 7, "late": 3}[phase]
    return pl.pallas_call(
        functools.partial(pair_kernel, lon_dev, base, tuple(plan), phase),
        out_shape=outs,
        in_specs=[SMEM_SPEC] * 3 + [VMEM_SPEC] * (len(first) + len(arrays)),
        out_specs=[VMEM_SPEC] * len(outs),
        scratch_shapes=scratch,
        compiler_params=pltpu.CompilerParams(vmem_limit_bytes=VMEM_LIMIT),
        cost_estimate=pl.CostEstimate(
            flops=FLOPS * count * weight * 256 * 256 * 768,
            bytes_accessed=16 * count * padded * channels,
            transcendentals=0,
        ),
        name="filter_" + phase,
    )(*scalars, *first, *arrays)


def chip_aware(fields, owner_slot, widths, tap_weights):
    lat_dev, lon_dev, channels = fields.shape
    n_lon = lax.axis_size("lon")
    at = lax.axis_index("lon")
    band = lax.axis_index("lat")
    core, x = at % 2, at // 2 % 2
    place = jnp.stack([band, core, x]).astype(jnp.int32)
    chunks = STAY + STAY + COME + COME
    taken, rows, slots = take_rows(jnp.transpose(fields, (1, 0, 2)), owner_slot, place, chunks)
    n_stay, n_come = len(STAY), len(COME)
    keep, give = taken[:n_stay], taken[n_stay : 2 * n_stay]
    straight, cross = taken[2 * n_stay : 2 * n_stay + n_come], taken[2 * n_stay + n_come :]

    across_core = [(i, i ^ 1) for i in range(n_lon)]
    across_x = [(i, i ^ 2) for i in range(n_lon)]
    across_x_core = [(i, i ^ 3) for i in range(n_lon)]
    across_z = [(i, (i + (4 if i // 2 % 2 == 0 else -4)) % n_lon) for i in range(n_lon)]
    back_z = [(i, (i + (-4 if i // 2 % 2 == 0 else 4)) % n_lon) for i in range(n_lon)]
    across_y = [(i, i ^ 1) for i in range(2 * n_lon)]
    across_both = [(i, i ^ 3) for i in range(2 * n_lon)]

    lines = tap_lines(tap_weights, 3 * lon_dev)
    scalars = rows, place, widths
    sizes = STAY + COME
    starts = [sum(sizes[:c]) for c in range(len(sizes))]
    done = {}

    def get(kind, i):
        if (kind, i) in done:
            return done[kind, i]

        def moved(operand, axes, pairs):
            first = [get(*g)[0] if g[0] in "ft" else get(*g) for g in WAITS.get((kind, i), ())]
            if first:
                operand = lax.optimization_barrier((operand, *first))[0]
            return lax.ppermute(operand, axes, pairs)

        if kind == "k":
            result = keep[i]
        elif kind == "c":
            result = moved(give[i], "lon", across_core)
        elif kind == "y":
            operand, pairs = ((straight, across_y), (cross, across_both))[i % 2]
            result = moved(operand[i // 2], ("lon", "lat"), pairs)
        elif kind == "x":
            result = moved(get(*PARTS[i]), "lon", across_x)
        elif kind == "z":
            result = moved(get("x", i), "lon", across_z)
        elif kind == "p":
            operand, pairs = ((keep[1], across_x), (give[1], across_x_core))[i]
            result = moved(operand, "lon", pairs)
        elif kind == "q":
            operand = get(*(("k", 0), ("c", 0), ("p", 0), ("p", 1))[i])
            result = moved(operand, "lon", back_z if i < 2 else across_z)
        elif kind == "t":
            here = [get("k", 0), get("c", 0)]
            beside = [get("p", 0), get("p", 1)]
            if i == 0:
                panels = here + beside + [get("q", 2), get("q", 3)]
            else:
                panels = beside + [get("q", 0), get("q", 1)] + here
            result = filter_pair(scalars, lines, [[(p, 0) for p in panels]], 0, lon_dev)
        elif kind == "b":
            operand, pairs = ((get("t", 0)[1], across_core), (get("t", 1)[0], across_x), (get("t", 1)[1], across_x_core))[i]
            result = moved(operand, "lon", pairs)
        elif kind == "f":
            places = []
            for row in FILTERS[i]:
                chunk, index = next((c, row - at) for c, at in enumerate(starts) if at <= row < at + sizes[c])
                if chunk < n_stay:
                    pair = ("k", chunk), ("c", chunk)
                else:
                    pair = ("y", 2 * (chunk - n_stay)), ("y", 2 * (chunk - n_stay) + 1)
                parts = [get(*p) for p in pair]
                parts += [get(axis, PARTS.index(p)) for axis in "xz" for p in pair]
                places.append([(p, index) for p in parts])
            base = FILTERS[i][0]
            if i < len(FILTERS) - 1:
                result = filter_pair(scalars, lines, places, base, lon_dev)
            else:
                early = filter_pair(scalars, lines, [p[:4] for p in places], base, lon_dev, "early")
                result = filter_pair(scalars, lines, [p[4:] for p in places], base, lon_dev, "late", early)
        else:
            result = moved(get("f", i)[1], "lon", across_core)
        done[kind, i] = result
        return result

    mine = [get("t", 0)[0], get("b", 1)] + [get("f", i)[0] for i in range(len(FILTERS))]
    theirs = [get("b", 0), get("b", 2)] + [get("o", i) for i in range(len(FILTERS))]
    out = put_rows(mine + theirs, slots, lon_dev, lat_dev)
    return jnp.transpose(out, (1, 0, 2))


def filter_kernel(reach, rows_ref, slots_ref, sector_ref, widths_ref, line_ref, *refs):
    ins, out_ref = refs[:-1], refs[-1]
    lon_dev, channels = out_ref.shape[1:]
    row = rows_ref[pl.program_id(0)]
    line = active_line(line_ref, row, widths_ref[row], (reach + 1) * lon_dev)
    total = ins[0][0].astype(jnp.float32)
    for group, ref in enumerate(ins):
        block = toeplitz(line, (sector_ref[group] + 1) * lon_dev, lon_dev, lon_dev)
        total += jnp.dot(block, ref[0], preferred_element_type=jnp.float32)[:lon_dev]
    out_ref[0] = total.astype(out_ref.dtype)


def filter_rows(rows, slots, sectors, widths, lines, arrays, reach):
    lat_dev, lon_dev, channels = arrays[0].shape
    row_spec = pl.BlockSpec((1, lon_dev, channels), lambda i, rows, slots, sectors, widths: (i, 0, 0))
    line_spec = pl.BlockSpec(lines.shape, lambda i, rows, slots, sectors, widths: (0, 0))
    out_spec = pl.BlockSpec((1, lon_dev, channels), lambda i, rows, slots, sectors, widths: (slots[i], 0, 0))
    return pl.pallas_call(
        functools.partial(filter_kernel, reach),
        out_shape=jax.ShapeDtypeStruct(arrays[0].shape, arrays[0].dtype),
        grid_spec=pltpu.PrefetchScalarGridSpec(
            num_scalar_prefetch=4,
            grid=(lat_dev,),
            in_specs=[line_spec] + [row_spec] * len(arrays),
            out_specs=out_spec,
        ),
        compiler_params=pltpu.CompilerParams(vmem_limit_bytes=VMEM_LIMIT),
        name="filter_rows",
    )(rows, slots, sectors, widths, lines, *arrays)


def any_mesh(fields, owner_slot, widths, tap_weights):
    lat_dev, lon_dev, channels = fields.shape
    n_lon = lax.axis_size("lon")
    n_lat = lax.axis_size("lat")
    reach = n_lon // 8
    band = lax.axis_index("lat")
    dest_band = owner_slot // lat_dev
    home_rows = band * lat_dev + jnp.arange(lat_dev, dtype=jnp.int32)
    ordering = jnp.argsort(dest_band[home_rows], stable=True)
    rows = jnp.argsort((dest_band != band).astype(jnp.int32), stable=True)[:lat_dev].astype(jnp.int32)
    slots = (owner_slot[rows] % lat_dev).astype(jnp.int32)
    outgoing = fields[ordering].reshape(n_lat, lat_dev // n_lat, lon_dev, channels)
    incoming = lax.all_to_all(outgoing, "lat", split_axis=0, concat_axis=0, tiled=True)
    own = incoming.reshape(lat_dev, lon_dev, channels)
    lines = tap_lines(tap_weights, (reach + 1) * lon_dev)
    arrays, order = [own], [reach]
    ahead = behind = own
    for step in range(1, reach + 1):
        ahead = shift_by(ahead, "lon", -1)
        behind = shift_by(behind, "lon", 1)
        arrays += [ahead, behind]
        order += [reach + step, reach - step]
    sectors = jnp.array(order, jnp.int32)
    return filter_rows(rows, slots, sectors, widths, lines, arrays, reach)


def solution(mesh):
    in_specs = (P("lat", "lon", None), P(), P(), P())
    out_specs = P("lat", "lon", None)
    chips = (mesh.shape["lon"], mesh.shape["lat"]) == (16, 2)

    def body(fields, owner_slot, widths, tap_weights):
        fits = chips and fields.shape[0] == 4 * sum(STAY)
        form = chip_aware if fits else any_mesh
        return form(fields, owner_slot, widths, tap_weights)

    return jax.shard_map(body, mesh=mesh, in_specs=in_specs, out_specs=out_specs, check_vma=False)
```

```python
import functools

import jax
import jax.numpy as jnp
from jax import lax
from jax.experimental import pallas as pl
from jax.experimental.pallas import tpu as pltpu
from jax.sharding import PartitionSpec as P

VMEM_LIMIT = 12 * 1024 * 1024
SMEM_SPEC = pl.BlockSpec(memory_space=pltpu.SMEM)
VMEM_SPEC = pl.BlockSpec(memory_space=pltpu.VMEM)
HBM_SPEC = pl.BlockSpec(memory_space=pltpu.HBM)
STAY = (2, 2)
COME = (2, 2)
PARTS = [("y", 0), ("y", 1), ("y", 2), ("y", 3)]
FILTERS = ((4, 5), (6, 7))
WAITS = {
    ("x", 0): [("p", 0)],
    ("x", 1): [("p", 1), ("q", 1)],
    ("x", 3): [("x", 1)],
    ("b", 1): [("t", 0)],
    ("b", 2): [("x", 3)],
    ("q", 2): [("q", 0)],
    ("q", 3): [("q", 1)],
    ("z", 0): [("q", 2)],
    ("z", 1): [("q", 3)],
    ("z", 2): [("z", 0)],
    ("z", 3): [("z", 1)],
    ("y", 2): [("y", 0), ("p", 0)],
    ("y", 3): [("y", 1)],
    ("y", 1): [("q", 0)],
}
FLOPS = 3


def up_to(value, multiple):
    return -(-value // multiple) * multiple


def shift_by(x, axis, by):
    count = lax.axis_size(axis)
    return lax.ppermute(x, axis, [(i, (i + by) % count) for i in range(count)])


def line_kernel(behind, taps_ref, line_ref):
    circle = taps_ref.shape[1]
    rows, lanes = line_ref.shape
    taps = taps_ref[...].astype(jnp.float32)
    pieces = [taps[:, circle - behind :], taps[:, :behind]]
    if lanes > 2 * behind:
        pieces.append(jnp.zeros((rows, lanes - 2 * behind), jnp.float32))
    line_ref[...] = jnp.concatenate(pieces, axis=1)


def tap_lines(tap_weights, behind):
    rows = tap_weights.shape[0]
    lanes = up_to(2 * behind, 128)
    return pl.pallas_call(
        functools.partial(line_kernel, behind),
        out_shape=jax.ShapeDtypeStruct((rows, lanes), jnp.float32),
        in_specs=[VMEM_SPEC],
        out_specs=VMEM_SPEC,
        compiler_params=pltpu.CompilerParams(vmem_limit_bytes=VMEM_LIMIT),
        cost_estimate=pl.CostEstimate(flops=0, bytes_accessed=2 * tap_weights.size, transcendentals=0),
        name="tap_lines",
    )(tap_weights)


def active_line(line_ref, row, width, behind):
    line = jnp.broadcast_to(line_ref[pl.ds(row, 1), :], (8, line_ref.shape[1]))
    distance = jnp.abs(lax.broadcasted_iota(jnp.int32, line.shape, 1) - behind)
    return jnp.where(distance <= width, line, 0.0)


def toeplitz(line, at, lon_dev, width):
    lanes = up_to(width, 128) + 128
    step = min(up_to(lon_dev, 16), 96)
    bands = []
    for start in range(0, up_to(lon_dev, step), step):
        taps = pltpu.roll(line, line.shape[1] + start - at, 1)
        taps = jnp.concatenate([taps[:, : lanes - 128], taps[:, -128:]], axis=1)
        band = pltpu.roll(jnp.concatenate([taps] * (step // 8), axis=0), 0, 1, stride=1, stride_axis=0)
        bands.append(band[:, :width].astype(jnp.bfloat16))
    return jnp.concatenate(bands, axis=0)


def take_kernel(chunks, lat_dev, block, slot_ref, place_ref, fields_ref, *refs):
    outs = refs[: len(chunks)]
    rows_ref, slots_ref, home_ref, take_ref = refs[len(chunks) :]
    lon_dev, _, channels = fields_ref.shape
    half, quarter = lat_dev // 2, lat_dev // 4
    starts = list(range(0, lon_dev, block))
    band, core, x = place_ref[0], place_ref[1], place_ref[2]

    def at(n):
        within = n % quarter
        return within + jnp.where(n // quarter == core, 0, quarter)

    def traded(n):
        within = n % quarter
        return n - within + (within + quarter // 2 * x) % quarter

    stay, leave, come = jnp.int32(0), jnp.int32(0), jnp.int32(0)
    for j in range(lat_dev):
        here = band * lat_dev + j
        there = (1 - band) * lat_dev + j
        stays = slot_ref[here] // lat_dev == band
        comes = slot_ref[there] // lat_dev == band
        home_ref[jnp.where(stays, traded(at(stay)), half + at(leave))] = jnp.int32(j)

        @pl.when(stays)
        def _():
            spot = traded(at(stay))
            spot = spot + jnp.where(spot >= quarter, quarter, 0)
            rows_ref[spot] = here
            slots_ref[spot] = slot_ref[here] % lat_dev

        @pl.when(comes)
        def _():
            spot = at(come)
            spot = spot + jnp.where(spot >= quarter, half, quarter)
            rows_ref[spot] = there
            slots_ref[spot] = slot_ref[there] % lat_dev

        stay = stay + stays.astype(jnp.int32)
        leave = leave + 1 - stays.astype(jnp.int32)
        come = come + comes.astype(jnp.int32)

    def selector(lon_in, lon_out):
        lon = lax.broadcasted_iota(jnp.int32, (lon_out, lon_in * lat_dev), 0)
        column = lax.broadcasted_iota(jnp.int32, (lon_out, lon_in * lat_dev), 1)
        strips = [jnp.where(column == lon * lat_dev + home_ref[p], 1.0, 0.0) for p in range(lat_dev)]
        return jnp.concatenate(strips, axis=0).astype(jnp.bfloat16)

    take_ref[...] = selector(block, block)
    for start in starts:
        lon_in = min(block, lon_dev - start)
        lon_out = min(block, outs[0].shape[1] - start)
        panel = fields_ref[start : start + lon_in].reshape(lon_in * lat_dev, channels)
        take = take_ref[...] if (lon_in, lon_out) == (block, block) else selector(lon_in, lon_out)
        taken = jnp.dot(take, panel, preferred_element_type=jnp.float32).astype(jnp.bfloat16)
        place = 0
        for out, count in zip(outs, chunks):
            for i in range(count):
                out[i, start : start + lon_out, :] = taken[place * lon_out : (place + 1) * lon_out]
                place += 1


def take_rows(fields, owner_slot, place, chunks):
    lon_dev, lat_dev, channels = fields.shape
    block = 16
    padded = up_to(lon_dev, 8)
    ints = jax.ShapeDtypeStruct((lat_dev,), jnp.int32)
    result = pl.pallas_call(
        functools.partial(take_kernel, chunks, lat_dev, block),
        out_shape=[jax.ShapeDtypeStruct((n, padded, channels), fields.dtype) for n in chunks] + [ints, ints],
        in_specs=[SMEM_SPEC, SMEM_SPEC, VMEM_SPEC],
        out_specs=[VMEM_SPEC] * len(chunks) + [SMEM_SPEC, SMEM_SPEC],
        scratch_shapes=[
            pltpu.SMEM((lat_dev,), jnp.int32),
            pltpu.VMEM((block * lat_dev, block * lat_dev), jnp.bfloat16),
        ],
        compiler_params=pltpu.CompilerParams(vmem_limit_bytes=VMEM_LIMIT),
        cost_estimate=pl.CostEstimate(
            flops=2 * fields.size * block * lat_dev, bytes_accessed=4 * fields.size, transcendentals=0
        ),
        name="take_rows",
    )(owner_slot, place, fields)
    return result[:-2], result[-2], result[-1]


def put_kernel(counts, lat_dev, block, slots_ref, *refs):
    ins, (out_ref, panel_ref, sems) = refs[:-3], refs[-3:]
    lon_dev, _, channels = out_ref.shape

    def selector(lon_in, lon_out):
        shape = (lon_out * lat_dev, lat_dev * lon_in)
        row = lax.broadcasted_iota(jnp.int32, shape, 0)
        column = lax.broadcasted_iota(jnp.int32, (8, lat_dev * lon_in), 1)
        wanted = column % lon_in * lat_dev
        for p in range(lat_dev):
            wanted += jnp.where(column // lon_in == p, slots_ref[p], 0)
        return jnp.where(row == wanted[:1], 1.0, 0.0).astype(jnp.bfloat16)

    whole = selector(block, block)
    copies = []
    for n, start in enumerate(range(0, lon_dev, block)):
        lon_out = min(block, lon_dev - start)
        lon_in = min(block, ins[0].shape[1] - start)
        pieces = [r[i, start : start + lon_in, :] for r, count in zip(ins, counts) for i in range(count)]
        put = whole if (lon_in, lon_out) == (block, block) else selector(lon_in, lon_out)
        spread = jnp.dot(put, jnp.concatenate(pieces, axis=0), preferred_element_type=jnp.float32)
        window = pl.ds(start, lon_out)
        panel_ref[window] = spread.astype(jnp.bfloat16).reshape(lon_out, lat_dev, channels)
        copies.append(pltpu.make_async_copy(panel_ref.at[window], out_ref.at[window], sems.at[n]))
        copies[-1].start()
    for copy in copies:
        copy.wait()


def put_rows(panels, slots, lon_dev, lat_dev):
    padded, channels = panels[0].shape[1:]
    block = 16
    counts = tuple(p.shape[0] for p in panels)
    shape = (lon_dev, lat_dev, channels)
    return pl.pallas_call(
        functools.partial(put_kernel, counts, lat_dev, block),
        out_shape=jax.ShapeDtypeStruct(shape, panels[0].dtype),
        in_specs=[SMEM_SPEC] + [VMEM_SPEC] * len(panels),
        out_specs=HBM_SPEC,
        scratch_shapes=[
            pltpu.VMEM(shape, panels[0].dtype),
            pltpu.SemaphoreType.DMA((pl.cdiv(lon_dev, block),)),
        ],
        compiler_params=pltpu.CompilerParams(vmem_limit_bytes=VMEM_LIMIT),
        cost_estimate=pl.CostEstimate(
            flops=2 * lon_dev * lat_dev * channels * block * lat_dev,
            bytes_accessed=4 * lon_dev * lat_dev * channels,
            transcendentals=0,
        ),
        name="put_rows",
    )(slots, *panels)


def pair_kernel(lon_dev, base, plan, phase, rows_ref, place_ref, widths_ref, *refs):
    count = len(plan)
    side, along = 1 - 2 * place_ref[1], 1 - 2 * place_ref[2]
    if phase == "late":
        (total_in, block_ref), refs = refs[:2], refs[2:]
    else:
        line_ref, refs = refs[0], refs[1:]
    if phase == "early":
        ins, (total_ref, block_ref) = refs[:-2], refs[-2:]
    elif phase == "late":
        ins, (out_own, out_other) = refs[:-2], refs[-2:]
    else:
        ins, (out_own, out_other, block_ref) = refs[:-3], refs[-3:]
    padded, channels = ins[0].shape[1:]

    def both(first, second):
        return jnp.concatenate([first[...], second[...]], axis=1)

    for n, places in enumerate(plan):
        panels = [ins[array].at[i] for array, i in places]

        def times(offset, panel):
            return jnp.dot(block_ref[n, 2 + offset], panel, preferred_element_type=jnp.float32)[:padded]

        def halves(first, second):
            return jnp.concatenate([first, second], axis=1)

        nothing = jnp.zeros((padded, channels), jnp.float32)
        same = side == along
        if phase != "late":
            own, other, x_own, x_other = panels[:4]
            row = rows_ref[base + n]
            line = active_line(line_ref, row, widths_ref[row], 3 * lon_dev)
            for s in range(5):
                block_ref[n, s] = toeplitz(line, (s + 1) * lon_dev, lon_dev, padded)
            here = both(own, other)
            total = here.astype(jnp.float32) + times(0, here)
            total += times(2 * along, both(x_own, x_other))
            total += jnp.concatenate([times(side, other[...]), times(-side, own[...])], axis=1)
            more = times(along, jnp.where(same, x_own[...], x_other[...]))
            total += halves(jnp.where(same, nothing, more), jnp.where(same, more, nothing))
            if phase == "early":
                total_ref[n] = total
        if phase != "early":
            z_own, z_other = panels[-2:]
            if phase == "late":
                total = total_in[n]
            total += times(-2 * along, both(z_own, z_other))
            more = times(-along, jnp.where(same, z_other[...], z_own[...]))
            total += halves(jnp.where(same, more, nothing), jnp.where(same, nothing, more))
            out_own[n] = total[:, :channels].astype(out_own.dtype)
            out_other[n] = total[:, channels:].astype(out_other.dtype)


def filter_pair(scalars, lines, places, base, lon_dev, phase="whole", early=()):
    arrays = []
    plan = []
    for row in places:
        found = []
        for array, i in row:
            at = next((n for n, a in enumerate(arrays) if a is array), len(arrays))
            if at == len(arrays):
                arrays.append(array)
            found.append((at, i))
        plan.append(tuple(found))
    count = len(plan)
    padded, channels = arrays[0].shape[1:]
    total = (count, padded, 2 * channels), jnp.float32
    block = (count, 5, up_to(lon_dev, 96), padded), jnp.bfloat16
    out = jax.ShapeDtypeStruct((count, padded, channels), arrays[0].dtype)
    first = [lines] if phase != "late" else list(early)
    if phase == "early":
        outs, scratch = [jax.ShapeDtypeStruct(*total), jax.ShapeDtypeStruct(*block)], []
    elif phase == "late":
        outs, scratch = [out, out], []
    else:
        outs, scratch = [out, out], [pltpu.VMEM(*block)]
    weight = {"whole": 10, "early": 7, "late": 3}[phase]
    return pl.pallas_call(
        functools.partial(pair_kernel, lon_dev, base, tuple(plan), phase),
        out_shape=outs,
        in_specs=[SMEM_SPEC] * 3 + [VMEM_SPEC] * (len(first) + len(arrays)),
        out_specs=[VMEM_SPEC] * len(outs),
        scratch_shapes=scratch,
        compiler_params=pltpu.CompilerParams(vmem_limit_bytes=VMEM_LIMIT),
        cost_estimate=pl.CostEstimate(
            flops=FLOPS * count * weight * 256 * 256 * 768,
            bytes_accessed=16 * count * padded * channels,
            transcendentals=0,
        ),
        name="filter_" + phase,
    )(*scalars, *first, *arrays)


def chip_aware(fields, owner_slot, widths, tap_weights):
    lat_dev, lon_dev, channels = fields.shape
    n_lon = lax.axis_size("lon")
    at = lax.axis_index("lon")
    band = lax.axis_index("lat")
    core, x = at % 2, at // 2 % 2
    place = jnp.stack([band, core, x]).astype(jnp.int32)
    chunks = STAY + STAY + COME + COME
    taken, rows, slots = take_rows(jnp.transpose(fields, (1, 0, 2)), owner_slot, place, chunks)
    n_stay, n_come = len(STAY), len(COME)
    keep, give = taken[:n_stay], taken[n_stay : 2 * n_stay]
    straight, cross = taken[2 * n_stay : 2 * n_stay + n_come], taken[2 * n_stay + n_come :]

    across_core = [(i, i ^ 1) for i in range(n_lon)]
    across_x = [(i, i ^ 2) for i in range(n_lon)]
    across_x_core = [(i, i ^ 3) for i in range(n_lon)]
    across_z = [(i, (i + (4 if i // 2 % 2 == 0 else -4)) % n_lon) for i in range(n_lon)]
    back_z = [(i, (i + (-4 if i // 2 % 2 == 0 else 4)) % n_lon) for i in range(n_lon)]
    across_y = [(i, i ^ 1) for i in range(2 * n_lon)]
    across_both = [(i, i ^ 3) for i in range(2 * n_lon)]

    lines = tap_lines(tap_weights, 3 * lon_dev)
    scalars = rows, place, widths
    sizes = STAY + COME
    starts = [sum(sizes[:c]) for c in range(len(sizes))]
    done = {}

    def get(kind, i):
        if (kind, i) in done:
            return done[kind, i]

        def moved(operand, axes, pairs):
            first = [get(*g)[0] if g[0] in "ft" else get(*g) for g in WAITS.get((kind, i), ())]
            if first:
                operand = lax.optimization_barrier((operand, *first))[0]
            return lax.ppermute(operand, axes, pairs)

        if kind == "k":
            result = keep[i]
        elif kind == "c":
            result = moved(give[i], "lon", across_core)
        elif kind == "y":
            operand, pairs = ((straight, across_y), (cross, across_both))[i % 2]
            result = moved(operand[i // 2], ("lon", "lat"), pairs)
        elif kind == "x":
            result = moved(get(*PARTS[i]), "lon", across_x)
        elif kind == "z":
            result = moved(get("x", i), "lon", across_z)
        elif kind == "p":
            operand, pairs = ((keep[1], across_x), (give[1], across_x_core))[i]
            result = moved(operand, "lon", pairs)
        elif kind == "q":
            operand = get(*(("k", 0), ("c", 0), ("p", 0), ("p", 1))[i])
            result = moved(operand, "lon", back_z if i < 2 else across_z)
        elif kind == "t":
            here = [get("k", 0), get("c", 0)]
            beside = [get("p", 0), get("p", 1)]
            if i == 0:
                panels = here + beside + [get("q", 2), get("q", 3)]
            else:
                panels = beside + [get("q", 0), get("q", 1)] + here
            places = [[(p, row) for p in panels] for row in range(STAY[0])]
            result = filter_pair(scalars, lines, places, 0, lon_dev)
        elif kind == "b":
            operand, pairs = ((get("t", 0)[1], across_core), (get("t", 1)[0], across_x), (get("t", 1)[1], across_x_core))[i]
            result = moved(operand, "lon", pairs)
        elif kind == "f":
            places = []
            for row in FILTERS[i]:
                chunk, index = next((c, row - at) for c, at in enumerate(starts) if at <= row < at + sizes[c])
                if chunk < n_stay:
                    pair = ("k", chunk), ("c", chunk)
                else:
                    pair = ("y", 2 * (chunk - n_stay)), ("y", 2 * (chunk - n_stay) + 1)
                parts = [get(*p) for p in pair]
                parts += [get(axis, PARTS.index(p)) for axis in "xz" for p in pair]
                places.append([(p, index) for p in parts])
            base = FILTERS[i][0]
            if i < len(FILTERS) - 1:
                result = filter_pair(scalars, lines, places, base, lon_dev)
            else:
                early = filter_pair(scalars, lines, [p[:4] for p in places], base, lon_dev, "early")
                result = filter_pair(scalars, lines, [p[4:] for p in places], base, lon_dev, "late", early)
        else:
            result = moved(get("f", i)[1], "lon", across_core)
        done[kind, i] = result
        return result

    mine = [get("t", 0)[0], get("b", 1)] + [get("f", i)[0] for i in range(len(FILTERS))]
    theirs = [get("b", 0), get("b", 2)] + [get("o", i) for i in range(len(FILTERS))]
    out = put_rows(mine + theirs, slots, lon_dev, lat_dev)
    return jnp.transpose(out, (1, 0, 2))


def filter_kernel(reach, rows_ref, slots_ref, sector_ref, widths_ref, line_ref, *refs):
    ins, out_ref = refs[:-1], refs[-1]
    lon_dev, channels = out_ref.shape[1:]
    row = rows_ref[pl.program_id(0)]
    line = active_line(line_ref, row, widths_ref[row], (reach + 1) * lon_dev)
    total = ins[0][0].astype(jnp.float32)
    for group, ref in enumerate(ins):
        block = toeplitz(line, (sector_ref[group] + 1) * lon_dev, lon_dev, lon_dev)
        total += jnp.dot(block, ref[0], preferred_element_type=jnp.float32)[:lon_dev]
    out_ref[0] = total.astype(out_ref.dtype)


def filter_rows(rows, slots, sectors, widths, lines, arrays, reach):
    lat_dev, lon_dev, channels = arrays[0].shape
    row_spec = pl.BlockSpec((1, lon_dev, channels), lambda i, rows, slots, sectors, widths: (i, 0, 0))
    line_spec = pl.BlockSpec(lines.shape, lambda i, rows, slots, sectors, widths: (0, 0))
    out_spec = pl.BlockSpec((1, lon_dev, channels), lambda i, rows, slots, sectors, widths: (slots[i], 0, 0))
    return pl.pallas_call(
        functools.partial(filter_kernel, reach),
        out_shape=jax.ShapeDtypeStruct(arrays[0].shape, arrays[0].dtype),
        grid_spec=pltpu.PrefetchScalarGridSpec(
            num_scalar_prefetch=4,
            grid=(lat_dev,),
            in_specs=[line_spec] + [row_spec] * len(arrays),
            out_specs=out_spec,
        ),
        compiler_params=pltpu.CompilerParams(vmem_limit_bytes=VMEM_LIMIT),
        name="filter_rows",
    )(rows, slots, sectors, widths, lines, *arrays)


def any_mesh(fields, owner_slot, widths, tap_weights):
    lat_dev, lon_dev, channels = fields.shape
    n_lon = lax.axis_size("lon")
    n_lat = lax.axis_size("lat")
    reach = n_lon // 8
    band = lax.axis_index("lat")
    dest_band = owner_slot // lat_dev
    home_rows = band * lat_dev + jnp.arange(lat_dev, dtype=jnp.int32)
    ordering = jnp.argsort(dest_band[home_rows], stable=True)
    rows = jnp.argsort((dest_band != band).astype(jnp.int32), stable=True)[:lat_dev].astype(jnp.int32)
    slots = (owner_slot[rows] % lat_dev).astype(jnp.int32)
    outgoing = fields[ordering].reshape(n_lat, lat_dev // n_lat, lon_dev, channels)
    incoming = lax.all_to_all(outgoing, "lat", split_axis=0, concat_axis=0, tiled=True)
    own = incoming.reshape(lat_dev, lon_dev, channels)
    lines = tap_lines(tap_weights, (reach + 1) * lon_dev)
    arrays, order = [own], [reach]
    ahead = behind = own
    for step in range(1, reach + 1):
        ahead = shift_by(ahead, "lon", -1)
        behind = shift_by(behind, "lon", 1)
        arrays += [ahead, behind]
        order += [reach + step, reach - step]
    sectors = jnp.array(order, jnp.int32)
    return filter_rows(rows, slots, sectors, widths, lines, arrays, reach)


def solution(mesh):
    in_specs = (P("lat", "lon", None), P(), P(), P())
    out_specs = P("lat", "lon", None)
    chips = (mesh.shape["lon"], mesh.shape["lat"]) == (16, 2)

    def body(fields, owner_slot, widths, tap_weights):
        fits = chips and fields.shape[0] == 4 * sum(STAY)
        form = chip_aware if fits else any_mesh
        return form(fields, owner_slot, widths, tap_weights)

    return jax.shard_map(body, mesh=mesh, in_specs=in_specs, out_specs=out_specs, check_vma=False)
```

```python
import functools

import jax
import jax.numpy as jnp
from jax import lax
from jax.experimental import pallas as pl
from jax.experimental.pallas import tpu as pltpu
from jax.sharding import PartitionSpec as P

VMEM_LIMIT = 12 * 1024 * 1024
SMEM_SPEC = pl.BlockSpec(memory_space=pltpu.SMEM)
VMEM_SPEC = pl.BlockSpec(memory_space=pltpu.VMEM)
HBM_SPEC = pl.BlockSpec(memory_space=pltpu.HBM)
STAY = (2, 2)
COME = (2, 2)
PARTS = [("y", 0), ("y", 1), ("y", 2), ("y", 3)]
FILTERS = ((4, 5), (6, 7))
WAITS = {
    ("x", 0): [("p", 0), ("y", 0)],
    ("x", 1): [("p", 1)],
    ("b", 2): [("x", 3)],
    ("q", 2): [("q", 0)],
    ("q", 3): [("q", 1)],
    ("z", 0): [("q", 2), ("q", 1)],
    ("z", 1): [("q", 3), ("t", 1)],
    ("z", 2): [("z", 0)],
    ("z", 3): [("z", 1)],
    ("y", 2): [("y", 0), ("p", 0)],
    ("y", 3): [("y", 1), ("x", 0)],
    ("y", 1): [("q", 0)],
}
FLOPS = 3


def up_to(value, multiple):
    return -(-value // multiple) * multiple


def shift_by(x, axis, by):
    count = lax.axis_size(axis)
    return lax.ppermute(x, axis, [(i, (i + by) % count) for i in range(count)])


def line_kernel(behind, taps_ref, line_ref):
    circle = taps_ref.shape[1]
    rows, lanes = line_ref.shape
    taps = taps_ref[...].astype(jnp.float32)
    pieces = [taps[:, circle - behind :], taps[:, :behind]]
    if lanes > 2 * behind:
        pieces.append(jnp.zeros((rows, lanes - 2 * behind), jnp.float32))
    line_ref[...] = jnp.concatenate(pieces, axis=1)


def tap_lines(tap_weights, behind):
    rows = tap_weights.shape[0]
    lanes = up_to(2 * behind, 128)
    return pl.pallas_call(
        functools.partial(line_kernel, behind),
        out_shape=jax.ShapeDtypeStruct((rows, lanes), jnp.float32),
        in_specs=[VMEM_SPEC],
        out_specs=VMEM_SPEC,
        compiler_params=pltpu.CompilerParams(vmem_limit_bytes=VMEM_LIMIT),
        cost_estimate=pl.CostEstimate(flops=0, bytes_accessed=2 * tap_weights.size, transcendentals=0),
        name="tap_lines",
    )(tap_weights)


def active_line(line_ref, row, width, behind):
    line = jnp.broadcast_to(line_ref[pl.ds(row, 1), :], (8, line_ref.shape[1]))
    distance = jnp.abs(lax.broadcasted_iota(jnp.int32, line.shape, 1) - behind)
    return jnp.where(distance <= width, line, 0.0)


def toeplitz(line, at, lon_dev, width):
    lanes = up_to(width, 128) + 128
    step = min(up_to(lon_dev, 16), 96)
    bands = []
    for start in range(0, up_to(lon_dev, step), step):
        taps = pltpu.roll(line, line.shape[1] + start - at, 1)
        taps = jnp.concatenate([taps[:, : lanes - 128], taps[:, -128:]], axis=1)
        band = pltpu.roll(jnp.concatenate([taps] * (step // 8), axis=0), 0, 1, stride=1, stride_axis=0)
        bands.append(band[:, :width].astype(jnp.bfloat16))
    return jnp.concatenate(bands, axis=0)


def take_kernel(chunks, lat_dev, block, slot_ref, place_ref, fields_ref, *refs):
    outs = refs[: len(chunks)]
    rows_ref, slots_ref, home_ref, take_ref = refs[len(chunks) :]
    lon_dev, _, channels = fields_ref.shape
    half, quarter = lat_dev // 2, lat_dev // 4
    starts = list(range(0, lon_dev, block))
    band, core, x = place_ref[0], place_ref[1], place_ref[2]

    def at(n):
        within = n % quarter
        return within + jnp.where(n // quarter == core, 0, quarter)

    def traded(n):
        within = n % quarter
        return n - within + (within + quarter // 2 * x) % quarter

    stay, leave, come = jnp.int32(0), jnp.int32(0), jnp.int32(0)
    for j in range(lat_dev):
        here = band * lat_dev + j
        there = (1 - band) * lat_dev + j
        stays = slot_ref[here] // lat_dev == band
        comes = slot_ref[there] // lat_dev == band
        home_ref[jnp.where(stays, traded(at(stay)), half + at(leave))] = jnp.int32(j)

        @pl.when(stays)
        def _():
            spot = traded(at(stay))
            spot = spot + jnp.where(spot >= quarter, quarter, 0)
            rows_ref[spot] = here
            slots_ref[spot] = slot_ref[here] % lat_dev

        @pl.when(comes)
        def _():
            spot = at(come)
            spot = spot + jnp.where(spot >= quarter, half, quarter)
            rows_ref[spot] = there
            slots_ref[spot] = slot_ref[there] % lat_dev

        stay = stay + stays.astype(jnp.int32)
        leave = leave + 1 - stays.astype(jnp.int32)
        come = come + comes.astype(jnp.int32)

    def selector(lon_in, lon_out):
        lon = lax.broadcasted_iota(jnp.int32, (lon_out, lon_in * lat_dev), 0)
        column = lax.broadcasted_iota(jnp.int32, (lon_out, lon_in * lat_dev), 1)
        strips = [jnp.where(column == lon * lat_dev + home_ref[p], 1.0, 0.0) for p in range(lat_dev)]
        return jnp.concatenate(strips, axis=0).astype(jnp.bfloat16)

    take_ref[...] = selector(block, block)
    for start in starts:
        lon_in = min(block, lon_dev - start)
        lon_out = min(block, outs[0].shape[1] - start)
        panel = fields_ref[start : start + lon_in].reshape(lon_in * lat_dev, channels)
        take = take_ref[...] if (lon_in, lon_out) == (block, block) else selector(lon_in, lon_out)
        taken = jnp.dot(take, panel, preferred_element_type=jnp.float32).astype(jnp.bfloat16)
        place = 0
        for out, count in zip(outs, chunks):
            for i in range(count):
                out[i, start : start + lon_out, :] = taken[place * lon_out : (place + 1) * lon_out]
                place += 1


def take_rows(fields, owner_slot, place, chunks):
    lon_dev, lat_dev, channels = fields.shape
    block = 16
    padded = up_to(lon_dev, 8)
    ints = jax.ShapeDtypeStruct((lat_dev,), jnp.int32)
    result = pl.pallas_call(
        functools.partial(take_kernel, chunks, lat_dev, block),
        out_shape=[jax.ShapeDtypeStruct((n, padded, channels), fields.dtype) for n in chunks] + [ints, ints],
        in_specs=[SMEM_SPEC, SMEM_SPEC, VMEM_SPEC],
        out_specs=[VMEM_SPEC] * len(chunks) + [SMEM_SPEC, SMEM_SPEC],
        scratch_shapes=[
            pltpu.SMEM((lat_dev,), jnp.int32),
            pltpu.VMEM((block * lat_dev, block * lat_dev), jnp.bfloat16),
        ],
        compiler_params=pltpu.CompilerParams(vmem_limit_bytes=VMEM_LIMIT),
        cost_estimate=pl.CostEstimate(
            flops=2 * fields.size * block * lat_dev, bytes_accessed=4 * fields.size, transcendentals=0
        ),
        name="take_rows",
    )(owner_slot, place, fields)
    return result[:-2], result[-2], result[-1]


def put_kernel(counts, lat_dev, block, slots_ref, *refs):
    ins, (out_ref, panel_ref, sems) = refs[:-3], refs[-3:]
    lon_dev, _, channels = out_ref.shape

    def selector(lon_in, lon_out):
        shape = (lon_out * lat_dev, lat_dev * lon_in)
        row = lax.broadcasted_iota(jnp.int32, shape, 0)
        column = lax.broadcasted_iota(jnp.int32, (8, lat_dev * lon_in), 1)
        wanted = column % lon_in * lat_dev
        for p in range(lat_dev):
            wanted += jnp.where(column // lon_in == p, slots_ref[p], 0)
        return jnp.where(row == wanted[:1], 1.0, 0.0).astype(jnp.bfloat16)

    whole = selector(block, block)
    copies = []
    for n, start in enumerate(range(0, lon_dev, block)):
        lon_out = min(block, lon_dev - start)
        lon_in = min(block, ins[0].shape[1] - start)
        pieces = [r[i, start : start + lon_in, :] for r, count in zip(ins, counts) for i in range(count)]
        put = whole if (lon_in, lon_out) == (block, block) else selector(lon_in, lon_out)
        spread = jnp.dot(put, jnp.concatenate(pieces, axis=0), preferred_element_type=jnp.float32)
        window = pl.ds(start, lon_out)
        panel_ref[window] = spread.astype(jnp.bfloat16).reshape(lon_out, lat_dev, channels)
        copies.append(pltpu.make_async_copy(panel_ref.at[window], out_ref.at[window], sems.at[n]))
        copies[-1].start()
    for copy in copies:
        copy.wait()


def put_rows(panels, slots, lon_dev, lat_dev):
    padded, channels = panels[0].shape[1:]
    block = 16
    counts = tuple(p.shape[0] for p in panels)
    shape = (lon_dev, lat_dev, channels)
    return pl.pallas_call(
        functools.partial(put_kernel, counts, lat_dev, block),
        out_shape=jax.ShapeDtypeStruct(shape, panels[0].dtype),
        in_specs=[SMEM_SPEC] + [VMEM_SPEC] * len(panels),
        out_specs=HBM_SPEC,
        scratch_shapes=[
            pltpu.VMEM(shape, panels[0].dtype),
            pltpu.SemaphoreType.DMA((pl.cdiv(lon_dev, block),)),
        ],
        compiler_params=pltpu.CompilerParams(vmem_limit_bytes=VMEM_LIMIT),
        cost_estimate=pl.CostEstimate(
            flops=2 * lon_dev * lat_dev * channels * block * lat_dev,
            bytes_accessed=4 * lon_dev * lat_dev * channels,
            transcendentals=0,
        ),
        name="put_rows",
    )(slots, *panels)


def pair_kernel(lon_dev, base, plan, phase, rows_ref, place_ref, widths_ref, *refs):
    count = len(plan)
    side, along = 1 - 2 * place_ref[1], 1 - 2 * place_ref[2]
    if phase == "late":
        (total_in, block_ref), refs = refs[:2], refs[2:]
    else:
        line_ref, refs = refs[0], refs[1:]
    if phase == "early":
        ins, (total_ref, block_ref) = refs[:-2], refs[-2:]
    elif phase == "late":
        ins, (out_own, out_other) = refs[:-2], refs[-2:]
    else:
        ins, (out_own, out_other, block_ref) = refs[:-3], refs[-3:]
    padded, channels = ins[0].shape[1:]

    def both(first, second):
        return jnp.concatenate([first[...], second[...]], axis=1)

    for n, places in enumerate(plan):
        panels = [ins[array].at[i] for array, i in places]

        def times(offset, panel):
            return jnp.dot(block_ref[n, 2 + offset], panel, preferred_element_type=jnp.float32)[:padded]

        def halves(first, second):
            return jnp.concatenate([first, second], axis=1)

        nothing = jnp.zeros((padded, channels), jnp.float32)
        same = side == along
        if phase != "late":
            own, other, x_own, x_other = panels[:4]
            row = rows_ref[base + n]
            line = active_line(line_ref, row, widths_ref[row], 3 * lon_dev)
            for s in range(5):
                block_ref[n, s] = toeplitz(line, (s + 1) * lon_dev, lon_dev, padded)
            here = both(own, other)
            total = here.astype(jnp.float32) + times(0, here)
            total += times(2 * along, both(x_own, x_other))
            total += jnp.concatenate([times(side, other[...]), times(-side, own[...])], axis=1)
            more = times(along, jnp.where(same, x_own[...], x_other[...]))
            total += halves(jnp.where(same, nothing, more), jnp.where(same, more, nothing))
            if phase == "early":
                total_ref[n] = total
        if phase != "early":
            z_own, z_other = panels[-2:]
            if phase == "late":
                total = total_in[n]
            total += times(-2 * along, both(z_own, z_other))
            more = times(-along, jnp.where(same, z_other[...], z_own[...]))
            total += halves(jnp.where(same, more, nothing), jnp.where(same, nothing, more))
            out_own[n] = total[:, :channels].astype(out_own.dtype)
            out_other[n] = total[:, channels:].astype(out_other.dtype)


def filter_pair(scalars, lines, places, base, lon_dev, phase="whole", early=()):
    arrays = []
    plan = []
    for row in places:
        found = []
        for array, i in row:
            at = next((n for n, a in enumerate(arrays) if a is array), len(arrays))
            if at == len(arrays):
                arrays.append(array)
            found.append((at, i))
        plan.append(tuple(found))
    count = len(plan)
    padded, channels = arrays[0].shape[1:]
    total = (count, padded, 2 * channels), jnp.float32
    block = (count, 5, up_to(lon_dev, 96), padded), jnp.bfloat16
    out = jax.ShapeDtypeStruct((count, padded, channels), arrays[0].dtype)
    first = [lines] if phase != "late" else list(early)
    if phase == "early":
        outs, scratch = [jax.ShapeDtypeStruct(*total), jax.ShapeDtypeStruct(*block)], []
    elif phase == "late":
        outs, scratch = [out, out], []
    else:
        outs, scratch = [out, out], [pltpu.VMEM(*block)]
    weight = {"whole": 10, "early": 7, "late": 3}[phase]
    return pl.pallas_call(
        functools.partial(pair_kernel, lon_dev, base, tuple(plan), phase),
        out_shape=outs,
        in_specs=[SMEM_SPEC] * 3 + [VMEM_SPEC] * (len(first) + len(arrays)),
        out_specs=[VMEM_SPEC] * len(outs),
        scratch_shapes=scratch,
        compiler_params=pltpu.CompilerParams(vmem_limit_bytes=VMEM_LIMIT),
        cost_estimate=pl.CostEstimate(
            flops=FLOPS * count * weight * 256 * 256 * 768,
            bytes_accessed=16 * count * padded * channels,
            transcendentals=0,
        ),
        name="filter_" + phase,
    )(*scalars, *first, *arrays)


def chip_aware(fields, owner_slot, widths, tap_weights):
    lat_dev, lon_dev, channels = fields.shape
    n_lon = lax.axis_size("lon")
    at = lax.axis_index("lon")
    band = lax.axis_index("lat")
    core, x = at % 2, at // 2 % 2
    place = jnp.stack([band, core, x]).astype(jnp.int32)
    chunks = STAY + STAY + COME + COME
    taken, rows, slots = take_rows(jnp.transpose(fields, (1, 0, 2)), owner_slot, place, chunks)
    n_stay, n_come = len(STAY), len(COME)
    keep, give = taken[:n_stay], taken[n_stay : 2 * n_stay]
    straight, cross = taken[2 * n_stay : 2 * n_stay + n_come], taken[2 * n_stay + n_come :]

    across_core = [(i, i ^ 1) for i in range(n_lon)]
    across_x = [(i, i ^ 2) for i in range(n_lon)]
    across_x_core = [(i, i ^ 3) for i in range(n_lon)]
    across_z = [(i, (i + (4 if i // 2 % 2 == 0 else -4)) % n_lon) for i in range(n_lon)]
    back_z = [(i, (i + (-4 if i // 2 % 2 == 0 else 4)) % n_lon) for i in range(n_lon)]
    across_y = [(i, i ^ 1) for i in range(2 * n_lon)]
    across_both = [(i, i ^ 3) for i in range(2 * n_lon)]

    lines = tap_lines(tap_weights, 3 * lon_dev)
    scalars = rows, place, widths
    sizes = STAY + COME
    starts = [sum(sizes[:c]) for c in range(len(sizes))]
    done = {}

    def get(kind, i):
        if (kind, i) in done:
            return done[kind, i]

        def moved(operand, axes, pairs):
            first = [get(*g)[0] if g[0] in "ft" else get(*g) for g in WAITS.get((kind, i), ())]
            if first:
                operand = lax.optimization_barrier((operand, *first))[0]
            return lax.ppermute(operand, axes, pairs)

        if kind == "k":
            result = keep[i]
        elif kind == "c":
            result = moved(give[i], "lon", across_core)
        elif kind == "y":
            operand, pairs = ((straight, across_y), (cross, across_both))[i % 2]
            result = moved(operand[i // 2], ("lon", "lat"), pairs)
        elif kind == "x":
            result = moved(get(*PARTS[i]), "lon", across_x)
        elif kind == "z":
            result = moved(get("x", i), "lon", across_z)
        elif kind == "p":
            operand, pairs = ((keep[1], across_x), (give[1], across_x_core))[i]
            result = moved(operand, "lon", pairs)
        elif kind == "q":
            operand = get(*(("k", 0), ("c", 0), ("p", 0), ("p", 1))[i])
            result = moved(operand, "lon", back_z if i < 2 else across_z)
        elif kind == "t":
            here = [get("k", 0), get("c", 0)]
            beside = [get("p", 0), get("p", 1)]
            if i == 0:
                panels = here + beside + [get("q", 2), get("q", 3)]
            else:
                panels = beside + [get("q", 0), get("q", 1)] + here
            places = [[(p, row) for p in panels] for row in range(STAY[0])]
            result = filter_pair(scalars, lines, places, 0, lon_dev)
        elif kind == "b":
            operand, pairs = ((get("t", 0)[1], across_core), (get("t", 1)[0], across_x), (get("t", 1)[1], across_x_core))[i]
            result = moved(operand, "lon", pairs)
        elif kind == "f":
            places = []
            for row in FILTERS[i]:
                chunk, index = next((c, row - at) for c, at in enumerate(starts) if at <= row < at + sizes[c])
                if chunk < n_stay:
                    pair = ("k", chunk), ("c", chunk)
                else:
                    pair = ("y", 2 * (chunk - n_stay)), ("y", 2 * (chunk - n_stay) + 1)
                parts = [get(*p) for p in pair]
                parts += [get(axis, PARTS.index(p)) for axis in "xz" for p in pair]
                places.append([(p, index) for p in parts])
            base = FILTERS[i][0]
            if i < len(FILTERS) - 1:
                result = filter_pair(scalars, lines, places, base, lon_dev)
            else:
                early = filter_pair(scalars, lines, [p[:4] for p in places], base, lon_dev, "early")
                result = filter_pair(scalars, lines, [p[4:] for p in places], base, lon_dev, "late", early)
        else:
            result = moved(get("f", i)[1], "lon", across_core)
        done[kind, i] = result
        return result

    mine = [get("t", 0)[0], get("b", 1)] + [get("f", i)[0] for i in range(len(FILTERS))]
    theirs = [get("b", 0), get("b", 2)] + [get("o", i) for i in range(len(FILTERS))]
    out = put_rows(mine + theirs, slots, lon_dev, lat_dev)
    return jnp.transpose(out, (1, 0, 2))


def filter_kernel(reach, rows_ref, slots_ref, sector_ref, widths_ref, line_ref, *refs):
    ins, out_ref = refs[:-1], refs[-1]
    lon_dev, channels = out_ref.shape[1:]
    row = rows_ref[pl.program_id(0)]
    line = active_line(line_ref, row, widths_ref[row], (reach + 1) * lon_dev)
    total = ins[0][0].astype(jnp.float32)
    for group, ref in enumerate(ins):
        block = toeplitz(line, (sector_ref[group] + 1) * lon_dev, lon_dev, lon_dev)
        total += jnp.dot(block, ref[0], preferred_element_type=jnp.float32)[:lon_dev]
    out_ref[0] = total.astype(out_ref.dtype)


def filter_rows(rows, slots, sectors, widths, lines, arrays, reach):
    lat_dev, lon_dev, channels = arrays[0].shape
    row_spec = pl.BlockSpec((1, lon_dev, channels), lambda i, rows, slots, sectors, widths: (i, 0, 0))
    line_spec = pl.BlockSpec(lines.shape, lambda i, rows, slots, sectors, widths: (0, 0))
    out_spec = pl.BlockSpec((1, lon_dev, channels), lambda i, rows, slots, sectors, widths: (slots[i], 0, 0))
    return pl.pallas_call(
        functools.partial(filter_kernel, reach),
        out_shape=jax.ShapeDtypeStruct(arrays[0].shape, arrays[0].dtype),
        grid_spec=pltpu.PrefetchScalarGridSpec(
            num_scalar_prefetch=4,
            grid=(lat_dev,),
            in_specs=[line_spec] + [row_spec] * len(arrays),
            out_specs=out_spec,
        ),
        compiler_params=pltpu.CompilerParams(vmem_limit_bytes=VMEM_LIMIT),
        name="filter_rows",
    )(rows, slots, sectors, widths, lines, *arrays)


def any_mesh(fields, owner_slot, widths, tap_weights):
    lat_dev, lon_dev, channels = fields.shape
    n_lon = lax.axis_size("lon")
    n_lat = lax.axis_size("lat")
    reach = n_lon // 8
    band = lax.axis_index("lat")
    dest_band = owner_slot // lat_dev
    home_rows = band * lat_dev + jnp.arange(lat_dev, dtype=jnp.int32)
    ordering = jnp.argsort(dest_band[home_rows], stable=True)
    rows = jnp.argsort((dest_band != band).astype(jnp.int32), stable=True)[:lat_dev].astype(jnp.int32)
    slots = (owner_slot[rows] % lat_dev).astype(jnp.int32)
    outgoing = fields[ordering].reshape(n_lat, lat_dev // n_lat, lon_dev, channels)
    incoming = lax.all_to_all(outgoing, "lat", split_axis=0, concat_axis=0, tiled=True)
    own = incoming.reshape(lat_dev, lon_dev, channels)
    lines = tap_lines(tap_weights, (reach + 1) * lon_dev)
    arrays, order = [own], [reach]
    ahead = behind = own
    for step in range(1, reach + 1):
        ahead = shift_by(ahead, "lon", -1)
        behind = shift_by(behind, "lon", 1)
        arrays += [ahead, behind]
        order += [reach + step, reach - step]
    sectors = jnp.array(order, jnp.int32)
    return filter_rows(rows, slots, sectors, widths, lines, arrays, reach)


def solution(mesh):
    in_specs = (P("lat", "lon", None), P(), P(), P())
    out_specs = P("lat", "lon", None)
    chips = (mesh.shape["lon"], mesh.shape["lat"]) == (16, 2)

    def body(fields, owner_slot, widths, tap_weights):
        fits = chips and fields.shape[0] == 4 * sum(STAY)
        form = chip_aware if fits else any_mesh
        return form(fields, owner_slot, widths, tap_weights)

    return jax.shard_map(body, mesh=mesh, in_specs=in_specs, out_specs=out_specs, check_vma=False)
```

```python
import functools

import jax
import jax.numpy as jnp
from jax import lax
from jax.experimental import pallas as pl
from jax.experimental.pallas import tpu as pltpu
from jax.sharding import PartitionSpec as P

VMEM_LIMIT = 12 * 1024 * 1024
SMEM_SPEC = pl.BlockSpec(memory_space=pltpu.SMEM)
VMEM_SPEC = pl.BlockSpec(memory_space=pltpu.VMEM)
HBM_SPEC = pl.BlockSpec(memory_space=pltpu.HBM)
STAY = (2, 2)
COME = (2, 2)
PARTS = [("y", 0), ("y", 1), ("y", 2), ("y", 3)]
FILTERS = ((4, 5), (6, 7))
WAITS = {
    ("x", 0): [("p", 0), ("y", 0)],
    ("x", 1): [("p", 1)],
    ("b", 2): [("x", 3)],
    ("q", 2): [("q", 0)],
    ("q", 3): [("q", 1)],
    ("z", 0): [("q", 2), ("q", 1)],
    ("z", 1): [("q", 3), ("t", 1)],
    ("z", 2): [("z", 0)],
    ("z", 3): [("z", 1)],
    ("y", 2): [("y", 0), ("p", 0)],
    ("y", 3): [("y", 1), ("x", 0)],
    ("y", 1): [("q", 0)],
}
FLOPS = 3


def up_to(value, multiple):
    return -(-value // multiple) * multiple


def shift_by(x, axis, by):
    count = lax.axis_size(axis)
    return lax.ppermute(x, axis, [(i, (i + by) % count) for i in range(count)])


def line_kernel(behind, taps_ref, line_ref):
    circle = taps_ref.shape[1]
    rows, lanes = line_ref.shape
    taps = taps_ref[...].astype(jnp.float32)
    pieces = [taps[:, circle - behind :], taps[:, :behind]]
    if lanes > 2 * behind:
        pieces.append(jnp.zeros((rows, lanes - 2 * behind), jnp.float32))
    line_ref[...] = jnp.concatenate(pieces, axis=1)


def tap_lines(tap_weights, behind):
    rows = tap_weights.shape[0]
    lanes = up_to(2 * behind, 128)
    return pl.pallas_call(
        functools.partial(line_kernel, behind),
        out_shape=jax.ShapeDtypeStruct((rows, lanes), jnp.float32),
        in_specs=[VMEM_SPEC],
        out_specs=VMEM_SPEC,
        compiler_params=pltpu.CompilerParams(vmem_limit_bytes=VMEM_LIMIT),
        cost_estimate=pl.CostEstimate(flops=0, bytes_accessed=2 * tap_weights.size, transcendentals=0),
        name="tap_lines",
    )(tap_weights)


def active_line(line_ref, row, width, behind):
    line = jnp.broadcast_to(line_ref[pl.ds(row, 1), :], (8, line_ref.shape[1]))
    distance = jnp.abs(lax.broadcasted_iota(jnp.int32, line.shape, 1) - behind)
    return jnp.where(distance <= width, line, 0.0)


def toeplitz(line, at, lon_dev, width):
    lanes = up_to(width, 128) + 128
    step = min(up_to(lon_dev, 16), 96)
    bands = []
    for start in range(0, up_to(lon_dev, step), step):
        taps = pltpu.roll(line, line.shape[1] + start - at, 1)
        taps = jnp.concatenate([taps[:, : lanes - 128], taps[:, -128:]], axis=1)
        band = pltpu.roll(jnp.concatenate([taps] * (step // 8), axis=0), 0, 1, stride=1, stride_axis=0)
        bands.append(band[:, :width].astype(jnp.bfloat16))
    return jnp.concatenate(bands, axis=0)


def take_kernel(chunks, lat_dev, block, place_ref, fields_ref, *refs):
    outs = refs[: len(chunks)]
    rows_ref, slots_ref, home_ref, take_ref = refs[len(chunks) :]
    lon_dev, _, channels = fields_ref.shape
    half, quarter = lat_dev // 2, lat_dev // 4
    starts = list(range(0, lon_dev, block))
    band, core, x = place_ref[0], place_ref[1], place_ref[2]

    def at(n):
        within = n % quarter
        return within + jnp.where(n // quarter == core, 0, quarter)

    def traded(n):
        within = n % quarter
        return n - within + (within + quarter // 2 * x) % quarter

    stay, leave, come = jnp.int32(0), jnp.int32(0), jnp.int32(0)
    for j in range(lat_dev):
        here = band * lat_dev + j
        there = (1 - band) * lat_dev + j
        stays = place_ref[3 + here] // lat_dev == band
        comes = place_ref[3 + there] // lat_dev == band
        home_ref[jnp.where(stays, traded(at(stay)), half + at(leave))] = jnp.int32(j)

        @pl.when(stays)
        def _():
            spot = traded(at(stay))
            spot = spot + jnp.where(spot >= quarter, quarter, 0)
            rows_ref[spot] = here
            slots_ref[spot] = place_ref[3 + here] % lat_dev

        @pl.when(comes)
        def _():
            spot = at(come)
            spot = spot + jnp.where(spot >= quarter, half, quarter)
            rows_ref[spot] = there
            slots_ref[spot] = place_ref[3 + there] % lat_dev

        stay = stay + stays.astype(jnp.int32)
        leave = leave + 1 - stays.astype(jnp.int32)
        come = come + comes.astype(jnp.int32)

    def selector(lon):
        row = lax.broadcasted_iota(jnp.int32, (lat_dev * lon, 128), 0)
        wanted = row % lon * lat_dev
        for p in range(lat_dev):
            wanted += jnp.where(row // lon == p, home_ref[p], 0)
        column = lax.broadcasted_iota(jnp.int32, (lat_dev * lon, lon * lat_dev), 1)
        return jnp.where(column == wanted[:, :1], 1.0, 0.0).astype(jnp.bfloat16)

    take_ref[...] = selector(block)
    for start in starts:
        lon = min(block, lon_dev - start)
        panel = fields_ref[start : start + lon].reshape(lon * lat_dev, channels)
        take = take_ref[...] if lon == block else selector(lon)
        taken = jnp.dot(take, panel, preferred_element_type=jnp.float32)
        place = 0
        for out, count in zip(outs, chunks):
            for i in range(count):
                piece = taken[place * lon : (place + 1) * lon].astype(out.dtype)
                out[i * lon_dev + start : i * lon_dev + start + lon, :] = piece
                place += 1


def take_rows(fields, place, chunks):
    lon_dev, lat_dev, channels = fields.shape
    block = 16
    ints = jax.ShapeDtypeStruct((lat_dev,), jnp.int32)
    result = pl.pallas_call(
        functools.partial(take_kernel, chunks, lat_dev, block),
        out_shape=[jax.ShapeDtypeStruct((n * lon_dev, channels), fields.dtype) for n in chunks] + [ints, ints],
        in_specs=[SMEM_SPEC, VMEM_SPEC],
        out_specs=[VMEM_SPEC] * len(chunks) + [SMEM_SPEC, SMEM_SPEC],
        scratch_shapes=[
            pltpu.SMEM((lat_dev,), jnp.int32),
            pltpu.VMEM((block * lat_dev, block * lat_dev), jnp.bfloat16),
        ],
        compiler_params=pltpu.CompilerParams(vmem_limit_bytes=VMEM_LIMIT),
        cost_estimate=pl.CostEstimate(
            flops=2 * fields.size * block * lat_dev, bytes_accessed=4 * fields.size, transcendentals=0
        ),
        name="take_rows",
    )(place, fields)
    return result[:-2], result[-2], result[-1]


def put_kernel(counts, lat_dev, block, slots_ref, *refs):
    ins, (out_ref, panel_ref, sems) = refs[:-3], refs[-3:]
    lon_dev, _, channels = out_ref.shape

    def selector(lon):
        row = lax.broadcasted_iota(jnp.int32, (lon * lat_dev, lat_dev * lon), 0)
        column = lax.broadcasted_iota(jnp.int32, (8, lat_dev * lon), 1)
        wanted = column % lon * lat_dev
        for p in range(lat_dev):
            wanted += jnp.where(column // lon == p, slots_ref[p], 0)
        return jnp.where(row == wanted[:1], 1.0, 0.0).astype(jnp.bfloat16)

    whole = selector(block)
    copies = []
    for n, start in enumerate(range(0, lon_dev, block)):
        lon = min(block, lon_dev - start)
        pieces = [r[i * lon_dev + start : i * lon_dev + start + lon, :] for r, count in zip(ins, counts) for i in range(count)]
        if lon < block:
            pieces = [p.astype(jnp.float32) for p in pieces]
        panel = jnp.concatenate(pieces, axis=0).astype(jnp.bfloat16)
        spread = jnp.dot(whole if lon == block else selector(lon), panel, preferred_element_type=jnp.float32)
        window = pl.ds(start, lon)
        panel_ref[window] = spread.astype(jnp.bfloat16).reshape(lon, lat_dev, channels)
        copies.append(pltpu.make_async_copy(panel_ref.at[window], out_ref.at[window], sems.at[n]))
        copies[-1].start()
    for copy in copies:
        copy.wait()


def put_rows(panels, slots, lon_dev, lat_dev):
    channels = panels[0].shape[1]
    block = 16
    counts = tuple(p.shape[0] // lon_dev for p in panels)
    shape = (lon_dev, lat_dev, channels)
    return pl.pallas_call(
        functools.partial(put_kernel, counts, lat_dev, block),
        out_shape=jax.ShapeDtypeStruct(shape, panels[0].dtype),
        in_specs=[SMEM_SPEC] + [VMEM_SPEC] * len(panels),
        out_specs=HBM_SPEC,
        scratch_shapes=[
            pltpu.VMEM(shape, panels[0].dtype),
            pltpu.SemaphoreType.DMA((pl.cdiv(lon_dev, block),)),
        ],
        compiler_params=pltpu.CompilerParams(vmem_limit_bytes=VMEM_LIMIT),
        cost_estimate=pl.CostEstimate(
            flops=2 * lon_dev * lat_dev * channels * block * lat_dev,
            bytes_accessed=4 * lon_dev * lat_dev * channels,
            transcendentals=0,
        ),
        name="put_rows",
    )(slots, *panels)


def pair_kernel(lon_dev, base, plan, phase, rows_ref, place_ref, widths_ref, *refs):
    count = len(plan)
    side, along = 1 - 2 * place_ref[1], 1 - 2 * place_ref[2]
    if phase == "late":
        (total_in, block_ref), refs = refs[:2], refs[2:]
    else:
        line_ref, refs = refs[0], refs[1:]
    if phase == "early":
        ins, (total_ref, block_ref) = refs[:-2], refs[-2:]
    elif phase == "late":
        ins, (out_own, out_other) = refs[:-2], refs[-2:]
    else:
        ins, (out_own, out_other, block_ref) = refs[:-3], refs[-3:]
    channels = ins[0].shape[1]

    def both(first, second):
        return jnp.concatenate([first[...], second[...]], axis=1)

    for n, places in enumerate(plan):
        panels = [ins[array].at[pl.ds(i * lon_dev, lon_dev), :] for array, i in places]

        def times(offset, panel):
            return jnp.dot(block_ref[n, 2 + offset], panel, preferred_element_type=jnp.float32)[:lon_dev]

        def halves(first, second):
            return jnp.concatenate([first, second], axis=1)

        nothing = jnp.zeros((lon_dev, channels), jnp.float32)
        same = side == along
        if phase != "late":
            own, other, x_own, x_other = panels[:4]
            row = rows_ref[base + n]
            line = active_line(line_ref, row, widths_ref[row], 3 * lon_dev)
            for s in range(5):
                block_ref[n, s] = toeplitz(line, (s + 1) * lon_dev, lon_dev, lon_dev)
            here = both(own, other)
            total = here.astype(jnp.float32) + times(0, here)
            total += times(2 * along, both(x_own, x_other))
            total += jnp.concatenate([times(side, other[...]), times(-side, own[...])], axis=1)
            more = times(along, jnp.where(same, x_own[...], x_other[...]))
            total += halves(jnp.where(same, nothing, more), jnp.where(same, more, nothing))
            if phase == "early":
                total_ref[n] = total
        if phase != "early":
            z_own, z_other = panels[-2:]
            if phase == "late":
                total = total_in[n]
            total += times(-2 * along, both(z_own, z_other))
            more = times(-along, jnp.where(same, z_other[...], z_own[...]))
            total += halves(jnp.where(same, more, nothing), jnp.where(same, nothing, more))
            here = pl.ds(n * lon_dev, lon_dev)
            out_own[here, :] = total[:, :channels].astype(out_own.dtype)
            out_other[here, :] = total[:, channels:].astype(out_other.dtype)


def filter_pair(scalars, lines, places, base, lon_dev, phase="whole", early=()):
    arrays = []
    plan = []
    for row in places:
        found = []
        for array, i in row:
            at = next((n for n, a in enumerate(arrays) if a is array), len(arrays))
            if at == len(arrays):
                arrays.append(array)
            found.append((at, i))
        plan.append(tuple(found))
    count = len(plan)
    channels = arrays[0].shape[1]
    total = (count, lon_dev, 2 * channels), jnp.float32
    block = (count, 5, up_to(lon_dev, 96), lon_dev), jnp.bfloat16
    out = jax.ShapeDtypeStruct((count * lon_dev, channels), arrays[0].dtype)
    first = [lines] if phase != "late" else list(early)
    if phase == "early":
        outs, scratch = [jax.ShapeDtypeStruct(*total), jax.ShapeDtypeStruct(*block)], []
    elif phase == "late":
        outs, scratch = [out, out], []
    else:
        outs, scratch = [out, out], [pltpu.VMEM(*block)]
    weight = {"whole": 10, "early": 7, "late": 3}[phase]
    return pl.pallas_call(
        functools.partial(pair_kernel, lon_dev, base, tuple(plan), phase),
        out_shape=outs,
        in_specs=[SMEM_SPEC] * 3 + [VMEM_SPEC] * (len(first) + len(arrays)),
        out_specs=[VMEM_SPEC] * len(outs),
        scratch_shapes=scratch,
        compiler_params=pltpu.CompilerParams(vmem_limit_bytes=VMEM_LIMIT),
        cost_estimate=pl.CostEstimate(
            flops=FLOPS * count * weight * 256 * 256 * 768,
            bytes_accessed=16 * count * lon_dev * channels,
            transcendentals=0,
        ),
        name="filter_" + phase,
    )(*scalars, *first, *arrays)


def chip_aware(fields, owner_slot, widths, tap_weights):
    lat_dev, lon_dev, channels = fields.shape
    n_lon = lax.axis_size("lon")
    at = lax.axis_index("lon")
    band = lax.axis_index("lat")
    core, x = at % 2, at // 2 % 2
    place = jnp.concatenate([jnp.stack([band, core, x]).astype(jnp.int32), owner_slot])
    chunks = STAY + STAY + COME + COME
    taken, rows, slots = take_rows(jnp.transpose(fields, (1, 0, 2)), place, chunks)
    n_stay, n_come = len(STAY), len(COME)
    keep, give = taken[:n_stay], taken[n_stay : 2 * n_stay]
    straight, cross = taken[2 * n_stay : 2 * n_stay + n_come], taken[2 * n_stay + n_come :]

    across_core = [(i, i ^ 1) for i in range(n_lon)]
    across_x = [(i, i ^ 2) for i in range(n_lon)]
    across_x_core = [(i, i ^ 3) for i in range(n_lon)]
    across_z = [(i, (i + (4 if i // 2 % 2 == 0 else -4)) % n_lon) for i in range(n_lon)]
    back_z = [(i, (i + (-4 if i // 2 % 2 == 0 else 4)) % n_lon) for i in range(n_lon)]
    across_y = [(i, i ^ 1) for i in range(2 * n_lon)]
    across_both = [(i, i ^ 3) for i in range(2 * n_lon)]

    lines = tap_lines(tap_weights, 3 * lon_dev)
    scalars = rows, place, widths
    sizes = STAY + COME
    starts = [sum(sizes[:c]) for c in range(len(sizes))]
    done = {}

    def get(kind, i):
        if (kind, i) in done:
            return done[kind, i]

        def moved(operand, axes, pairs):
            first = [get(*g)[0] if g[0] in "ft" else get(*g) for g in WAITS.get((kind, i), ())]
            if first:
                operand = lax.optimization_barrier((operand, *first))[0]
            return lax.ppermute(operand, axes, pairs)

        if kind == "k":
            result = keep[i]
        elif kind == "c":
            result = moved(give[i], "lon", across_core)
        elif kind == "y":
            operand, pairs = ((straight, across_y), (cross, across_both))[i % 2]
            result = moved(operand[i // 2], ("lon", "lat"), pairs)
        elif kind == "x":
            result = moved(get(*PARTS[i]), "lon", across_x)
        elif kind == "z":
            result = moved(get("x", i), "lon", across_z)
        elif kind == "p":
            operand, pairs = ((keep[1], across_x), (give[1], across_x_core))[i]
            result = moved(operand, "lon", pairs)
        elif kind == "q":
            operand = get(*(("k", 0), ("c", 0), ("p", 0), ("p", 1))[i])
            result = moved(operand, "lon", back_z if i < 2 else across_z)
        elif kind == "t":
            here = [get("k", 0), get("c", 0)]
            beside = [get("p", 0), get("p", 1)]
            if i == 0:
                panels = here + beside + [get("q", 2), get("q", 3)]
            else:
                panels = beside + [get("q", 0), get("q", 1)] + here
            places = [[(p, row) for p in panels] for row in range(STAY[0])]
            result = filter_pair(scalars, lines, places, 0, lon_dev)
        elif kind == "b":
            operand, pairs = ((get("t", 0)[1], across_core), (get("t", 1)[0], across_x), (get("t", 1)[1], across_x_core))[i]
            result = moved(operand, "lon", pairs)
        elif kind == "f":
            places = []
            for row in FILTERS[i]:
                chunk, index = next((c, row - at) for c, at in enumerate(starts) if at <= row < at + sizes[c])
                if chunk < n_stay:
                    pair = ("k", chunk), ("c", chunk)
                else:
                    pair = ("y", 2 * (chunk - n_stay)), ("y", 2 * (chunk - n_stay) + 1)
                parts = [get(*p) for p in pair]
                parts += [get(axis, PARTS.index(p)) for axis in "xz" for p in pair]
                places.append([(p, index) for p in parts])
            base = FILTERS[i][0]
            if i < len(FILTERS) - 1:
                result = filter_pair(scalars, lines, places, base, lon_dev)
            else:
                early = filter_pair(scalars, lines, [p[:4] for p in places], base, lon_dev, "early")
                result = filter_pair(scalars, lines, [p[4:] for p in places], base, lon_dev, "late", early)
        else:
            result = moved(get("f", i)[1], "lon", across_core)
        done[kind, i] = result
        return result

    mine = [get("t", 0)[0], get("b", 1)] + [get("f", i)[0] for i in range(len(FILTERS))]
    theirs = [get("b", 0), get("b", 2)] + [get("o", i) for i in range(len(FILTERS))]
    out = put_rows(mine + theirs, slots, lon_dev, lat_dev)
    return jnp.transpose(out, (1, 0, 2))


def filter_kernel(reach, rows_ref, slots_ref, sector_ref, widths_ref, line_ref, *refs):
    ins, out_ref = refs[:-1], refs[-1]
    lon_dev, channels = out_ref.shape[1:]
    row = rows_ref[pl.program_id(0)]
    line = active_line(line_ref, row, widths_ref[row], (reach + 1) * lon_dev)
    total = ins[0][0].astype(jnp.float32)
    for group, ref in enumerate(ins):
        block = toeplitz(line, (sector_ref[group] + 1) * lon_dev, lon_dev, lon_dev)
        total += jnp.dot(block, ref[0], preferred_element_type=jnp.float32)[:lon_dev]
    out_ref[0] = total.astype(out_ref.dtype)


def filter_rows(rows, slots, sectors, widths, lines, arrays, reach):
    lat_dev, lon_dev, channels = arrays[0].shape
    row_spec = pl.BlockSpec((1, lon_dev, channels), lambda i, rows, slots, sectors, widths: (i, 0, 0))
    line_spec = pl.BlockSpec(lines.shape, lambda i, rows, slots, sectors, widths: (0, 0))
    out_spec = pl.BlockSpec((1, lon_dev, channels), lambda i, rows, slots, sectors, widths: (slots[i], 0, 0))
    return pl.pallas_call(
        functools.partial(filter_kernel, reach),
        out_shape=jax.ShapeDtypeStruct(arrays[0].shape, arrays[0].dtype),
        grid_spec=pltpu.PrefetchScalarGridSpec(
            num_scalar_prefetch=4,
            grid=(lat_dev,),
            in_specs=[line_spec] + [row_spec] * len(arrays),
            out_specs=out_spec,
        ),
        compiler_params=pltpu.CompilerParams(vmem_limit_bytes=VMEM_LIMIT),
        name="filter_rows",
    )(rows, slots, sectors, widths, lines, *arrays)


def any_mesh(fields, owner_slot, widths, tap_weights):
    lat_dev, lon_dev, channels = fields.shape
    n_lon = lax.axis_size("lon")
    n_lat = lax.axis_size("lat")
    reach = n_lon // 8
    band = lax.axis_index("lat")
    dest_band = owner_slot // lat_dev
    home_rows = band * lat_dev + jnp.arange(lat_dev, dtype=jnp.int32)
    ordering = jnp.argsort(dest_band[home_rows], stable=True)
    rows = jnp.argsort((dest_band != band).astype(jnp.int32), stable=True)[:lat_dev].astype(jnp.int32)
    slots = (owner_slot[rows] % lat_dev).astype(jnp.int32)
    outgoing = fields[ordering].reshape(n_lat, lat_dev // n_lat, lon_dev, channels)
    incoming = lax.all_to_all(outgoing, "lat", split_axis=0, concat_axis=0, tiled=True)
    own = incoming.reshape(lat_dev, lon_dev, channels)
    lines = tap_lines(tap_weights, (reach + 1) * lon_dev)
    arrays, order = [own], [reach]
    ahead = behind = own
    for step in range(1, reach + 1):
        ahead = shift_by(ahead, "lon", -1)
        behind = shift_by(behind, "lon", 1)
        arrays += [ahead, behind]
        order += [reach + step, reach - step]
    sectors = jnp.array(order, jnp.int32)
    return filter_rows(rows, slots, sectors, widths, lines, arrays, reach)


def solution(mesh):
    in_specs = (P("lat", "lon", None), P(), P(), P())
    out_specs = P("lat", "lon", None)
    chips = (mesh.shape["lon"], mesh.shape["lat"]) == (16, 2)

    def body(fields, owner_slot, widths, tap_weights):
        fits = chips and fields.shape[0] == 4 * sum(STAY)
        form = chip_aware if fits else any_mesh
        return form(fields, owner_slot, widths, tap_weights)

    return jax.shard_map(body, mesh=mesh, in_specs=in_specs, out_specs=out_specs, check_vma=False)
```

```python
import functools

import jax
import jax.numpy as jnp
from jax import lax
from jax.experimental import pallas as pl
from jax.experimental.pallas import tpu as pltpu
from jax.sharding import PartitionSpec as P

VMEM_LIMIT = 12 * 1024 * 1024
TAKE_VMEM_LIMIT = 50 * 1024 * 1024
PIECE = 3
AHEAD = 2
SMEM_SPEC = pl.BlockSpec(memory_space=pltpu.SMEM)
VMEM_SPEC = pl.BlockSpec(memory_space=pltpu.VMEM)
HBM_SPEC = pl.BlockSpec(memory_space=pltpu.HBM)
STAY = (2, 2)
COME = (2, 2)
PARTS = [("y", 0), ("y", 1), ("y", 2), ("y", 3)]
FILTERS = ((4, 5), (6, 7))
WAITS = {
    ("x", 0): [("p", 0), ("y", 0)],
    ("x", 1): [("p", 1)],
    ("b", 2): [("x", 3)],
    ("q", 2): [("q", 0)],
    ("q", 3): [("q", 1)],
    ("z", 0): [("q", 2), ("q", 1)],
    ("z", 1): [("q", 3), ("t", 1)],
    ("z", 2): [("z", 0)],
    ("z", 3): [("z", 1)],
    ("y", 2): [("y", 0), ("p", 0)],
    ("y", 3): [("y", 1), ("x", 0)],
    ("y", 1): [("q", 0)],
}
FLOPS = 3


def up_to(value, multiple):
    return -(-value // multiple) * multiple


def shift_by(x, axis, by):
    count = lax.axis_size(axis)
    return lax.ppermute(x, axis, [(i, (i + by) % count) for i in range(count)])


def line_kernel(behind, taps_ref, line_ref):
    circle = taps_ref.shape[1]
    rows, lanes = line_ref.shape
    taps = taps_ref[...].astype(jnp.float32)
    pieces = [taps[:, circle - behind :], taps[:, :behind]]
    if lanes > 2 * behind:
        pieces.append(jnp.zeros((rows, lanes - 2 * behind), jnp.float32))
    line_ref[...] = jnp.concatenate(pieces, axis=1)


def tap_lines(tap_weights, behind):
    rows = tap_weights.shape[0]
    lanes = up_to(2 * behind, 128)
    return pl.pallas_call(
        functools.partial(line_kernel, behind),
        out_shape=jax.ShapeDtypeStruct((rows, lanes), jnp.float32),
        in_specs=[VMEM_SPEC],
        out_specs=VMEM_SPEC,
        compiler_params=pltpu.CompilerParams(vmem_limit_bytes=VMEM_LIMIT),
        cost_estimate=pl.CostEstimate(flops=0, bytes_accessed=2 * tap_weights.size, transcendentals=0),
        name="tap_lines",
    )(tap_weights)


def active_line(line_ref, row, width, behind):
    line = jnp.broadcast_to(line_ref[pl.ds(row, 1), :], (8, line_ref.shape[1]))
    distance = jnp.abs(lax.broadcasted_iota(jnp.int32, line.shape, 1) - behind)
    return jnp.where(distance <= width, line, 0.0)


def toeplitz(line, at, lon_dev, width):
    lanes = up_to(width, 128) + 128
    step = min(up_to(lon_dev, 16), 96)
    bands = []
    for start in range(0, up_to(lon_dev, step), step):
        taps = pltpu.roll(line, line.shape[1] + start - at, 1)
        taps = jnp.concatenate([taps[:, : lanes - 128], taps[:, -128:]], axis=1)
        band = pltpu.roll(jnp.concatenate([taps] * (step // 8), axis=0), 0, 1, stride=1, stride_axis=0)
        bands.append(band[:, :width].astype(jnp.bfloat16))
    return jnp.concatenate(bands, axis=0)


def listed(n, quarter, core):
    within = n % quarter
    return within + jnp.where(n // quarter == core, 0, quarter)


def traded(n, quarter, x):
    within = n % quarter
    return n - within + (within + quarter // 2 * x) % quarter


def list_kernel(lat_dev, place_ref, rows_ref, slots_ref):
    half, quarter = lat_dev // 2, lat_dev // 4
    band, core, x = place_ref[0], place_ref[1], place_ref[2]
    stay, come = jnp.int32(0), jnp.int32(0)
    for j in range(lat_dev):
        here = band * lat_dev + j
        there = (1 - band) * lat_dev + j
        stays = place_ref[3 + here] // lat_dev == band
        comes = place_ref[3 + there] // lat_dev == band

        @pl.when(stays)
        def _():
            spot = traded(listed(stay, quarter, core), quarter, x)
            spot = spot + jnp.where(spot >= quarter, quarter, 0)
            rows_ref[spot] = here
            slots_ref[spot] = place_ref[3 + here] % lat_dev

        @pl.when(comes)
        def _():
            spot = listed(come, quarter, core)
            spot = spot + jnp.where(spot >= quarter, half, quarter)
            rows_ref[spot] = there
            slots_ref[spot] = place_ref[3 + there] % lat_dev

        stay = stay + stays.astype(jnp.int32)
        come = come + comes.astype(jnp.int32)


def list_rows(place, lat_dev):
    ints = jax.ShapeDtypeStruct((lat_dev,), jnp.int32)
    return pl.pallas_call(
        functools.partial(list_kernel, lat_dev),
        out_shape=[ints, ints],
        in_specs=[SMEM_SPEC],
        out_specs=[SMEM_SPEC, SMEM_SPEC],
        compiler_params=pltpu.CompilerParams(vmem_limit_bytes=VMEM_LIMIT),
        cost_estimate=pl.CostEstimate(flops=0, bytes_accessed=256, transcendentals=0),
        name="list_rows",
    )(place)


def take_kernel(chunks, lat_dev, block, place_ref, fields_ref, *refs):
    outs = refs[: len(chunks)]
    home_ref, take_ref, panel_ref, sems = refs[len(chunks) :]
    lon_dev, _, channels = fields_ref.shape
    half, quarter = lat_dev // 2, lat_dev // 4
    copies = []
    for n, start in enumerate(range(0, lon_dev, PIECE * block)):
        window = pl.ds(start, min(PIECE * block, lon_dev - start))
        copies.append(pltpu.make_async_copy(fields_ref.at[window], panel_ref.at[window], sems.at[n]))
    for copy in copies[:AHEAD]:
        copy.start()

    band, core, x = place_ref[0], place_ref[1], place_ref[2]
    stay, leave = jnp.int32(0), jnp.int32(0)
    for j in range(lat_dev):
        stays = place_ref[3 + band * lat_dev + j] // lat_dev == band
        spot = traded(listed(stay, quarter, core), quarter, x)
        home_ref[jnp.where(stays, spot, half + listed(leave, quarter, core))] = jnp.int32(j)
        stay = stay + stays.astype(jnp.int32)
        leave = leave + 1 - stays.astype(jnp.int32)

    def selector(lon):
        row = lax.broadcasted_iota(jnp.int32, (lat_dev * lon, 128), 0)
        if lon % 8 == 0:
            home = jnp.concatenate([jnp.full((lon, 128), home_ref[p], jnp.int32) for p in range(lat_dev)], axis=0)
        else:
            home = sum(jnp.where(row // lon == p, home_ref[p], 0) for p in range(lat_dev))
        wanted = row % lon * lat_dev + home
        column = lax.broadcasted_iota(jnp.int32, (lat_dev * lon, lon * lat_dev), 1)
        return jnp.where(column == wanted[:, :1], 1.0, 0.0).astype(jnp.bfloat16)

    take_ref[...] = selector(block)
    rest = lon_dev % block
    small = selector(rest) if rest else None
    for n, start in enumerate(range(0, lon_dev, block)):
        if n % PIECE == 0:
            copies[n // PIECE].wait()
            if n // PIECE + AHEAD < len(copies):
                copies[n // PIECE + AHEAD].start()
        lon = min(block, lon_dev - start)
        panel = panel_ref[start : start + lon].reshape(lon * lat_dev, channels)
        take = take_ref[...] if lon == block else small
        taken = jnp.dot(take, panel, preferred_element_type=jnp.float32)
        place = 0
        for out, count in zip(outs, chunks):
            for i in range(count):
                piece = taken[place * lon : (place + 1) * lon].astype(out.dtype)
                out[i * lon_dev + start : i * lon_dev + start + lon, :] = piece
                place += 1


def take_rows(fields, place, chunks):
    lon_dev, lat_dev, channels = fields.shape
    block = 16
    return pl.pallas_call(
        functools.partial(take_kernel, chunks, lat_dev, block),
        out_shape=[jax.ShapeDtypeStruct((n * lon_dev, channels), fields.dtype) for n in chunks],
        in_specs=[SMEM_SPEC, HBM_SPEC],
        out_specs=[VMEM_SPEC] * len(chunks),
        scratch_shapes=[
            pltpu.SMEM((lat_dev,), jnp.int32),
            pltpu.VMEM((block * lat_dev, block * lat_dev), jnp.bfloat16),
            pltpu.VMEM(fields.shape, fields.dtype),
            pltpu.SemaphoreType.DMA((pl.cdiv(lon_dev, PIECE * block),)),
        ],
        compiler_params=pltpu.CompilerParams(vmem_limit_bytes=TAKE_VMEM_LIMIT),
        cost_estimate=pl.CostEstimate(
            flops=2 * fields.size * block * lat_dev, bytes_accessed=4 * fields.size, transcendentals=0
        ),
        name="take_rows",
    )(place, fields)


def put_kernel(counts, lat_dev, block, slots_ref, *refs):
    ins, (out_ref, panel_ref, sems) = refs[:-3], refs[-3:]
    lon_dev, _, channels = out_ref.shape

    def selector(lon):
        row = lax.broadcasted_iota(jnp.int32, (lon * lat_dev, lat_dev * lon), 0)
        column = lax.broadcasted_iota(jnp.int32, (8, lat_dev * lon), 1)
        wanted = column % lon * lat_dev
        for p in range(lat_dev):
            wanted += jnp.where(column // lon == p, slots_ref[p], 0)
        return jnp.where(row == wanted[:1], 1.0, 0.0).astype(jnp.bfloat16)

    whole = selector(block)
    rest = lon_dev % block
    small = selector(rest) if rest else None
    copies = []
    for n, start in enumerate(range(0, lon_dev, block)):
        lon = min(block, lon_dev - start)
        pieces = [r[i * lon_dev + start : i * lon_dev + start + lon, :] for r, count in zip(ins, counts) for i in range(count)]
        if lon < block:
            pieces = [p.astype(jnp.float32) for p in pieces]
        panel = jnp.concatenate(pieces, axis=0).astype(jnp.bfloat16)
        spread = jnp.dot(whole if lon == block else small, panel, preferred_element_type=jnp.float32)
        window = pl.ds(start, lon)
        panel_ref[window] = spread.astype(jnp.bfloat16).reshape(lon, lat_dev, channels)
        copies.append(pltpu.make_async_copy(panel_ref.at[window], out_ref.at[window], sems.at[n]))
        copies[-1].start()
    for copy in copies:
        copy.wait()


def put_rows(panels, slots, lon_dev, lat_dev):
    channels = panels[0].shape[1]
    block = 16
    counts = tuple(p.shape[0] // lon_dev for p in panels)
    shape = (lon_dev, lat_dev, channels)
    return pl.pallas_call(
        functools.partial(put_kernel, counts, lat_dev, block),
        out_shape=jax.ShapeDtypeStruct(shape, panels[0].dtype),
        in_specs=[SMEM_SPEC] + [VMEM_SPEC] * len(panels),
        out_specs=HBM_SPEC,
        scratch_shapes=[
            pltpu.VMEM(shape, panels[0].dtype),
            pltpu.SemaphoreType.DMA((pl.cdiv(lon_dev, block),)),
        ],
        compiler_params=pltpu.CompilerParams(vmem_limit_bytes=VMEM_LIMIT),
        cost_estimate=pl.CostEstimate(
            flops=2 * lon_dev * lat_dev * channels * block * lat_dev,
            bytes_accessed=4 * lon_dev * lat_dev * channels,
            transcendentals=0,
        ),
        name="put_rows",
    )(slots, *panels)


def pair_kernel(lon_dev, base, plan, phase, rows_ref, place_ref, widths_ref, *refs):
    count = len(plan)
    side, along = 1 - 2 * place_ref[1], 1 - 2 * place_ref[2]
    if phase == "late":
        (total_in, block_ref), refs = refs[:2], refs[2:]
    else:
        line_ref, refs = refs[0], refs[1:]
    if phase == "early":
        ins, (total_ref, block_ref) = refs[:-2], refs[-2:]
    elif phase == "late":
        ins, (out_own, out_other) = refs[:-2], refs[-2:]
    else:
        ins, (out_own, out_other, block_ref) = refs[:-3], refs[-3:]
    channels = ins[0].shape[1]

    def both(first, second):
        return jnp.concatenate([first[...], second[...]], axis=1)

    for n, places in enumerate(plan):
        panels = [ins[array].at[pl.ds(i * lon_dev, lon_dev), :] for array, i in places]

        def times(offset, panel):
            return jnp.dot(block_ref[n, 2 + offset], panel, preferred_element_type=jnp.float32)[:lon_dev]

        def halves(first, second):
            return jnp.concatenate([first, second], axis=1)

        nothing = jnp.zeros((lon_dev, channels), jnp.float32)
        same = side == along
        if phase != "late":
            own, other, x_own, x_other = panels[:4]
            row = rows_ref[base + n]
            line = active_line(line_ref, row, widths_ref[row], 3 * lon_dev)
            for s in range(5):
                block_ref[n, s] = toeplitz(line, (s + 1) * lon_dev, lon_dev, lon_dev)
            here = both(own, other)
            total = here.astype(jnp.float32) + times(0, here)
            total += times(2 * along, both(x_own, x_other))
            total += jnp.concatenate([times(side, other[...]), times(-side, own[...])], axis=1)
            more = times(along, jnp.where(same, x_own[...], x_other[...]))
            total += halves(jnp.where(same, nothing, more), jnp.where(same, more, nothing))
            if phase == "early":
                total_ref[n] = total
        if phase != "early":
            z_own, z_other = panels[-2:]
            if phase == "late":
                total = total_in[n]
            total += times(-2 * along, both(z_own, z_other))
            more = times(-along, jnp.where(same, z_other[...], z_own[...]))
            total += halves(jnp.where(same, more, nothing), jnp.where(same, nothing, more))
            here = pl.ds(n * lon_dev, lon_dev)
            out_own[here, :] = total[:, :channels].astype(out_own.dtype)
            out_other[here, :] = total[:, channels:].astype(out_other.dtype)


def filter_pair(scalars, lines, places, base, lon_dev, phase="whole", early=()):
    arrays = []
    plan = []
    for row in places:
        found = []
        for array, i in row:
            at = next((n for n, a in enumerate(arrays) if a is array), len(arrays))
            if at == len(arrays):
                arrays.append(array)
            found.append((at, i))
        plan.append(tuple(found))
    count = len(plan)
    channels = arrays[0].shape[1]
    total = (count, lon_dev, 2 * channels), jnp.float32
    block = (count, 5, up_to(lon_dev, 96), lon_dev), jnp.bfloat16
    out = jax.ShapeDtypeStruct((count * lon_dev, channels), arrays[0].dtype)
    first = [lines] if phase != "late" else list(early)
    if phase == "early":
        outs, scratch = [jax.ShapeDtypeStruct(*total), jax.ShapeDtypeStruct(*block)], []
    elif phase == "late":
        outs, scratch = [out, out], []
    else:
        outs, scratch = [out, out], [pltpu.VMEM(*block)]
    weight = {"whole": 10, "early": 7, "late": 3}[phase]
    return pl.pallas_call(
        functools.partial(pair_kernel, lon_dev, base, tuple(plan), phase),
        out_shape=outs,
        in_specs=[SMEM_SPEC] * 3 + [VMEM_SPEC] * (len(first) + len(arrays)),
        out_specs=[VMEM_SPEC] * len(outs),
        scratch_shapes=scratch,
        compiler_params=pltpu.CompilerParams(vmem_limit_bytes=VMEM_LIMIT),
        cost_estimate=pl.CostEstimate(
            flops=FLOPS * count * weight * 256 * 256 * 768,
            bytes_accessed=16 * count * lon_dev * channels,
            transcendentals=0,
        ),
        name="filter_" + phase,
    )(*scalars, *first, *arrays)


def chip_aware(fields, owner_slot, widths, tap_weights):
    lat_dev, lon_dev, channels = fields.shape
    n_lon = lax.axis_size("lon")
    at = lax.axis_index("lon")
    band = lax.axis_index("lat")
    core, x = at % 2, at // 2 % 2
    place = jnp.concatenate([jnp.stack([band, core, x]).astype(jnp.int32), owner_slot])
    chunks = STAY + STAY + COME + COME
    taken = take_rows(jnp.transpose(fields, (1, 0, 2)), place, chunks)
    n_stay, n_come = len(STAY), len(COME)
    keep, give = taken[:n_stay], taken[n_stay : 2 * n_stay]
    straight, cross = taken[2 * n_stay : 2 * n_stay + n_come], taken[2 * n_stay + n_come :]

    across_core = [(i, i ^ 1) for i in range(n_lon)]
    across_x = [(i, i ^ 2) for i in range(n_lon)]
    across_x_core = [(i, i ^ 3) for i in range(n_lon)]
    across_z = [(i, (i + (4 if i // 2 % 2 == 0 else -4)) % n_lon) for i in range(n_lon)]
    back_z = [(i, (i + (-4 if i // 2 % 2 == 0 else 4)) % n_lon) for i in range(n_lon)]
    across_y = [(i, i ^ 1) for i in range(2 * n_lon)]
    across_both = [(i, i ^ 3) for i in range(2 * n_lon)]

    lines = tap_lines(tap_weights, 3 * lon_dev)
    rows, slots = list_rows(place, lat_dev)
    scalars = rows, place, widths
    sizes = STAY + COME
    starts = [sum(sizes[:c]) for c in range(len(sizes))]
    done = {}

    def get(kind, i):
        if (kind, i) in done:
            return done[kind, i]

        def moved(operand, axes, pairs):
            first = [get(*g)[0] if g[0] in "ft" else get(*g) for g in WAITS.get((kind, i), ())]
            if first:
                operand = lax.optimization_barrier((operand, *first))[0]
            return lax.ppermute(operand, axes, pairs)

        if kind == "k":
            result = keep[i]
        elif kind == "c":
            result = moved(give[i], "lon", across_core)
        elif kind == "y":
            operand, pairs = ((straight, across_y), (cross, across_both))[i % 2]
            result = moved(operand[i // 2], ("lon", "lat"), pairs)
        elif kind == "x":
            result = moved(get(*PARTS[i]), "lon", across_x)
        elif kind == "z":
            result = moved(get("x", i), "lon", across_z)
        elif kind == "p":
            operand, pairs = ((keep[1], across_x), (give[1], across_x_core))[i]
            result = moved(operand, "lon", pairs)
        elif kind == "q":
            operand = get(*(("k", 0), ("c", 0), ("p", 0), ("p", 1))[i])
            result = moved(operand, "lon", back_z if i < 2 else across_z)
        elif kind == "t":
            here = [get("k", 0), get("c", 0)]
            beside = [get("p", 0), get("p", 1)]
            if i == 0:
                panels = here + beside + [get("q", 2), get("q", 3)]
            else:
                panels = beside + [get("q", 0), get("q", 1)] + here
            places = [[(p, row) for p in panels] for row in range(STAY[0])]
            result = filter_pair(scalars, lines, places, 0, lon_dev)
        elif kind == "b":
            operand, pairs = ((get("t", 0)[1], across_core), (get("t", 1)[0], across_x), (get("t", 1)[1], across_x_core))[i]
            result = moved(operand, "lon", pairs)
        elif kind == "f":
            places = []
            for row in FILTERS[i]:
                chunk, index = next((c, row - at) for c, at in enumerate(starts) if at <= row < at + sizes[c])
                if chunk < n_stay:
                    pair = ("k", chunk), ("c", chunk)
                else:
                    pair = ("y", 2 * (chunk - n_stay)), ("y", 2 * (chunk - n_stay) + 1)
                parts = [get(*p) for p in pair]
                parts += [get(axis, PARTS.index(p)) for axis in "xz" for p in pair]
                places.append([(p, index) for p in parts])
            base = FILTERS[i][0]
            if i < len(FILTERS) - 1:
                result = filter_pair(scalars, lines, places, base, lon_dev)
            else:
                early = filter_pair(scalars, lines, [p[:4] for p in places], base, lon_dev, "early")
                result = filter_pair(scalars, lines, [p[4:] for p in places], base, lon_dev, "late", early)
        else:
            result = moved(get("f", i)[1], "lon", across_core)
        done[kind, i] = result
        return result

    mine = [get("t", 0)[0], get("b", 1)] + [get("f", i)[0] for i in range(len(FILTERS))]
    theirs = [get("b", 0), get("b", 2)] + [get("o", i) for i in range(len(FILTERS))]
    out = put_rows(mine + theirs, slots, lon_dev, lat_dev)
    return jnp.transpose(out, (1, 0, 2))


def filter_kernel(reach, rows_ref, slots_ref, sector_ref, widths_ref, line_ref, *refs):
    ins, out_ref = refs[:-1], refs[-1]
    lon_dev, channels = out_ref.shape[1:]
    row = rows_ref[pl.program_id(0)]
    line = active_line(line_ref, row, widths_ref[row], (reach + 1) * lon_dev)
    total = ins[0][0].astype(jnp.float32)
    for group, ref in enumerate(ins):
        block = toeplitz(line, (sector_ref[group] + 1) * lon_dev, lon_dev, lon_dev)
        total += jnp.dot(block, ref[0], preferred_element_type=jnp.float32)[:lon_dev]
    out_ref[0] = total.astype(out_ref.dtype)


def filter_rows(rows, slots, sectors, widths, lines, arrays, reach):
    lat_dev, lon_dev, channels = arrays[0].shape
    row_spec = pl.BlockSpec((1, lon_dev, channels), lambda i, rows, slots, sectors, widths: (i, 0, 0))
    line_spec = pl.BlockSpec(lines.shape, lambda i, rows, slots, sectors, widths: (0, 0))
    out_spec = pl.BlockSpec((1, lon_dev, channels), lambda i, rows, slots, sectors, widths: (slots[i], 0, 0))
    return pl.pallas_call(
        functools.partial(filter_kernel, reach),
        out_shape=jax.ShapeDtypeStruct(arrays[0].shape, arrays[0].dtype),
        grid_spec=pltpu.PrefetchScalarGridSpec(
            num_scalar_prefetch=4,
            grid=(lat_dev,),
            in_specs=[line_spec] + [row_spec] * len(arrays),
            out_specs=out_spec,
        ),
        compiler_params=pltpu.CompilerParams(vmem_limit_bytes=VMEM_LIMIT),
        name="filter_rows",
    )(rows, slots, sectors, widths, lines, *arrays)


def any_mesh(fields, owner_slot, widths, tap_weights):
    lat_dev, lon_dev, channels = fields.shape
    n_lon = lax.axis_size("lon")
    n_lat = lax.axis_size("lat")
    reach = n_lon // 8
    band = lax.axis_index("lat")
    dest_band = owner_slot // lat_dev
    home_rows = band * lat_dev + jnp.arange(lat_dev, dtype=jnp.int32)
    ordering = jnp.argsort(dest_band[home_rows], stable=True)
    rows = jnp.argsort((dest_band != band).astype(jnp.int32), stable=True)[:lat_dev].astype(jnp.int32)
    slots = (owner_slot[rows] % lat_dev).astype(jnp.int32)
    outgoing = fields[ordering].reshape(n_lat, lat_dev // n_lat, lon_dev, channels)
    incoming = lax.all_to_all(outgoing, "lat", split_axis=0, concat_axis=0, tiled=True)
    own = incoming.reshape(lat_dev, lon_dev, channels)
    lines = tap_lines(tap_weights, (reach + 1) * lon_dev)
    arrays, order = [own], [reach]
    ahead = behind = own
    for step in range(1, reach + 1):
        ahead = shift_by(ahead, "lon", -1)
        behind = shift_by(behind, "lon", 1)
        arrays += [ahead, behind]
        order += [reach + step, reach - step]
    sectors = jnp.array(order, jnp.int32)
    return filter_rows(rows, slots, sectors, widths, lines, arrays, reach)


def solution(mesh):
    in_specs = (P("lat", "lon", None), P(), P(), P())
    out_specs = P("lat", "lon", None)
    chips = (mesh.shape["lon"], mesh.shape["lat"]) == (16, 2)

    def body(fields, owner_slot, widths, tap_weights):
        fits = chips and fields.shape[0] == 4 * sum(STAY)
        form = chip_aware if fits else any_mesh
        return form(fields, owner_slot, widths, tap_weights)

    return jax.shard_map(body, mesh=mesh, in_specs=in_specs, out_specs=out_specs, check_vma=False)
```

```python
import functools

import jax
import jax.numpy as jnp
from jax import lax
from jax.experimental import pallas as pl
from jax.experimental.pallas import tpu as pltpu
from jax.sharding import PartitionSpec as P

VMEM_LIMIT = 12 * 1024 * 1024
TAKE_VMEM_LIMIT = 50 * 1024 * 1024
PIECE = 3
AHEAD = 2
SMEM_SPEC = pl.BlockSpec(memory_space=pltpu.SMEM)
VMEM_SPEC = pl.BlockSpec(memory_space=pltpu.VMEM)
HBM_SPEC = pl.BlockSpec(memory_space=pltpu.HBM)
STAY = (2, 2)
COME = (2, 2)
PARTS = [("y", 0), ("y", 1), ("y", 2), ("y", 3)]
FILTERS = ((4, 5), (6, 7))
WAITS = {
    ("x", 0): [("p", 0), ("y", 0)],
    ("x", 1): [("p", 1)],
    ("b", 2): [("x", 3)],
    ("q", 2): [("q", 0)],
    ("q", 3): [("q", 1)],
    ("z", 0): [("q", 2), ("q", 1)],
    ("z", 1): [("q", 3), ("t", 1)],
    ("z", 2): [("z", 0)],
    ("z", 3): [("z", 1)],
    ("y", 2): [("y", 0), ("p", 0)],
    ("y", 3): [("y", 1), ("x", 0)],
    ("y", 1): [("q", 0), ("l", 0), ("l", 1)],
}
FLOPS = 3


def up_to(value, multiple):
    return -(-value // multiple) * multiple


def shift_by(x, axis, by):
    count = lax.axis_size(axis)
    return lax.ppermute(x, axis, [(i, (i + by) % count) for i in range(count)])


def line_kernel(behind, taps_ref, line_ref):
    circle = taps_ref.shape[1]
    rows, lanes = line_ref.shape
    taps = taps_ref[...].astype(jnp.float32)
    pieces = [taps[:, circle - behind :], taps[:, :behind]]
    if lanes > 2 * behind:
        pieces.append(jnp.zeros((rows, lanes - 2 * behind), jnp.float32))
    line_ref[...] = jnp.concatenate(pieces, axis=1)


def tap_lines(tap_weights, behind):
    rows = tap_weights.shape[0]
    lanes = up_to(2 * behind, 128)
    return pl.pallas_call(
        functools.partial(line_kernel, behind),
        out_shape=jax.ShapeDtypeStruct((rows, lanes), jnp.float32),
        in_specs=[VMEM_SPEC],
        out_specs=VMEM_SPEC,
        compiler_params=pltpu.CompilerParams(vmem_limit_bytes=VMEM_LIMIT),
        cost_estimate=pl.CostEstimate(flops=0, bytes_accessed=2 * tap_weights.size, transcendentals=0),
        name="tap_lines",
    )(tap_weights)


def active_line(line_ref, row, width, behind):
    line = jnp.broadcast_to(line_ref[pl.ds(row, 1), :], (8, line_ref.shape[1]))
    distance = jnp.abs(lax.broadcasted_iota(jnp.int32, line.shape, 1) - behind)
    return jnp.where(distance <= width, line, 0.0)


def toeplitz(line, at, lon_dev, width):
    lanes = up_to(width, 128) + 128
    step = min(up_to(lon_dev, 16), 96)
    bands = []
    for start in range(0, up_to(lon_dev, step), step):
        taps = pltpu.roll(line, line.shape[1] + start - at, 1)
        taps = jnp.concatenate([taps[:, : lanes - 128], taps[:, -128:]], axis=1)
        band = pltpu.roll(jnp.concatenate([taps] * (step // 8), axis=0), 0, 1, stride=1, stride_axis=0)
        bands.append(band[:, :width].astype(jnp.bfloat16))
    return jnp.concatenate(bands, axis=0)


def listed(n, quarter, core):
    within = n % quarter
    return within + jnp.where(n // quarter == core, 0, quarter)


def traded(n, quarter, x):
    within = n % quarter
    return n - within + (within + quarter // 2 * x) % quarter


def list_kernel(lat_dev, place_ref, rows_ref, slots_ref):
    half, quarter = lat_dev // 2, lat_dev // 4
    band, core, x = place_ref[0], place_ref[1], place_ref[2]
    stay, come = jnp.int32(0), jnp.int32(0)
    for j in range(lat_dev):
        here = band * lat_dev + j
        there = (1 - band) * lat_dev + j
        stays = place_ref[3 + here] // lat_dev == band
        comes = place_ref[3 + there] // lat_dev == band

        spot = traded(listed(stay, quarter, core), quarter, x)
        spot = jnp.where(stays, spot + jnp.where(spot >= quarter, quarter, 0), lat_dev)
        rows_ref[spot] = here
        slots_ref[spot] = place_ref[3 + here] % lat_dev
        spot = listed(come, quarter, core)
        spot = jnp.where(comes, spot + jnp.where(spot >= quarter, half, quarter), lat_dev)
        rows_ref[spot] = there
        slots_ref[spot] = place_ref[3 + there] % lat_dev
        stay = stay + stays.astype(jnp.int32)
        come = come + comes.astype(jnp.int32)


def list_rows(place, lat_dev):
    ints = jax.ShapeDtypeStruct((lat_dev + 1,), jnp.int32)
    return pl.pallas_call(
        functools.partial(list_kernel, lat_dev),
        out_shape=[ints, ints],
        in_specs=[SMEM_SPEC],
        out_specs=[SMEM_SPEC, SMEM_SPEC],
        compiler_params=pltpu.CompilerParams(vmem_limit_bytes=VMEM_LIMIT),
        cost_estimate=pl.CostEstimate(flops=0, bytes_accessed=256, transcendentals=0),
        name="list_rows",
    )(place)


def take_kernel(chunks, lat_dev, block, place_ref, fields_ref, *refs):
    outs = refs[: len(chunks)]
    home_ref, take_ref, panel_ref, sems = refs[len(chunks) :]
    lon_dev, _, channels = fields_ref.shape
    half, quarter = lat_dev // 2, lat_dev // 4
    copies = []
    for n, start in enumerate(range(0, lon_dev, PIECE * block)):
        window = pl.ds(start, min(PIECE * block, lon_dev - start))
        copies.append(pltpu.make_async_copy(fields_ref.at[window], panel_ref.at[window], sems.at[n]))
    for copy in copies[:AHEAD]:
        copy.start()

    band, core, x = place_ref[0], place_ref[1], place_ref[2]
    stay, leave = jnp.int32(0), jnp.int32(0)
    for j in range(lat_dev):
        stays = place_ref[3 + band * lat_dev + j] // lat_dev == band
        spot = traded(listed(stay, quarter, core), quarter, x)
        home_ref[jnp.where(stays, spot, half + listed(leave, quarter, core))] = jnp.int32(j)
        stay = stay + stays.astype(jnp.int32)
        leave = leave + 1 - stays.astype(jnp.int32)

    def selector(lon):
        row = lax.broadcasted_iota(jnp.int32, (lat_dev * lon, 128), 0)
        if lon % 8 == 0:
            home = jnp.concatenate([jnp.full((lon, 128), home_ref[p], jnp.int32) for p in range(lat_dev)], axis=0)
        else:
            home = sum(jnp.where(row // lon == p, home_ref[p], 0) for p in range(lat_dev))
        wanted = row % lon * lat_dev + home
        column = lax.broadcasted_iota(jnp.int32, (lat_dev * lon, lon * lat_dev), 1)
        return jnp.where(column == wanted[:, :1], 1.0, 0.0).astype(jnp.bfloat16)

    take_ref[...] = selector(block)
    rest = lon_dev % block
    small = selector(rest) if rest else None
    for n, start in enumerate(range(0, lon_dev, block)):
        if n % PIECE == 0:
            copies[n // PIECE].wait()
            if n // PIECE + AHEAD < len(copies):
                copies[n // PIECE + AHEAD].start()
        lon = min(block, lon_dev - start)
        panel = panel_ref[start : start + lon].reshape(lon * lat_dev, channels)
        take = take_ref[...] if lon == block else small
        taken = jnp.dot(take, panel, preferred_element_type=jnp.float32)
        place = 0
        for out, count in zip(outs, chunks):
            for i in range(count):
                piece = taken[place * lon : (place + 1) * lon].astype(out.dtype)
                out[i * lon_dev + start : i * lon_dev + start + lon, :] = piece
                place += 1


def take_rows(fields, place, chunks):
    lon_dev, lat_dev, channels = fields.shape
    block = 16
    return pl.pallas_call(
        functools.partial(take_kernel, chunks, lat_dev, block),
        out_shape=[jax.ShapeDtypeStruct((n * lon_dev, channels), fields.dtype) for n in chunks],
        in_specs=[SMEM_SPEC, HBM_SPEC],
        out_specs=[VMEM_SPEC] * len(chunks),
        scratch_shapes=[
            pltpu.SMEM((lat_dev,), jnp.int32),
            pltpu.VMEM((block * lat_dev, block * lat_dev), jnp.bfloat16),
            pltpu.VMEM(fields.shape, fields.dtype),
            pltpu.SemaphoreType.DMA((pl.cdiv(lon_dev, PIECE * block),)),
        ],
        compiler_params=pltpu.CompilerParams(vmem_limit_bytes=TAKE_VMEM_LIMIT),
        cost_estimate=pl.CostEstimate(
            flops=2 * fields.size * block * lat_dev, bytes_accessed=4 * fields.size, transcendentals=0
        ),
        name="take_rows",
    )(place, fields)


def put_kernel(counts, lat_dev, block, slots_ref, *refs):
    ins, (out_ref, panel_ref, sems) = refs[:-3], refs[-3:]
    lon_dev, _, channels = out_ref.shape

    def selector(lon):
        row = lax.broadcasted_iota(jnp.int32, (lon * lat_dev, lat_dev * lon), 0)
        column = lax.broadcasted_iota(jnp.int32, (8, lat_dev * lon), 1)
        wanted = column % lon * lat_dev
        for p in range(lat_dev):
            wanted += jnp.where(column // lon == p, slots_ref[p], 0)
        return jnp.where(row == wanted[:1], 1.0, 0.0).astype(jnp.bfloat16)

    whole = selector(block)
    rest = lon_dev % block
    small = selector(rest) if rest else None
    copies = []
    for n, start in enumerate(range(0, lon_dev, block)):
        lon = min(block, lon_dev - start)
        pieces = [r[i * lon_dev + start : i * lon_dev + start + lon, :] for r, count in zip(ins, counts) for i in range(count)]
        if lon < block:
            pieces = [p.astype(jnp.float32) for p in pieces]
        panel = jnp.concatenate(pieces, axis=0).astype(jnp.bfloat16)
        spread = jnp.dot(whole if lon == block else small, panel, preferred_element_type=jnp.float32)
        window = pl.ds(start, lon)
        panel_ref[window] = spread.astype(jnp.bfloat16).reshape(lon, lat_dev, channels)
        copies.append(pltpu.make_async_copy(panel_ref.at[window], out_ref.at[window], sems.at[n]))
        copies[-1].start()
    for copy in copies:
        copy.wait()


def put_rows(panels, slots, lon_dev, lat_dev):
    channels = panels[0].shape[1]
    block = 16
    counts = tuple(p.shape[0] // lon_dev for p in panels)
    shape = (lon_dev, lat_dev, channels)
    return pl.pallas_call(
        functools.partial(put_kernel, counts, lat_dev, block),
        out_shape=jax.ShapeDtypeStruct(shape, panels[0].dtype),
        in_specs=[SMEM_SPEC] + [VMEM_SPEC] * len(panels),
        out_specs=HBM_SPEC,
        scratch_shapes=[
            pltpu.VMEM(shape, panels[0].dtype),
            pltpu.SemaphoreType.DMA((pl.cdiv(lon_dev, block),)),
        ],
        compiler_params=pltpu.CompilerParams(vmem_limit_bytes=VMEM_LIMIT),
        cost_estimate=pl.CostEstimate(
            flops=2 * lon_dev * lat_dev * channels * block * lat_dev,
            bytes_accessed=4 * lon_dev * lat_dev * channels,
            transcendentals=0,
        ),
        name="put_rows",
    )(slots, *panels)


def pair_kernel(lon_dev, base, plan, phase, rows_ref, place_ref, widths_ref, *refs):
    count = len(plan)
    side, along = 1 - 2 * place_ref[1], 1 - 2 * place_ref[2]
    if phase == "late":
        (total_in, block_ref), refs = refs[:2], refs[2:]
    else:
        line_ref, refs = refs[0], refs[1:]
    if phase == "early":
        ins, (total_ref, block_ref) = refs[:-2], refs[-2:]
    elif phase == "late":
        ins, (out_own, out_other) = refs[:-2], refs[-2:]
    else:
        ins, (out_own, out_other, block_ref) = refs[:-3], refs[-3:]
    channels = ins[0].shape[1]

    def both(first, second):
        return jnp.concatenate([first[...], second[...]], axis=1)

    for n, places in enumerate(plan):
        panels = [ins[array].at[pl.ds(i * lon_dev, lon_dev), :] for array, i in places]

        def times(offset, panel):
            return jnp.dot(block_ref[n, 2 + offset], panel, preferred_element_type=jnp.float32)[:lon_dev]

        def halves(first, second):
            return jnp.concatenate([first, second], axis=1)

        nothing = jnp.zeros((lon_dev, channels), jnp.float32)
        same = side == along
        if phase != "late":
            own, other, x_own, x_other = panels[:4]
            row = rows_ref[base + n]
            line = active_line(line_ref, row, widths_ref[row], 3 * lon_dev)
            for s in range(5):
                block_ref[n, s] = toeplitz(line, (s + 1) * lon_dev, lon_dev, lon_dev)
            here = both(own, other)
            total = here.astype(jnp.float32) + times(0, here)
            total += times(2 * along, both(x_own, x_other))
            total += jnp.concatenate([times(side, other[...]), times(-side, own[...])], axis=1)
            more = times(along, jnp.where(same, x_own[...], x_other[...]))
            total += halves(jnp.where(same, nothing, more), jnp.where(same, more, nothing))
            if phase == "early":
                total_ref[n] = total
        if phase != "early":
            z_own, z_other = panels[-2:]
            if phase == "late":
                total = total_in[n]
            total += times(-2 * along, both(z_own, z_other))
            more = times(-along, jnp.where(same, z_other[...], z_own[...]))
            total += halves(jnp.where(same, more, nothing), jnp.where(same, nothing, more))
            here = pl.ds(n * lon_dev, lon_dev)
            out_own[here, :] = total[:, :channels].astype(out_own.dtype)
            out_other[here, :] = total[:, channels:].astype(out_other.dtype)


def filter_pair(scalars, lines, places, base, lon_dev, phase="whole", early=()):
    arrays = []
    plan = []
    for row in places:
        found = []
        for array, i in row:
            at = next((n for n, a in enumerate(arrays) if a is array), len(arrays))
            if at == len(arrays):
                arrays.append(array)
            found.append((at, i))
        plan.append(tuple(found))
    count = len(plan)
    channels = arrays[0].shape[1]
    total = (count, lon_dev, 2 * channels), jnp.float32
    block = (count, 5, up_to(lon_dev, 96), lon_dev), jnp.bfloat16
    out = jax.ShapeDtypeStruct((count * lon_dev, channels), arrays[0].dtype)
    first = [lines] if phase != "late" else list(early)
    if phase == "early":
        outs, scratch = [jax.ShapeDtypeStruct(*total), jax.ShapeDtypeStruct(*block)], []
    elif phase == "late":
        outs, scratch = [out, out], []
    else:
        outs, scratch = [out, out], [pltpu.VMEM(*block)]
    weight = {"whole": 10, "early": 7, "late": 3}[phase]
    return pl.pallas_call(
        functools.partial(pair_kernel, lon_dev, base, tuple(plan), phase),
        out_shape=outs,
        in_specs=[SMEM_SPEC] * 3 + [VMEM_SPEC] * (len(first) + len(arrays)),
        out_specs=[VMEM_SPEC] * len(outs),
        scratch_shapes=scratch,
        compiler_params=pltpu.CompilerParams(vmem_limit_bytes=VMEM_LIMIT),
        cost_estimate=pl.CostEstimate(
            flops=FLOPS * count * weight * 256 * 256 * 768,
            bytes_accessed=16 * count * lon_dev * channels,
            transcendentals=0,
        ),
        name="filter_" + phase,
    )(*scalars, *first, *arrays)


def chip_aware(fields, owner_slot, widths, tap_weights):
    lat_dev, lon_dev, channels = fields.shape
    n_lon = lax.axis_size("lon")
    at = lax.axis_index("lon")
    band = lax.axis_index("lat")
    core, x = at % 2, at // 2 % 2
    place = jnp.concatenate([jnp.stack([band, core, x]).astype(jnp.int32), owner_slot])
    chunks = STAY + STAY + COME + COME
    taken = take_rows(jnp.transpose(fields, (1, 0, 2)), place, chunks)
    n_stay, n_come = len(STAY), len(COME)
    keep, give = taken[:n_stay], taken[n_stay : 2 * n_stay]
    straight, cross = taken[2 * n_stay : 2 * n_stay + n_come], taken[2 * n_stay + n_come :]

    across_core = [(i, i ^ 1) for i in range(n_lon)]
    across_x = [(i, i ^ 2) for i in range(n_lon)]
    across_x_core = [(i, i ^ 3) for i in range(n_lon)]
    across_z = [(i, (i + (4 if i // 2 % 2 == 0 else -4)) % n_lon) for i in range(n_lon)]
    back_z = [(i, (i + (-4 if i // 2 % 2 == 0 else 4)) % n_lon) for i in range(n_lon)]
    across_y = [(i, i ^ 1) for i in range(2 * n_lon)]
    across_both = [(i, i ^ 3) for i in range(2 * n_lon)]

    lines = tap_lines(tap_weights, 3 * lon_dev)
    rows, slots = list_rows(place, lat_dev)
    scalars = rows, place, widths
    sizes = STAY + COME
    starts = [sum(sizes[:c]) for c in range(len(sizes))]
    done = {}

    def get(kind, i):
        if (kind, i) in done:
            return done[kind, i]

        def moved(operand, axes, pairs):
            first = [get(*g)[0] if g[0] in "ft" else get(*g) for g in WAITS.get((kind, i), ())]
            if first:
                operand = lax.optimization_barrier((operand, *first))[0]
            return lax.ppermute(operand, axes, pairs)

        if kind == "k":
            result = keep[i]
        elif kind == "l":
            result = (rows, lines)[i]
        elif kind == "c":
            result = moved(give[i], "lon", across_core)
        elif kind == "y":
            operand, pairs = ((straight, across_y), (cross, across_both))[i % 2]
            result = moved(operand[i // 2], ("lon", "lat"), pairs)
        elif kind == "x":
            result = moved(get(*PARTS[i]), "lon", across_x)
        elif kind == "z":
            result = moved(get("x", i), "lon", across_z)
        elif kind == "p":
            operand, pairs = ((keep[1], across_x), (give[1], across_x_core))[i]
            result = moved(operand, "lon", pairs)
        elif kind == "q":
            operand = get(*(("k", 0), ("c", 0), ("p", 0), ("p", 1))[i])
            result = moved(operand, "lon", back_z if i < 2 else across_z)
        elif kind == "t":
            here = [get("k", 0), get("c", 0)]
            beside = [get("p", 0), get("p", 1)]
            if i == 0:
                panels = here + beside + [get("q", 2), get("q", 3)]
            else:
                panels = beside + [get("q", 0), get("q", 1)] + here
            places = [[(p, row) for p in panels] for row in range(STAY[0])]
            result = filter_pair(scalars, lines, places, 0, lon_dev)
        elif kind == "b":
            operand, pairs = ((get("t", 0)[1], across_core), (get("t", 1)[0], across_x), (get("t", 1)[1], across_x_core))[i]
            result = moved(operand, "lon", pairs)
        elif kind == "f":
            places = []
            for row in FILTERS[i]:
                chunk, index = next((c, row - at) for c, at in enumerate(starts) if at <= row < at + sizes[c])
                if chunk < n_stay:
                    pair = ("k", chunk), ("c", chunk)
                else:
                    pair = ("y", 2 * (chunk - n_stay)), ("y", 2 * (chunk - n_stay) + 1)
                parts = [get(*p) for p in pair]
                parts += [get(axis, PARTS.index(p)) for axis in "xz" for p in pair]
                places.append([(p, index) for p in parts])
            base = FILTERS[i][0]
            if i < len(FILTERS) - 1:
                result = filter_pair(scalars, lines, places, base, lon_dev)
            else:
                early = filter_pair(scalars, lines, [p[:4] for p in places], base, lon_dev, "early")
                result = filter_pair(scalars, lines, [p[4:] for p in places], base, lon_dev, "late", early)
        else:
            result = moved(get("f", i)[1], "lon", across_core)
        done[kind, i] = result
        return result

    mine = [get("t", 0)[0], get("b", 1)] + [get("f", i)[0] for i in range(len(FILTERS))]
    theirs = [get("b", 0), get("b", 2)] + [get("o", i) for i in range(len(FILTERS))]
    out = put_rows(mine + theirs, slots, lon_dev, lat_dev)
    return jnp.transpose(out, (1, 0, 2))


def filter_kernel(reach, rows_ref, slots_ref, sector_ref, widths_ref, line_ref, *refs):
    ins, out_ref = refs[:-1], refs[-1]
    lon_dev, channels = out_ref.shape[1:]
    row = rows_ref[pl.program_id(0)]
    line = active_line(line_ref, row, widths_ref[row], (reach + 1) * lon_dev)
    total = ins[0][0].astype(jnp.float32)
    for group, ref in enumerate(ins):
        block = toeplitz(line, (sector_ref[group] + 1) * lon_dev, lon_dev, lon_dev)
        total += jnp.dot(block, ref[0], preferred_element_type=jnp.float32)[:lon_dev]
    out_ref[0] = total.astype(out_ref.dtype)


def filter_rows(rows, slots, sectors, widths, lines, arrays, reach):
    lat_dev, lon_dev, channels = arrays[0].shape
    row_spec = pl.BlockSpec((1, lon_dev, channels), lambda i, rows, slots, sectors, widths: (i, 0, 0))
    line_spec = pl.BlockSpec(lines.shape, lambda i, rows, slots, sectors, widths: (0, 0))
    out_spec = pl.BlockSpec((1, lon_dev, channels), lambda i, rows, slots, sectors, widths: (slots[i], 0, 0))
    return pl.pallas_call(
        functools.partial(filter_kernel, reach),
        out_shape=jax.ShapeDtypeStruct(arrays[0].shape, arrays[0].dtype),
        grid_spec=pltpu.PrefetchScalarGridSpec(
            num_scalar_prefetch=4,
            grid=(lat_dev,),
            in_specs=[line_spec] + [row_spec] * len(arrays),
            out_specs=out_spec,
        ),
        compiler_params=pltpu.CompilerParams(vmem_limit_bytes=VMEM_LIMIT),
        name="filter_rows",
    )(rows, slots, sectors, widths, lines, *arrays)


def any_mesh(fields, owner_slot, widths, tap_weights):
    lat_dev, lon_dev, channels = fields.shape
    n_lon = lax.axis_size("lon")
    n_lat = lax.axis_size("lat")
    reach = n_lon // 8
    band = lax.axis_index("lat")
    dest_band = owner_slot // lat_dev
    home_rows = band * lat_dev + jnp.arange(lat_dev, dtype=jnp.int32)
    ordering = jnp.argsort(dest_band[home_rows], stable=True)
    rows = jnp.argsort((dest_band != band).astype(jnp.int32), stable=True)[:lat_dev].astype(jnp.int32)
    slots = (owner_slot[rows] % lat_dev).astype(jnp.int32)
    outgoing = fields[ordering].reshape(n_lat, lat_dev // n_lat, lon_dev, channels)
    incoming = lax.all_to_all(outgoing, "lat", split_axis=0, concat_axis=0, tiled=True)
    own = incoming.reshape(lat_dev, lon_dev, channels)
    lines = tap_lines(tap_weights, (reach + 1) * lon_dev)
    arrays, order = [own], [reach]
    ahead = behind = own
    for step in range(1, reach + 1):
        ahead = shift_by(ahead, "lon", -1)
        behind = shift_by(behind, "lon", 1)
        arrays += [ahead, behind]
        order += [reach + step, reach - step]
    sectors = jnp.array(order, jnp.int32)
    return filter_rows(rows, slots, sectors, widths, lines, arrays, reach)


def solution(mesh):
    in_specs = (P("lat", "lon", None), P(), P(), P())
    out_specs = P("lat", "lon", None)
    chips = (mesh.shape["lon"], mesh.shape["lat"]) == (16, 2)

    def body(fields, owner_slot, widths, tap_weights):
        fits = chips and fields.shape[0] == 4 * sum(STAY)
        form = chip_aware if fits else any_mesh
        return form(fields, owner_slot, widths, tap_weights)

    return jax.shard_map(body, mesh=mesh, in_specs=in_specs, out_specs=out_specs, check_vma=False)
```

```python
import functools

import jax
import jax.numpy as jnp
from jax import lax
from jax.experimental import pallas as pl
from jax.experimental.pallas import tpu as pltpu
from jax.sharding import PartitionSpec as P

VMEM_LIMIT = 12 * 1024 * 1024
TAKE_VMEM_LIMIT = 50 * 1024 * 1024
PIECE = 2
AHEAD = 3
SMEM_SPEC = pl.BlockSpec(memory_space=pltpu.SMEM)
VMEM_SPEC = pl.BlockSpec(memory_space=pltpu.VMEM)
HBM_SPEC = pl.BlockSpec(memory_space=pltpu.HBM)
STAY = (2, 2)
COME = (2, 2)
PARTS = [("y", 0), ("y", 1), ("y", 2), ("y", 3)]
FILTERS = ((4, 5), (6, 7))
WAITS = {
    ("x", 0): [("p", 0), ("y", 0)],
    ("x", 1): [("p", 1)],
    ("b", 2): [("x", 3)],
    ("q", 2): [("q", 0)],
    ("q", 3): [("q", 1)],
    ("z", 0): [("q", 2), ("q", 1)],
    ("z", 1): [("q", 3), ("t", 1)],
    ("z", 2): [("z", 0)],
    ("z", 3): [("z", 1)],
    ("y", 2): [("y", 0), ("p", 0)],
    ("y", 3): [("y", 1), ("x", 0)],
    ("y", 1): [("q", 0), ("l", 0), ("l", 1)],
}
FLOPS = 3


def up_to(value, multiple):
    return -(-value // multiple) * multiple


def shift_by(x, axis, by):
    count = lax.axis_size(axis)
    return lax.ppermute(x, axis, [(i, (i + by) % count) for i in range(count)])


def line_kernel(behind, taps_ref, line_ref):
    circle = taps_ref.shape[1]
    rows, lanes = line_ref.shape
    taps = taps_ref[...].astype(jnp.float32)
    pieces = [taps[:, circle - behind :], taps[:, :behind]]
    if lanes > 2 * behind:
        pieces.append(jnp.zeros((rows, lanes - 2 * behind), jnp.float32))
    line_ref[...] = jnp.concatenate(pieces, axis=1)


def tap_lines(tap_weights, behind):
    rows = tap_weights.shape[0]
    lanes = up_to(2 * behind, 128)
    return pl.pallas_call(
        functools.partial(line_kernel, behind),
        out_shape=jax.ShapeDtypeStruct((rows, lanes), jnp.float32),
        in_specs=[VMEM_SPEC],
        out_specs=VMEM_SPEC,
        compiler_params=pltpu.CompilerParams(vmem_limit_bytes=VMEM_LIMIT),
        cost_estimate=pl.CostEstimate(flops=0, bytes_accessed=2 * tap_weights.size, transcendentals=0),
        name="tap_lines",
    )(tap_weights)


def active_line(line_ref, row, width, behind):
    line = jnp.broadcast_to(line_ref[pl.ds(row, 1), :], (8, line_ref.shape[1]))
    distance = jnp.abs(lax.broadcasted_iota(jnp.int32, line.shape, 1) - behind)
    return jnp.where(distance <= width, line, 0.0)


def toeplitz(line, at, lon_dev, width):
    lanes = up_to(width, 128) + 128
    step = min(up_to(lon_dev, 16), 96)
    bands = []
    for start in range(0, up_to(lon_dev, step), step):
        taps = pltpu.roll(line, line.shape[1] + start - at, 1)
        taps = jnp.concatenate([taps[:, : lanes - 128], taps[:, -128:]], axis=1)
        band = pltpu.roll(jnp.concatenate([taps] * (step // 8), axis=0), 0, 1, stride=1, stride_axis=0)
        bands.append(band[:, :width].astype(jnp.bfloat16))
    return jnp.concatenate(bands, axis=0)


def listed(n, quarter, core):
    within = n % quarter
    return within + jnp.where(n // quarter == core, 0, quarter)


def traded(n, quarter, x):
    within = n % quarter
    return n - within + (within + quarter // 2 * x) % quarter


def list_kernel(lat_dev, place_ref, rows_ref, slots_ref):
    half, quarter = lat_dev // 2, lat_dev // 4
    band, core, x = place_ref[0], place_ref[1], place_ref[2]
    stay, come = jnp.int32(0), jnp.int32(0)
    for j in range(lat_dev):
        here = band * lat_dev + j
        there = (1 - band) * lat_dev + j
        stays = place_ref[3 + here] // lat_dev == band
        comes = place_ref[3 + there] // lat_dev == band

        spot = traded(listed(stay, quarter, core), quarter, x)
        spot = jnp.where(stays, spot + jnp.where(spot >= quarter, quarter, 0), lat_dev)
        rows_ref[spot] = here
        slots_ref[spot] = place_ref[3 + here] % lat_dev
        spot = listed(come, quarter, core)
        spot = jnp.where(comes, spot + jnp.where(spot >= quarter, half, quarter), lat_dev)
        rows_ref[spot] = there
        slots_ref[spot] = place_ref[3 + there] % lat_dev
        stay = stay + stays.astype(jnp.int32)
        come = come + comes.astype(jnp.int32)


def list_rows(place, lat_dev):
    ints = jax.ShapeDtypeStruct((lat_dev + 1,), jnp.int32)
    return pl.pallas_call(
        functools.partial(list_kernel, lat_dev),
        out_shape=[ints, ints],
        in_specs=[SMEM_SPEC],
        out_specs=[SMEM_SPEC, SMEM_SPEC],
        compiler_params=pltpu.CompilerParams(vmem_limit_bytes=VMEM_LIMIT),
        cost_estimate=pl.CostEstimate(flops=0, bytes_accessed=256, transcendentals=0),
        name="list_rows",
    )(place)


def take_kernel(chunks, lat_dev, block, place_ref, fields_ref, *refs):
    outs = refs[: len(chunks)]
    home_ref, take_ref, panel_ref, sems = refs[len(chunks) :]
    lon_dev, _, channels = fields_ref.shape
    half, quarter = lat_dev // 2, lat_dev // 4
    copies = []
    for n, start in enumerate(range(0, lon_dev, PIECE * block)):
        window = pl.ds(start, min(PIECE * block, lon_dev - start))
        copies.append(pltpu.make_async_copy(fields_ref.at[window], panel_ref.at[window], sems.at[n]))
    for copy in copies[:AHEAD]:
        copy.start()

    band, core, x = place_ref[0], place_ref[1], place_ref[2]
    stay, leave = jnp.int32(0), jnp.int32(0)
    for j in range(lat_dev):
        stays = place_ref[3 + band * lat_dev + j] // lat_dev == band
        spot = traded(listed(stay, quarter, core), quarter, x)
        home_ref[jnp.where(stays, spot, half + listed(leave, quarter, core))] = jnp.int32(j)
        stay = stay + stays.astype(jnp.int32)
        leave = leave + 1 - stays.astype(jnp.int32)

    def selector(lon):
        row = lax.broadcasted_iota(jnp.int32, (lat_dev * lon, 128), 0)
        if lon % 8 == 0:
            home = jnp.concatenate([jnp.full((lon, 128), home_ref[p], jnp.int32) for p in range(lat_dev)], axis=0)
        else:
            home = sum(jnp.where(row // lon == p, home_ref[p], 0) for p in range(lat_dev))
        wanted = row % lon * lat_dev + home
        column = lax.broadcasted_iota(jnp.int32, (lat_dev * lon, lon * lat_dev), 1)
        return jnp.where(column == wanted[:, :1], 1.0, 0.0).astype(jnp.bfloat16)

    take_ref[...] = selector(block)
    rest = lon_dev % block
    small = selector(rest) if rest else None
    for n, start in enumerate(range(0, lon_dev, block)):
        if n % PIECE == 0:
            copies[n // PIECE].wait()
            if n // PIECE + AHEAD < len(copies):
                copies[n // PIECE + AHEAD].start()
        lon = min(block, lon_dev - start)
        panel = panel_ref[start : start + lon].reshape(lon * lat_dev, channels)
        take = take_ref[...] if lon == block else small
        taken = jnp.dot(take, panel, preferred_element_type=jnp.float32)
        place = 0
        for out, count in zip(outs, chunks):
            for i in range(count):
                piece = taken[place * lon : (place + 1) * lon].astype(out.dtype)
                out[i * lon_dev + start : i * lon_dev + start + lon, :] = piece
                place += 1


def take_rows(fields, place, chunks):
    lon_dev, lat_dev, channels = fields.shape
    block = 16
    return pl.pallas_call(
        functools.partial(take_kernel, chunks, lat_dev, block),
        out_shape=[jax.ShapeDtypeStruct((n * lon_dev, channels), fields.dtype) for n in chunks],
        in_specs=[SMEM_SPEC, HBM_SPEC],
        out_specs=[VMEM_SPEC] * len(chunks),
        scratch_shapes=[
            pltpu.SMEM((lat_dev,), jnp.int32),
            pltpu.VMEM((block * lat_dev, block * lat_dev), jnp.bfloat16),
            pltpu.VMEM(fields.shape, fields.dtype),
            pltpu.SemaphoreType.DMA((pl.cdiv(lon_dev, PIECE * block),)),
        ],
        compiler_params=pltpu.CompilerParams(vmem_limit_bytes=TAKE_VMEM_LIMIT),
        cost_estimate=pl.CostEstimate(
            flops=2 * fields.size * block * lat_dev, bytes_accessed=4 * fields.size, transcendentals=0
        ),
        name="take_rows",
    )(place, fields)


def put_kernel(counts, lat_dev, block, slots_ref, *refs):
    ins, (out_ref, panel_ref, sems) = refs[:-3], refs[-3:]
    lon_dev, _, channels = out_ref.shape

    def selector(lon):
        row = lax.broadcasted_iota(jnp.int32, (lon * lat_dev, lat_dev * lon), 0)
        column = lax.broadcasted_iota(jnp.int32, (8, lat_dev * lon), 1)
        wanted = column % lon * lat_dev
        for p in range(lat_dev):
            wanted += jnp.where(column // lon == p, slots_ref[p], 0)
        return jnp.where(row == wanted[:1], 1.0, 0.0).astype(jnp.bfloat16)

    whole = selector(block)
    rest = lon_dev % block
    small = selector(rest) if rest else None
    copies = []
    for n, start in enumerate(range(0, lon_dev, block)):
        lon = min(block, lon_dev - start)
        pieces = [r[i * lon_dev + start : i * lon_dev + start + lon, :] for r, count in zip(ins, counts) for i in range(count)]
        if lon < block:
            pieces = [p.astype(jnp.float32) for p in pieces]
        panel = jnp.concatenate(pieces, axis=0).astype(jnp.bfloat16)
        spread = jnp.dot(whole if lon == block else small, panel, preferred_element_type=jnp.float32)
        window = pl.ds(start, lon)
        panel_ref[window] = spread.astype(jnp.bfloat16).reshape(lon, lat_dev, channels)
        copies.append(pltpu.make_async_copy(panel_ref.at[window], out_ref.at[window], sems.at[n]))
        copies[-1].start()
    for copy in copies:
        copy.wait()


def put_rows(panels, slots, lon_dev, lat_dev):
    channels = panels[0].shape[1]
    block = 16
    counts = tuple(p.shape[0] // lon_dev for p in panels)
    shape = (lon_dev, lat_dev, channels)
    return pl.pallas_call(
        functools.partial(put_kernel, counts, lat_dev, block),
        out_shape=jax.ShapeDtypeStruct(shape, panels[0].dtype),
        in_specs=[SMEM_SPEC] + [VMEM_SPEC] * len(panels),
        out_specs=HBM_SPEC,
        scratch_shapes=[
            pltpu.VMEM(shape, panels[0].dtype),
            pltpu.SemaphoreType.DMA((pl.cdiv(lon_dev, block),)),
        ],
        compiler_params=pltpu.CompilerParams(vmem_limit_bytes=VMEM_LIMIT),
        cost_estimate=pl.CostEstimate(
            flops=2 * lon_dev * lat_dev * channels * block * lat_dev,
            bytes_accessed=4 * lon_dev * lat_dev * channels,
            transcendentals=0,
        ),
        name="put_rows",
    )(slots, *panels)


def pair_kernel(lon_dev, base, plan, phase, rows_ref, place_ref, widths_ref, *refs):
    count = len(plan)
    side, along = 1 - 2 * place_ref[1], 1 - 2 * place_ref[2]
    if phase == "late":
        (total_in, block_ref), refs = refs[:2], refs[2:]
    else:
        line_ref, refs = refs[0], refs[1:]
    if phase == "early":
        ins, (total_ref, block_ref) = refs[:-2], refs[-2:]
    elif phase == "late":
        ins, (out_own, out_other) = refs[:-2], refs[-2:]
    else:
        ins, (out_own, out_other, block_ref) = refs[:-3], refs[-3:]
    channels = ins[0].shape[1]

    def both(first, second):
        return jnp.concatenate([first[...], second[...]], axis=1)

    for n, places in enumerate(plan):
        panels = [ins[array].at[pl.ds(i * lon_dev, lon_dev), :] for array, i in places]

        def times(offset, panel):
            return jnp.dot(block_ref[n, 2 + offset], panel, preferred_element_type=jnp.float32)[:lon_dev]

        def halves(first, second):
            return jnp.concatenate([first, second], axis=1)

        nothing = jnp.zeros((lon_dev, channels), jnp.float32)
        same = side == along
        if phase != "late":
            own, other, x_own, x_other = panels[:4]
            row = rows_ref[base + n]
            line = active_line(line_ref, row, widths_ref[row], 3 * lon_dev)
            for s in range(5):
                block_ref[n, s] = toeplitz(line, (s + 1) * lon_dev, lon_dev, lon_dev)
            here = both(own, other)
            total = here.astype(jnp.float32) + times(0, here)
            total += times(2 * along, both(x_own, x_other))
            total += jnp.concatenate([times(side, other[...]), times(-side, own[...])], axis=1)
            more = times(along, jnp.where(same, x_own[...], x_other[...]))
            total += halves(jnp.where(same, nothing, more), jnp.where(same, more, nothing))
            if phase == "early":
                total_ref[n] = total
        if phase != "early":
            z_own, z_other = panels[-2:]
            if phase == "late":
                total = total_in[n]
            total += times(-2 * along, both(z_own, z_other))
            more = times(-along, jnp.where(same, z_other[...], z_own[...]))
            total += halves(jnp.where(same, more, nothing), jnp.where(same, nothing, more))
            here = pl.ds(n * lon_dev, lon_dev)
            out_own[here, :] = total[:, :channels].astype(out_own.dtype)
            out_other[here, :] = total[:, channels:].astype(out_other.dtype)


def filter_pair(scalars, lines, places, base, lon_dev, phase="whole", early=()):
    arrays = []
    plan = []
    for row in places:
        found = []
        for array, i in row:
            at = next((n for n, a in enumerate(arrays) if a is array), len(arrays))
            if at == len(arrays):
                arrays.append(array)
            found.append((at, i))
        plan.append(tuple(found))
    count = len(plan)
    channels = arrays[0].shape[1]
    total = (count, lon_dev, 2 * channels), jnp.float32
    block = (count, 5, up_to(lon_dev, 96), lon_dev), jnp.bfloat16
    out = jax.ShapeDtypeStruct((count * lon_dev, channels), arrays[0].dtype)
    first = [lines] if phase != "late" else list(early)
    if phase == "early":
        outs, scratch = [jax.ShapeDtypeStruct(*total), jax.ShapeDtypeStruct(*block)], []
    elif phase == "late":
        outs, scratch = [out, out], []
    else:
        outs, scratch = [out, out], [pltpu.VMEM(*block)]
    weight = {"whole": 10, "early": 7, "late": 3}[phase]
    return pl.pallas_call(
        functools.partial(pair_kernel, lon_dev, base, tuple(plan), phase),
        out_shape=outs,
        in_specs=[SMEM_SPEC] * 3 + [VMEM_SPEC] * (len(first) + len(arrays)),
        out_specs=[VMEM_SPEC] * len(outs),
        scratch_shapes=scratch,
        compiler_params=pltpu.CompilerParams(vmem_limit_bytes=VMEM_LIMIT),
        cost_estimate=pl.CostEstimate(
            flops=FLOPS * count * weight * 256 * 256 * 768,
            bytes_accessed=16 * count * lon_dev * channels,
            transcendentals=0,
        ),
        name="filter_" + phase,
    )(*scalars, *first, *arrays)


def chip_aware(fields, owner_slot, widths, tap_weights):
    lat_dev, lon_dev, channels = fields.shape
    n_lon = lax.axis_size("lon")
    at = lax.axis_index("lon")
    band = lax.axis_index("lat")
    core, x = at % 2, at // 2 % 2
    place = jnp.concatenate([jnp.stack([band, core, x]).astype(jnp.int32), owner_slot])
    chunks = STAY + STAY + COME + COME
    taken = take_rows(jnp.transpose(fields, (1, 0, 2)), place, chunks)
    n_stay, n_come = len(STAY), len(COME)
    keep, give = taken[:n_stay], taken[n_stay : 2 * n_stay]
    straight, cross = taken[2 * n_stay : 2 * n_stay + n_come], taken[2 * n_stay + n_come :]

    across_core = [(i, i ^ 1) for i in range(n_lon)]
    across_x = [(i, i ^ 2) for i in range(n_lon)]
    across_x_core = [(i, i ^ 3) for i in range(n_lon)]
    across_z = [(i, (i + (4 if i // 2 % 2 == 0 else -4)) % n_lon) for i in range(n_lon)]
    back_z = [(i, (i + (-4 if i // 2 % 2 == 0 else 4)) % n_lon) for i in range(n_lon)]
    across_y = [(i, i ^ 1) for i in range(2 * n_lon)]
    across_both = [(i, i ^ 3) for i in range(2 * n_lon)]

    lines = tap_lines(tap_weights, 3 * lon_dev)
    rows, slots = list_rows(place, lat_dev)
    scalars = rows, place, widths
    sizes = STAY + COME
    starts = [sum(sizes[:c]) for c in range(len(sizes))]
    done = {}

    def get(kind, i):
        if (kind, i) in done:
            return done[kind, i]

        def moved(operand, axes, pairs):
            first = [get(*g)[0] if g[0] in "ft" else get(*g) for g in WAITS.get((kind, i), ())]
            if first:
                operand = lax.optimization_barrier((operand, *first))[0]
            return lax.ppermute(operand, axes, pairs)

        if kind == "k":
            result = keep[i]
        elif kind == "l":
            result = (rows, lines)[i]
        elif kind == "c":
            result = moved(give[i], "lon", across_core)
        elif kind == "y":
            operand, pairs = ((straight, across_y), (cross, across_both))[i % 2]
            result = moved(operand[i // 2], ("lon", "lat"), pairs)
        elif kind == "x":
            result = moved(get(*PARTS[i]), "lon", across_x)
        elif kind == "z":
            result = moved(get("x", i), "lon", across_z)
        elif kind == "p":
            operand, pairs = ((keep[1], across_x), (give[1], across_x_core))[i]
            result = moved(operand, "lon", pairs)
        elif kind == "q":
            operand = get(*(("k", 0), ("c", 0), ("p", 0), ("p", 1))[i])
            result = moved(operand, "lon", back_z if i < 2 else across_z)
        elif kind == "t":
            here = [get("k", 0), get("c", 0)]
            beside = [get("p", 0), get("p", 1)]
            if i == 0:
                panels = here + beside + [get("q", 2), get("q", 3)]
            else:
                panels = beside + [get("q", 0), get("q", 1)] + here
            places = [[(p, row) for p in panels] for row in range(STAY[0])]
            result = filter_pair(scalars, lines, places, 0, lon_dev)
        elif kind == "b":
            operand, pairs = ((get("t", 0)[1], across_core), (get("t", 1)[0], across_x), (get("t", 1)[1], across_x_core))[i]
            result = moved(operand, "lon", pairs)
        elif kind == "f":
            places = []
            for row in FILTERS[i]:
                chunk, index = next((c, row - at) for c, at in enumerate(starts) if at <= row < at + sizes[c])
                if chunk < n_stay:
                    pair = ("k", chunk), ("c", chunk)
                else:
                    pair = ("y", 2 * (chunk - n_stay)), ("y", 2 * (chunk - n_stay) + 1)
                parts = [get(*p) for p in pair]
                parts += [get(axis, PARTS.index(p)) for axis in "xz" for p in pair]
                places.append([(p, index) for p in parts])
            base = FILTERS[i][0]
            if i < len(FILTERS) - 1:
                result = filter_pair(scalars, lines, places, base, lon_dev)
            else:
                early = filter_pair(scalars, lines, [p[:4] for p in places], base, lon_dev, "early")
                result = filter_pair(scalars, lines, [p[4:] for p in places], base, lon_dev, "late", early)
        else:
            result = moved(get("f", i)[1], "lon", across_core)
        done[kind, i] = result
        return result

    mine = [get("t", 0)[0], get("b", 1)] + [get("f", i)[0] for i in range(len(FILTERS))]
    theirs = [get("b", 0), get("b", 2)] + [get("o", i) for i in range(len(FILTERS))]
    out = put_rows(mine + theirs, slots, lon_dev, lat_dev)
    return jnp.transpose(out, (1, 0, 2))


def filter_kernel(reach, rows_ref, slots_ref, sector_ref, widths_ref, line_ref, *refs):
    ins, out_ref = refs[:-1], refs[-1]
    lon_dev, channels = out_ref.shape[1:]
    row = rows_ref[pl.program_id(0)]
    line = active_line(line_ref, row, widths_ref[row], (reach + 1) * lon_dev)
    total = ins[0][0].astype(jnp.float32)
    for group, ref in enumerate(ins):
        block = toeplitz(line, (sector_ref[group] + 1) * lon_dev, lon_dev, lon_dev)
        total += jnp.dot(block, ref[0], preferred_element_type=jnp.float32)[:lon_dev]
    out_ref[0] = total.astype(out_ref.dtype)


def filter_rows(rows, slots, sectors, widths, lines, arrays, reach):
    lat_dev, lon_dev, channels = arrays[0].shape
    row_spec = pl.BlockSpec((1, lon_dev, channels), lambda i, rows, slots, sectors, widths: (i, 0, 0))
    line_spec = pl.BlockSpec(lines.shape, lambda i, rows, slots, sectors, widths: (0, 0))
    out_spec = pl.BlockSpec((1, lon_dev, channels), lambda i, rows, slots, sectors, widths: (slots[i], 0, 0))
    return pl.pallas_call(
        functools.partial(filter_kernel, reach),
        out_shape=jax.ShapeDtypeStruct(arrays[0].shape, arrays[0].dtype),
        grid_spec=pltpu.PrefetchScalarGridSpec(
            num_scalar_prefetch=4,
            grid=(lat_dev,),
            in_specs=[line_spec] + [row_spec] * len(arrays),
            out_specs=out_spec,
        ),
        compiler_params=pltpu.CompilerParams(vmem_limit_bytes=VMEM_LIMIT),
        name="filter_rows",
    )(rows, slots, sectors, widths, lines, *arrays)


def any_mesh(fields, owner_slot, widths, tap_weights):
    lat_dev, lon_dev, channels = fields.shape
    n_lon = lax.axis_size("lon")
    n_lat = lax.axis_size("lat")
    reach = n_lon // 8
    band = lax.axis_index("lat")
    dest_band = owner_slot // lat_dev
    home_rows = band * lat_dev + jnp.arange(lat_dev, dtype=jnp.int32)
    ordering = jnp.argsort(dest_band[home_rows], stable=True)
    rows = jnp.argsort((dest_band != band).astype(jnp.int32), stable=True)[:lat_dev].astype(jnp.int32)
    slots = (owner_slot[rows] % lat_dev).astype(jnp.int32)
    outgoing = fields[ordering].reshape(n_lat, lat_dev // n_lat, lon_dev, channels)
    incoming = lax.all_to_all(outgoing, "lat", split_axis=0, concat_axis=0, tiled=True)
    own = incoming.reshape(lat_dev, lon_dev, channels)
    lines = tap_lines(tap_weights, (reach + 1) * lon_dev)
    arrays, order = [own], [reach]
    ahead = behind = own
    for step in range(1, reach + 1):
        ahead = shift_by(ahead, "lon", -1)
        behind = shift_by(behind, "lon", 1)
        arrays += [ahead, behind]
        order += [reach + step, reach - step]
    sectors = jnp.array(order, jnp.int32)
    return filter_rows(rows, slots, sectors, widths, lines, arrays, reach)


def solution(mesh):
    in_specs = (P("lat", "lon", None), P(), P(), P())
    out_specs = P("lat", "lon", None)
    chips = (mesh.shape["lon"], mesh.shape["lat"]) == (16, 2)

    def body(fields, owner_slot, widths, tap_weights):
        fits = chips and fields.shape[0] == 4 * sum(STAY)
        form = chip_aware if fits else any_mesh
        return form(fields, owner_slot, widths, tap_weights)

    return jax.shard_map(body, mesh=mesh, in_specs=in_specs, out_specs=out_specs, check_vma=False)
```

```python
import functools

import jax
import jax.numpy as jnp
from jax import lax
from jax.experimental import pallas as pl
from jax.experimental.pallas import tpu as pltpu
from jax.sharding import PartitionSpec as P

VMEM_LIMIT = 12 * 1024 * 1024
TAKE_VMEM_LIMIT = 50 * 1024 * 1024
PIECE = 3
AHEAD = 2
SMEM_SPEC = pl.BlockSpec(memory_space=pltpu.SMEM)
VMEM_SPEC = pl.BlockSpec(memory_space=pltpu.VMEM)
HBM_SPEC = pl.BlockSpec(memory_space=pltpu.HBM)
STAY = (2, 2)
COME = (2, 2)
PARTS = [("y", 0), ("y", 1), ("y", 2), ("y", 3)]
FILTERS = ((4, 5), (6, 7))
WAITS = {
    ("x", 0): [("p", 0), ("y", 0)],
    ("x", 1): [("p", 1)],
    ("b", 2): [("x", 3)],
    ("q", 2): [("q", 0), ("l", 0), ("l", 1)],
    ("q", 3): [("q", 1)],
    ("z", 0): [("q", 2), ("q", 1)],
    ("z", 1): [("q", 3), ("t", 1)],
    ("z", 2): [("z", 0)],
    ("z", 3): [("z", 1)],
    ("y", 2): [("y", 0), ("p", 0)],
    ("y", 3): [("y", 1), ("x", 0)],
    ("y", 1): [("q", 0)],
}
FLOPS = 3


def up_to(value, multiple):
    return -(-value // multiple) * multiple


def shift_by(x, axis, by):
    count = lax.axis_size(axis)
    return lax.ppermute(x, axis, [(i, (i + by) % count) for i in range(count)])


def line_kernel(behind, taps_ref, line_ref):
    circle = taps_ref.shape[1]
    rows, lanes = line_ref.shape
    taps = taps_ref[...].astype(jnp.float32)
    pieces = [taps[:, circle - behind :], taps[:, :behind]]
    if lanes > 2 * behind:
        pieces.append(jnp.zeros((rows, lanes - 2 * behind), jnp.float32))
    line_ref[...] = jnp.concatenate(pieces, axis=1)


def tap_lines(tap_weights, behind):
    rows = tap_weights.shape[0]
    lanes = up_to(2 * behind, 128)
    return pl.pallas_call(
        functools.partial(line_kernel, behind),
        out_shape=jax.ShapeDtypeStruct((rows, lanes), jnp.float32),
        in_specs=[VMEM_SPEC],
        out_specs=VMEM_SPEC,
        compiler_params=pltpu.CompilerParams(vmem_limit_bytes=VMEM_LIMIT),
        cost_estimate=pl.CostEstimate(flops=0, bytes_accessed=2 * tap_weights.size, transcendentals=0),
        name="tap_lines",
    )(tap_weights)


def active_line(line_ref, row, width, behind):
    line = jnp.broadcast_to(line_ref[pl.ds(row, 1), :], (8, line_ref.shape[1]))
    distance = jnp.abs(lax.broadcasted_iota(jnp.int32, line.shape, 1) - behind)
    return jnp.where(distance <= width, line, 0.0)


def toeplitz(line, at, lon_dev, width):
    lanes = up_to(width, 128) + 128
    step = min(up_to(lon_dev, 16), 96)
    bands = []
    for start in range(0, up_to(lon_dev, step), step):
        taps = pltpu.roll(line, line.shape[1] + start - at, 1)
        taps = jnp.concatenate([taps[:, : lanes - 128], taps[:, -128:]], axis=1)
        band = pltpu.roll(jnp.concatenate([taps] * (step // 8), axis=0), 0, 1, stride=1, stride_axis=0)
        bands.append(band[:, :width].astype(jnp.bfloat16))
    return jnp.concatenate(bands, axis=0)


def listed(n, quarter, core):
    within = n % quarter
    return within + jnp.where(n // quarter == core, 0, quarter)


def traded(n, quarter, x):
    within = n % quarter
    return n - within + (within + quarter // 2 * x) % quarter


def list_kernel(lat_dev, place_ref, rows_ref, slots_ref):
    half, quarter = lat_dev // 2, lat_dev // 4
    band, core, x = place_ref[0], place_ref[1], place_ref[2]
    stay, come = jnp.int32(0), jnp.int32(0)
    for j in range(lat_dev):
        here = band * lat_dev + j
        there = (1 - band) * lat_dev + j
        stays = place_ref[3 + here] // lat_dev == band
        comes = place_ref[3 + there] // lat_dev == band

        spot = traded(listed(stay, quarter, core), quarter, x)
        spot = jnp.where(stays, spot + jnp.where(spot >= quarter, quarter, 0), lat_dev)
        rows_ref[spot] = here
        slots_ref[spot] = place_ref[3 + here] % lat_dev
        spot = listed(come, quarter, core)
        spot = jnp.where(comes, spot + jnp.where(spot >= quarter, half, quarter), lat_dev)
        rows_ref[spot] = there
        slots_ref[spot] = place_ref[3 + there] % lat_dev
        stay = stay + stays.astype(jnp.int32)
        come = come + comes.astype(jnp.int32)


def list_rows(place, lat_dev):
    ints = jax.ShapeDtypeStruct((lat_dev + 1,), jnp.int32)
    return pl.pallas_call(
        functools.partial(list_kernel, lat_dev),
        out_shape=[ints, ints],
        in_specs=[SMEM_SPEC],
        out_specs=[SMEM_SPEC, SMEM_SPEC],
        compiler_params=pltpu.CompilerParams(vmem_limit_bytes=VMEM_LIMIT),
        cost_estimate=pl.CostEstimate(flops=0, bytes_accessed=256, transcendentals=0),
        name="list_rows",
    )(place)


def take_kernel(chunks, lat_dev, block, place_ref, fields_ref, *refs):
    outs = refs[: len(chunks)]
    home_ref, take_ref, panel_ref, sems = refs[len(chunks) :]
    lon_dev, _, channels = fields_ref.shape
    half, quarter = lat_dev // 2, lat_dev // 4
    copies = []
    for n, start in enumerate(range(0, lon_dev, PIECE * block)):
        window = pl.ds(start, min(PIECE * block, lon_dev - start))
        copies.append(pltpu.make_async_copy(fields_ref.at[window], panel_ref.at[window], sems.at[n]))
    for copy in copies[:AHEAD]:
        copy.start()

    band, core, x = place_ref[0], place_ref[1], place_ref[2]
    stay, leave = jnp.int32(0), jnp.int32(0)
    for j in range(lat_dev):
        stays = place_ref[3 + band * lat_dev + j] // lat_dev == band
        spot = traded(listed(stay, quarter, core), quarter, x)
        home_ref[jnp.where(stays, spot, half + listed(leave, quarter, core))] = jnp.int32(j)
        stay = stay + stays.astype(jnp.int32)
        leave = leave + 1 - stays.astype(jnp.int32)

    def selector(lon):
        row = lax.broadcasted_iota(jnp.int32, (lat_dev * lon, 128), 0)
        if lon % 8 == 0:
            home = jnp.concatenate([jnp.full((lon, 128), home_ref[p], jnp.int32) for p in range(lat_dev)], axis=0)
        else:
            home = sum(jnp.where(row // lon == p, home_ref[p], 0) for p in range(lat_dev))
        wanted = row % lon * lat_dev + home
        column = lax.broadcasted_iota(jnp.int32, (lat_dev * lon, lon * lat_dev), 1)
        return jnp.where(column == wanted[:, :1], 1.0, 0.0).astype(jnp.bfloat16)

    take_ref[...] = selector(block)
    rest = lon_dev % block
    small = selector(rest) if rest else None
    for n, start in enumerate(range(0, lon_dev, block)):
        if n % PIECE == 0:
            copies[n // PIECE].wait()
            if n // PIECE + AHEAD < len(copies):
                copies[n // PIECE + AHEAD].start()
        lon = min(block, lon_dev - start)
        panel = panel_ref[start : start + lon].reshape(lon * lat_dev, channels)
        take = take_ref[...] if lon == block else small
        taken = jnp.dot(take, panel, preferred_element_type=jnp.float32)
        place = 0
        for out, count in zip(outs, chunks):
            for i in range(count):
                piece = taken[place * lon : (place + 1) * lon].astype(out.dtype)
                out[i * lon_dev + start : i * lon_dev + start + lon, :] = piece
                place += 1


def take_rows(fields, place, chunks):
    lon_dev, lat_dev, channels = fields.shape
    block = 16
    return pl.pallas_call(
        functools.partial(take_kernel, chunks, lat_dev, block),
        out_shape=[jax.ShapeDtypeStruct((n * lon_dev, channels), fields.dtype) for n in chunks],
        in_specs=[SMEM_SPEC, HBM_SPEC],
        out_specs=[VMEM_SPEC] * len(chunks),
        scratch_shapes=[
            pltpu.SMEM((lat_dev,), jnp.int32),
            pltpu.VMEM((block * lat_dev, block * lat_dev), jnp.bfloat16),
            pltpu.VMEM(fields.shape, fields.dtype),
            pltpu.SemaphoreType.DMA((pl.cdiv(lon_dev, PIECE * block),)),
        ],
        compiler_params=pltpu.CompilerParams(vmem_limit_bytes=TAKE_VMEM_LIMIT),
        cost_estimate=pl.CostEstimate(
            flops=2 * fields.size * block * lat_dev, bytes_accessed=4 * fields.size, transcendentals=0
        ),
        name="take_rows",
    )(place, fields)


def put_kernel(counts, lat_dev, block, slots_ref, *refs):
    ins, (out_ref, panel_ref, sems) = refs[:-3], refs[-3:]
    lon_dev, _, channels = out_ref.shape

    def selector(lon):
        row = lax.broadcasted_iota(jnp.int32, (lon * lat_dev, lat_dev * lon), 0)
        column = lax.broadcasted_iota(jnp.int32, (8, lat_dev * lon), 1)
        wanted = column % lon * lat_dev
        for p in range(lat_dev):
            wanted += jnp.where(column // lon == p, slots_ref[p], 0)
        return jnp.where(row == wanted[:1], 1.0, 0.0).astype(jnp.bfloat16)

    whole = selector(block)
    rest = lon_dev % block
    small = selector(rest) if rest else None
    copies = []
    for n, start in enumerate(range(0, lon_dev, block)):
        lon = min(block, lon_dev - start)
        pieces = [r[i * lon_dev + start : i * lon_dev + start + lon, :] for r, count in zip(ins, counts) for i in range(count)]
        if lon < block:
            pieces = [p.astype(jnp.float32) for p in pieces]
        panel = jnp.concatenate(pieces, axis=0).astype(jnp.bfloat16)
        spread = jnp.dot(whole if lon == block else small, panel, preferred_element_type=jnp.float32)
        window = pl.ds(start, lon)
        panel_ref[window] = spread.astype(jnp.bfloat16).reshape(lon, lat_dev, channels)
        copies.append(pltpu.make_async_copy(panel_ref.at[window], out_ref.at[window], sems.at[n]))
        copies[-1].start()
    for copy in copies:
        copy.wait()


def put_rows(panels, slots, lon_dev, lat_dev):
    channels = panels[0].shape[1]
    block = 16
    counts = tuple(p.shape[0] // lon_dev for p in panels)
    shape = (lon_dev, lat_dev, channels)
    return pl.pallas_call(
        functools.partial(put_kernel, counts, lat_dev, block),
        out_shape=jax.ShapeDtypeStruct(shape, panels[0].dtype),
        in_specs=[SMEM_SPEC] + [VMEM_SPEC] * len(panels),
        out_specs=HBM_SPEC,
        scratch_shapes=[
            pltpu.VMEM(shape, panels[0].dtype),
            pltpu.SemaphoreType.DMA((pl.cdiv(lon_dev, block),)),
        ],
        compiler_params=pltpu.CompilerParams(vmem_limit_bytes=VMEM_LIMIT),
        cost_estimate=pl.CostEstimate(
            flops=2 * lon_dev * lat_dev * channels * block * lat_dev,
            bytes_accessed=4 * lon_dev * lat_dev * channels,
            transcendentals=0,
        ),
        name="put_rows",
    )(slots, *panels)


def pair_kernel(lon_dev, base, plan, phase, rows_ref, place_ref, widths_ref, *refs):
    count = len(plan)
    side, along = 1 - 2 * place_ref[1], 1 - 2 * place_ref[2]
    if phase == "late":
        (total_in, block_ref), refs = refs[:2], refs[2:]
    else:
        line_ref, refs = refs[0], refs[1:]
    if phase == "early":
        ins, (total_ref, block_ref) = refs[:-2], refs[-2:]
    elif phase == "late":
        ins, (out_own, out_other) = refs[:-2], refs[-2:]
    else:
        ins, (out_own, out_other, block_ref) = refs[:-3], refs[-3:]
    channels = ins[0].shape[1]

    def both(first, second):
        return jnp.concatenate([first[...], second[...]], axis=1)

    for n, places in enumerate(plan):
        panels = [ins[array].at[pl.ds(i * lon_dev, lon_dev), :] for array, i in places]

        def times(offset, panel):
            return jnp.dot(block_ref[n, 2 + offset], panel, preferred_element_type=jnp.float32)[:lon_dev]

        def halves(first, second):
            return jnp.concatenate([first, second], axis=1)

        nothing = jnp.zeros((lon_dev, channels), jnp.float32)
        same = side == along
        if phase != "late":
            own, other, x_own, x_other = panels[:4]
            row = rows_ref[base + n]
            line = active_line(line_ref, row, widths_ref[row], 3 * lon_dev)
            for s in range(5):
                block_ref[n, s] = toeplitz(line, (s + 1) * lon_dev, lon_dev, lon_dev)
            here = both(own, other)
            total = here.astype(jnp.float32) + times(0, here)
            total += times(2 * along, both(x_own, x_other))
            total += jnp.concatenate([times(side, other[...]), times(-side, own[...])], axis=1)
            more = times(along, jnp.where(same, x_own[...], x_other[...]))
            total += halves(jnp.where(same, nothing, more), jnp.where(same, more, nothing))
            if phase == "early":
                total_ref[n] = total
        if phase != "early":
            z_own, z_other = panels[-2:]
            if phase == "late":
                total = total_in[n]
            total += times(-2 * along, both(z_own, z_other))
            more = times(-along, jnp.where(same, z_other[...], z_own[...]))
            total += halves(jnp.where(same, more, nothing), jnp.where(same, nothing, more))
            here = pl.ds(n * lon_dev, lon_dev)
            out_own[here, :] = total[:, :channels].astype(out_own.dtype)
            out_other[here, :] = total[:, channels:].astype(out_other.dtype)


def filter_pair(scalars, lines, places, base, lon_dev, phase="whole", early=()):
    arrays = []
    plan = []
    for row in places:
        found = []
        for array, i in row:
            at = next((n for n, a in enumerate(arrays) if a is array), len(arrays))
            if at == len(arrays):
                arrays.append(array)
            found.append((at, i))
        plan.append(tuple(found))
    count = len(plan)
    channels = arrays[0].shape[1]
    total = (count, lon_dev, 2 * channels), jnp.float32
    block = (count, 5, up_to(lon_dev, 96), lon_dev), jnp.bfloat16
    out = jax.ShapeDtypeStruct((count * lon_dev, channels), arrays[0].dtype)
    first = [lines] if phase != "late" else list(early)
    if phase == "early":
        outs, scratch = [jax.ShapeDtypeStruct(*total), jax.ShapeDtypeStruct(*block)], []
    elif phase == "late":
        outs, scratch = [out, out], []
    else:
        outs, scratch = [out, out], [pltpu.VMEM(*block)]
    weight = {"whole": 10, "early": 7, "late": 3}[phase]
    return pl.pallas_call(
        functools.partial(pair_kernel, lon_dev, base, tuple(plan), phase),
        out_shape=outs,
        in_specs=[SMEM_SPEC] * 3 + [VMEM_SPEC] * (len(first) + len(arrays)),
        out_specs=[VMEM_SPEC] * len(outs),
        scratch_shapes=scratch,
        compiler_params=pltpu.CompilerParams(vmem_limit_bytes=VMEM_LIMIT),
        cost_estimate=pl.CostEstimate(
            flops=FLOPS * count * weight * 256 * 256 * 768,
            bytes_accessed=16 * count * lon_dev * channels,
            transcendentals=0,
        ),
        name="filter_" + phase,
    )(*scalars, *first, *arrays)


def chip_aware(fields, owner_slot, widths, tap_weights):
    lat_dev, lon_dev, channels = fields.shape
    n_lon = lax.axis_size("lon")
    at = lax.axis_index("lon")
    band = lax.axis_index("lat")
    core, x = at % 2, at // 2 % 2
    place = jnp.concatenate([jnp.stack([band, core, x]).astype(jnp.int32), owner_slot])
    chunks = STAY + STAY + COME + COME
    taken = take_rows(jnp.transpose(fields, (1, 0, 2)), place, chunks)
    n_stay, n_come = len(STAY), len(COME)
    keep, give = taken[:n_stay], taken[n_stay : 2 * n_stay]
    straight, cross = taken[2 * n_stay : 2 * n_stay + n_come], taken[2 * n_stay + n_come :]

    across_core = [(i, i ^ 1) for i in range(n_lon)]
    across_x = [(i, i ^ 2) for i in range(n_lon)]
    across_x_core = [(i, i ^ 3) for i in range(n_lon)]
    across_z = [(i, (i + (4 if i // 2 % 2 == 0 else -4)) % n_lon) for i in range(n_lon)]
    back_z = [(i, (i + (-4 if i // 2 % 2 == 0 else 4)) % n_lon) for i in range(n_lon)]
    across_y = [(i, i ^ 1) for i in range(2 * n_lon)]
    across_both = [(i, i ^ 3) for i in range(2 * n_lon)]

    lines = tap_lines(tap_weights, 3 * lon_dev)
    rows, slots = list_rows(place, lat_dev)
    scalars = rows, place, widths
    sizes = STAY + COME
    starts = [sum(sizes[:c]) for c in range(len(sizes))]
    done = {}

    def get(kind, i):
        if (kind, i) in done:
            return done[kind, i]

        def moved(operand, axes, pairs):
            first = [get(*g)[0] if g[0] in "ft" else get(*g) for g in WAITS.get((kind, i), ())]
            if first:
                operand = lax.optimization_barrier((operand, *first))[0]
            return lax.ppermute(operand, axes, pairs)

        if kind == "k":
            result = keep[i]
        elif kind == "l":
            result = (rows, lines)[i]
        elif kind == "c":
            result = moved(give[i], "lon", across_core)
        elif kind == "y":
            operand, pairs = ((straight, across_y), (cross, across_both))[i % 2]
            result = moved(operand[i // 2], ("lon", "lat"), pairs)
        elif kind == "x":
            result = moved(get(*PARTS[i]), "lon", across_x)
        elif kind == "z":
            result = moved(get("x", i), "lon", across_z)
        elif kind == "p":
            operand, pairs = ((keep[1], across_x), (give[1], across_x_core))[i]
            result = moved(operand, "lon", pairs)
        elif kind == "q":
            operand = get(*(("k", 0), ("c", 0), ("p", 0), ("p", 1))[i])
            result = moved(operand, "lon", back_z if i < 2 else across_z)
        elif kind == "t":
            here = [get("k", 0), get("c", 0)]
            beside = [get("p", 0), get("p", 1)]
            if i == 0:
                panels = here + beside + [get("q", 2), get("q", 3)]
            else:
                panels = beside + [get("q", 0), get("q", 1)] + here
            places = [[(p, row) for p in panels] for row in range(STAY[0])]
            result = filter_pair(scalars, lines, places, 0, lon_dev)
        elif kind == "b":
            operand, pairs = ((get("t", 0)[1], across_core), (get("t", 1)[0], across_x), (get("t", 1)[1], across_x_core))[i]
            result = moved(operand, "lon", pairs)
        elif kind == "f":
            places = []
            for row in FILTERS[i]:
                chunk, index = next((c, row - at) for c, at in enumerate(starts) if at <= row < at + sizes[c])
                if chunk < n_stay:
                    pair = ("k", chunk), ("c", chunk)
                else:
                    pair = ("y", 2 * (chunk - n_stay)), ("y", 2 * (chunk - n_stay) + 1)
                parts = [get(*p) for p in pair]
                parts += [get(axis, PARTS.index(p)) for axis in "xz" for p in pair]
                places.append([(p, index) for p in parts])
            base = FILTERS[i][0]
            if i < len(FILTERS) - 1:
                result = filter_pair(scalars, lines, places, base, lon_dev)
            else:
                early = filter_pair(scalars, lines, [p[:4] for p in places], base, lon_dev, "early")
                result = filter_pair(scalars, lines, [p[4:] for p in places], base, lon_dev, "late", early)
        else:
            result = moved(get("f", i)[1], "lon", across_core)
        done[kind, i] = result
        return result

    mine = [get("t", 0)[0], get("b", 1)] + [get("f", i)[0] for i in range(len(FILTERS))]
    theirs = [get("b", 0), get("b", 2)] + [get("o", i) for i in range(len(FILTERS))]
    out = put_rows(mine + theirs, slots, lon_dev, lat_dev)
    return jnp.transpose(out, (1, 0, 2))


def filter_kernel(reach, rows_ref, slots_ref, sector_ref, widths_ref, line_ref, *refs):
    ins, out_ref = refs[:-1], refs[-1]
    lon_dev, channels = out_ref.shape[1:]
    row = rows_ref[pl.program_id(0)]
    line = active_line(line_ref, row, widths_ref[row], (reach + 1) * lon_dev)
    total = ins[0][0].astype(jnp.float32)
    for group, ref in enumerate(ins):
        block = toeplitz(line, (sector_ref[group] + 1) * lon_dev, lon_dev, lon_dev)
        total += jnp.dot(block, ref[0], preferred_element_type=jnp.float32)[:lon_dev]
    out_ref[0] = total.astype(out_ref.dtype)


def filter_rows(rows, slots, sectors, widths, lines, arrays, reach):
    lat_dev, lon_dev, channels = arrays[0].shape
    row_spec = pl.BlockSpec((1, lon_dev, channels), lambda i, rows, slots, sectors, widths: (i, 0, 0))
    line_spec = pl.BlockSpec(lines.shape, lambda i, rows, slots, sectors, widths: (0, 0))
    out_spec = pl.BlockSpec((1, lon_dev, channels), lambda i, rows, slots, sectors, widths: (slots[i], 0, 0))
    return pl.pallas_call(
        functools.partial(filter_kernel, reach),
        out_shape=jax.ShapeDtypeStruct(arrays[0].shape, arrays[0].dtype),
        grid_spec=pltpu.PrefetchScalarGridSpec(
            num_scalar_prefetch=4,
            grid=(lat_dev,),
            in_specs=[line_spec] + [row_spec] * len(arrays),
            out_specs=out_spec,
        ),
        compiler_params=pltpu.CompilerParams(vmem_limit_bytes=VMEM_LIMIT),
        name="filter_rows",
    )(rows, slots, sectors, widths, lines, *arrays)


def any_mesh(fields, owner_slot, widths, tap_weights):
    lat_dev, lon_dev, channels = fields.shape
    n_lon = lax.axis_size("lon")
    n_lat = lax.axis_size("lat")
    reach = n_lon // 8
    band = lax.axis_index("lat")
    dest_band = owner_slot // lat_dev
    home_rows = band * lat_dev + jnp.arange(lat_dev, dtype=jnp.int32)
    ordering = jnp.argsort(dest_band[home_rows], stable=True)
    rows = jnp.argsort((dest_band != band).astype(jnp.int32), stable=True)[:lat_dev].astype(jnp.int32)
    slots = (owner_slot[rows] % lat_dev).astype(jnp.int32)
    outgoing = fields[ordering].reshape(n_lat, lat_dev // n_lat, lon_dev, channels)
    incoming = lax.all_to_all(outgoing, "lat", split_axis=0, concat_axis=0, tiled=True)
    own = incoming.reshape(lat_dev, lon_dev, channels)
    lines = tap_lines(tap_weights, (reach + 1) * lon_dev)
    arrays, order = [own], [reach]
    ahead = behind = own
    for step in range(1, reach + 1):
        ahead = shift_by(ahead, "lon", -1)
        behind = shift_by(behind, "lon", 1)
        arrays += [ahead, behind]
        order += [reach + step, reach - step]
    sectors = jnp.array(order, jnp.int32)
    return filter_rows(rows, slots, sectors, widths, lines, arrays, reach)


def solution(mesh):
    in_specs = (P("lat", "lon", None), P(), P(), P())
    out_specs = P("lat", "lon", None)
    chips = (mesh.shape["lon"], mesh.shape["lat"]) == (16, 2)

    def body(fields, owner_slot, widths, tap_weights):
        fits = chips and fields.shape[0] == 4 * sum(STAY)
        form = chip_aware if fits else any_mesh
        return form(fields, owner_slot, widths, tap_weights)

    return jax.shard_map(body, mesh=mesh, in_specs=in_specs, out_specs=out_specs, check_vma=False)
```

```python
import functools

import jax
import jax.numpy as jnp
from jax import lax
from jax.experimental import pallas as pl
from jax.experimental.pallas import tpu as pltpu
from jax.sharding import PartitionSpec as P

VMEM_LIMIT = 12 * 1024 * 1024
TAKE_VMEM_LIMIT = 50 * 1024 * 1024
PIECE = 3
AHEAD = 4
SMEM_SPEC = pl.BlockSpec(memory_space=pltpu.SMEM)
VMEM_SPEC = pl.BlockSpec(memory_space=pltpu.VMEM)
HBM_SPEC = pl.BlockSpec(memory_space=pltpu.HBM)
STAY = (2, 2)
COME = (2, 2)
PARTS = [("y", 0), ("y", 1), ("y", 2), ("y", 3)]
FILTERS = ((4, 5), (6, 7))
WAITS = {
    ("x", 0): [("p", 0), ("y", 0)],
    ("x", 1): [("p", 1)],
    ("b", 2): [("x", 3)],
    ("q", 2): [("q", 0), ("l", 0), ("l", 1)],
    ("q", 3): [("q", 1)],
    ("z", 0): [("q", 2), ("q", 1)],
    ("z", 1): [("q", 3), ("t", 1)],
    ("z", 2): [("z", 0)],
    ("z", 3): [("z", 1)],
    ("y", 2): [("y", 0), ("p", 0)],
    ("y", 3): [("y", 1), ("x", 0)],
    ("y", 1): [("q", 0)],
}
FLOPS = 3


def up_to(value, multiple):
    return -(-value // multiple) * multiple


def shift_by(x, axis, by):
    count = lax.axis_size(axis)
    return lax.ppermute(x, axis, [(i, (i + by) % count) for i in range(count)])


def line_kernel(behind, taps_ref, line_ref):
    circle = taps_ref.shape[1]
    rows, lanes = line_ref.shape
    taps = taps_ref[...].astype(jnp.float32)
    pieces = [taps[:, circle - behind :], taps[:, :behind]]
    if lanes > 2 * behind:
        pieces.append(jnp.zeros((rows, lanes - 2 * behind), jnp.float32))
    line_ref[...] = jnp.concatenate(pieces, axis=1)


def tap_lines(tap_weights, behind):
    rows = tap_weights.shape[0]
    lanes = up_to(2 * behind, 128)
    return pl.pallas_call(
        functools.partial(line_kernel, behind),
        out_shape=jax.ShapeDtypeStruct((rows, lanes), jnp.float32),
        in_specs=[VMEM_SPEC],
        out_specs=VMEM_SPEC,
        compiler_params=pltpu.CompilerParams(vmem_limit_bytes=VMEM_LIMIT),
        cost_estimate=pl.CostEstimate(flops=0, bytes_accessed=2 * tap_weights.size, transcendentals=0),
        name="tap_lines",
    )(tap_weights)


def active_line(line_ref, row, width, behind):
    line = jnp.broadcast_to(line_ref[pl.ds(row, 1), :], (8, line_ref.shape[1]))
    distance = jnp.abs(lax.broadcasted_iota(jnp.int32, line.shape, 1) - behind)
    return jnp.where(distance <= width, line, 0.0)


def toeplitz(line, at, lon_dev, width):
    lanes = up_to(width, 128) + 128
    step = min(up_to(lon_dev, 16), 96)
    bands = []
    for start in range(0, up_to(lon_dev, step), step):
        taps = pltpu.roll(line, line.shape[1] + start - at, 1)
        taps = jnp.concatenate([taps[:, : lanes - 128], taps[:, -128:]], axis=1)
        band = pltpu.roll(jnp.concatenate([taps] * (step // 8), axis=0), 0, 1, stride=1, stride_axis=0)
        bands.append(band[:, :width].astype(jnp.bfloat16))
    return jnp.concatenate(bands, axis=0)


def listed(n, quarter, core):
    within = n % quarter
    return within + jnp.where(n // quarter == core, 0, quarter)


def traded(n, quarter, x):
    within = n % quarter
    return n - within + (within + quarter // 2 * x) % quarter


def list_kernel(lat_dev, place_ref, rows_ref, slots_ref):
    half, quarter = lat_dev // 2, lat_dev // 4
    band, core, x = place_ref[0], place_ref[1], place_ref[2]
    stay, come = jnp.int32(0), jnp.int32(0)
    for j in range(lat_dev):
        here = band * lat_dev + j
        there = (1 - band) * lat_dev + j
        stays = place_ref[3 + here] // lat_dev == band
        comes = place_ref[3 + there] // lat_dev == band

        spot = traded(listed(stay, quarter, core), quarter, x)
        spot = jnp.where(stays, spot + jnp.where(spot >= quarter, quarter, 0), lat_dev)
        rows_ref[spot] = here
        slots_ref[spot] = place_ref[3 + here] % lat_dev
        spot = listed(come, quarter, core)
        spot = jnp.where(comes, spot + jnp.where(spot >= quarter, half, quarter), lat_dev)
        rows_ref[spot] = there
        slots_ref[spot] = place_ref[3 + there] % lat_dev
        stay = stay + stays.astype(jnp.int32)
        come = come + comes.astype(jnp.int32)


def list_rows(place, lat_dev):
    ints = jax.ShapeDtypeStruct((lat_dev + 1,), jnp.int32)
    return pl.pallas_call(
        functools.partial(list_kernel, lat_dev),
        out_shape=[ints, ints],
        in_specs=[SMEM_SPEC],
        out_specs=[SMEM_SPEC, SMEM_SPEC],
        compiler_params=pltpu.CompilerParams(vmem_limit_bytes=VMEM_LIMIT),
        cost_estimate=pl.CostEstimate(flops=0, bytes_accessed=256, transcendentals=0),
        name="list_rows",
    )(place)


def take_kernel(chunks, lat_dev, block, place_ref, fields_ref, *refs):
    outs = refs[: len(chunks)]
    home_ref, take_ref, panel_ref, sems = refs[len(chunks) :]
    lon_dev, _, channels = fields_ref.shape
    half, quarter = lat_dev // 2, lat_dev // 4
    copies = []
    for n, start in enumerate(range(0, lon_dev, PIECE * block)):
        window = pl.ds(start, min(PIECE * block, lon_dev - start))
        copies.append(pltpu.make_async_copy(fields_ref.at[window], panel_ref.at[window], sems.at[n]))
    for copy in copies[:AHEAD]:
        copy.start()

    band, core, x = place_ref[0], place_ref[1], place_ref[2]
    stay, leave = jnp.int32(0), jnp.int32(0)
    for j in range(lat_dev):
        stays = place_ref[3 + band * lat_dev + j] // lat_dev == band
        spot = traded(listed(stay, quarter, core), quarter, x)
        home_ref[jnp.where(stays, spot, half + listed(leave, quarter, core))] = jnp.int32(j)
        stay = stay + stays.astype(jnp.int32)
        leave = leave + 1 - stays.astype(jnp.int32)

    def selector(lon):
        row = lax.broadcasted_iota(jnp.int32, (lat_dev * lon, 128), 0)
        if lon % 8 == 0:
            home = jnp.concatenate([jnp.full((lon, 128), home_ref[p], jnp.int32) for p in range(lat_dev)], axis=0)
        else:
            home = sum(jnp.where(row // lon == p, home_ref[p], 0) for p in range(lat_dev))
        wanted = row % lon * lat_dev + home
        column = lax.broadcasted_iota(jnp.int32, (lat_dev * lon, lon * lat_dev), 1)
        return jnp.where(column == wanted[:, :1], 1.0, 0.0).astype(jnp.bfloat16)

    take_ref[...] = selector(block)
    rest = lon_dev % block
    small = selector(rest) if rest else None
    for n, start in enumerate(range(0, lon_dev, block)):
        if n % PIECE == 0:
            copies[n // PIECE].wait()
            if n // PIECE + AHEAD < len(copies):
                copies[n // PIECE + AHEAD].start()
        lon = min(block, lon_dev - start)
        panel = panel_ref[start : start + lon].reshape(lon * lat_dev, channels)
        take = take_ref[...] if lon == block else small
        taken = jnp.dot(take, panel, preferred_element_type=jnp.float32)
        place = 0
        for out, count in zip(outs, chunks):
            for i in range(count):
                piece = taken[place * lon : (place + 1) * lon].astype(out.dtype)
                out[i * lon_dev + start : i * lon_dev + start + lon, :] = piece
                place += 1


def take_rows(fields, place, chunks):
    lon_dev, lat_dev, channels = fields.shape
    block = 16
    return pl.pallas_call(
        functools.partial(take_kernel, chunks, lat_dev, block),
        out_shape=[jax.ShapeDtypeStruct((n * lon_dev, channels), fields.dtype) for n in chunks],
        in_specs=[SMEM_SPEC, HBM_SPEC],
        out_specs=[VMEM_SPEC] * len(chunks),
        scratch_shapes=[
            pltpu.SMEM((lat_dev,), jnp.int32),
            pltpu.VMEM((block * lat_dev, block * lat_dev), jnp.bfloat16),
            pltpu.VMEM(fields.shape, fields.dtype),
            pltpu.SemaphoreType.DMA((pl.cdiv(lon_dev, PIECE * block),)),
        ],
        compiler_params=pltpu.CompilerParams(vmem_limit_bytes=TAKE_VMEM_LIMIT),
        cost_estimate=pl.CostEstimate(
            flops=2 * fields.size * block * lat_dev, bytes_accessed=4 * fields.size, transcendentals=0
        ),
        name="take_rows",
    )(place, fields)


def put_kernel(counts, lat_dev, block, slots_ref, *refs):
    ins, (out_ref, panel_ref, sems) = refs[:-3], refs[-3:]
    lon_dev, _, channels = out_ref.shape

    def selector(lon):
        row = lax.broadcasted_iota(jnp.int32, (lon * lat_dev, lat_dev * lon), 0)
        column = lax.broadcasted_iota(jnp.int32, (8, lat_dev * lon), 1)
        wanted = column % lon * lat_dev
        for p in range(lat_dev):
            wanted += jnp.where(column // lon == p, slots_ref[p], 0)
        return jnp.where(row == wanted[:1], 1.0, 0.0).astype(jnp.bfloat16)

    whole = selector(block)
    rest = lon_dev % block
    small = selector(rest) if rest else None
    copies = []
    for n, start in enumerate(range(0, lon_dev, block)):
        lon = min(block, lon_dev - start)
        pieces = [r[i * lon_dev + start : i * lon_dev + start + lon, :] for r, count in zip(ins, counts) for i in range(count)]
        if lon < block:
            pieces = [p.astype(jnp.float32) for p in pieces]
        panel = jnp.concatenate(pieces, axis=0).astype(jnp.bfloat16)
        spread = jnp.dot(whole if lon == block else small, panel, preferred_element_type=jnp.float32)
        window = pl.ds(start, lon)
        panel_ref[window] = spread.astype(jnp.bfloat16).reshape(lon, lat_dev, channels)
        copies.append(pltpu.make_async_copy(panel_ref.at[window], out_ref.at[window], sems.at[n]))
        copies[-1].start()
    for copy in copies:
        copy.wait()


def put_rows(panels, slots, lon_dev, lat_dev):
    channels = panels[0].shape[1]
    block = 16
    counts = tuple(p.shape[0] // lon_dev for p in panels)
    shape = (lon_dev, lat_dev, channels)
    return pl.pallas_call(
        functools.partial(put_kernel, counts, lat_dev, block),
        out_shape=jax.ShapeDtypeStruct(shape, panels[0].dtype),
        in_specs=[SMEM_SPEC] + [VMEM_SPEC] * len(panels),
        out_specs=HBM_SPEC,
        scratch_shapes=[
            pltpu.VMEM(shape, panels[0].dtype),
            pltpu.SemaphoreType.DMA((pl.cdiv(lon_dev, block),)),
        ],
        compiler_params=pltpu.CompilerParams(vmem_limit_bytes=VMEM_LIMIT),
        cost_estimate=pl.CostEstimate(
            flops=2 * lon_dev * lat_dev * channels * block * lat_dev,
            bytes_accessed=4 * lon_dev * lat_dev * channels,
            transcendentals=0,
        ),
        name="put_rows",
    )(slots, *panels)


def pair_kernel(lon_dev, base, plan, phase, rows_ref, place_ref, widths_ref, *refs):
    count = len(plan)
    side, along = 1 - 2 * place_ref[1], 1 - 2 * place_ref[2]
    if phase == "late":
        (total_in, block_ref), refs = refs[:2], refs[2:]
    else:
        line_ref, refs = refs[0], refs[1:]
    if phase == "early":
        ins, (total_ref, block_ref) = refs[:-2], refs[-2:]
    elif phase == "late":
        ins, (out_own, out_other) = refs[:-2], refs[-2:]
    else:
        ins, (out_own, out_other, block_ref) = refs[:-3], refs[-3:]
    channels = ins[0].shape[1]

    def both(first, second):
        return jnp.concatenate([first[...], second[...]], axis=1)

    for n, places in enumerate(plan):
        panels = [ins[array].at[pl.ds(i * lon_dev, lon_dev), :] for array, i in places]

        def times(offset, panel):
            return jnp.dot(block_ref[n, 2 + offset], panel, preferred_element_type=jnp.float32)[:lon_dev]

        def halves(first, second):
            return jnp.concatenate([first, second], axis=1)

        nothing = jnp.zeros((lon_dev, channels), jnp.float32)
        same = side == along
        if phase != "late":
            own, other, x_own, x_other = panels[:4]
            row = rows_ref[base + n]
            line = active_line(line_ref, row, widths_ref[row], 3 * lon_dev)
            for s in range(5):
                block_ref[n, s] = toeplitz(line, (s + 1) * lon_dev, lon_dev, lon_dev)
            here = both(own, other)
            total = here.astype(jnp.float32) + times(0, here)
            total += times(2 * along, both(x_own, x_other))
            total += jnp.concatenate([times(side, other[...]), times(-side, own[...])], axis=1)
            more = times(along, jnp.where(same, x_own[...], x_other[...]))
            total += halves(jnp.where(same, nothing, more), jnp.where(same, more, nothing))
            if phase == "early":
                total_ref[n] = total
        if phase != "early":
            z_own, z_other = panels[-2:]
            if phase == "late":
                total = total_in[n]
            total += times(-2 * along, both(z_own, z_other))
            more = times(-along, jnp.where(same, z_other[...], z_own[...]))
            total += halves(jnp.where(same, more, nothing), jnp.where(same, nothing, more))
            here = pl.ds(n * lon_dev, lon_dev)
            out_own[here, :] = total[:, :channels].astype(out_own.dtype)
            out_other[here, :] = total[:, channels:].astype(out_other.dtype)


def filter_pair(scalars, lines, places, base, lon_dev, phase="whole", early=()):
    arrays = []
    plan = []
    for row in places:
        found = []
        for array, i in row:
            at = next((n for n, a in enumerate(arrays) if a is array), len(arrays))
            if at == len(arrays):
                arrays.append(array)
            found.append((at, i))
        plan.append(tuple(found))
    count = len(plan)
    channels = arrays[0].shape[1]
    total = (count, lon_dev, 2 * channels), jnp.float32
    block = (count, 5, up_to(lon_dev, 96), lon_dev), jnp.bfloat16
    out = jax.ShapeDtypeStruct((count * lon_dev, channels), arrays[0].dtype)
    first = [lines] if phase != "late" else list(early)
    if phase == "early":
        outs, scratch = [jax.ShapeDtypeStruct(*total), jax.ShapeDtypeStruct(*block)], []
    elif phase == "late":
        outs, scratch = [out, out], []
    else:
        outs, scratch = [out, out], [pltpu.VMEM(*block)]
    weight = {"whole": 10, "early": 7, "late": 3}[phase]
    return pl.pallas_call(
        functools.partial(pair_kernel, lon_dev, base, tuple(plan), phase),
        out_shape=outs,
        in_specs=[SMEM_SPEC] * 3 + [VMEM_SPEC] * (len(first) + len(arrays)),
        out_specs=[VMEM_SPEC] * len(outs),
        scratch_shapes=scratch,
        compiler_params=pltpu.CompilerParams(vmem_limit_bytes=VMEM_LIMIT),
        cost_estimate=pl.CostEstimate(
            flops=FLOPS * count * weight * 256 * 256 * 768,
            bytes_accessed=16 * count * lon_dev * channels,
            transcendentals=0,
        ),
        name="filter_" + phase,
    )(*scalars, *first, *arrays)


def chip_aware(fields, owner_slot, widths, tap_weights):
    lat_dev, lon_dev, channels = fields.shape
    n_lon = lax.axis_size("lon")
    at = lax.axis_index("lon")
    band = lax.axis_index("lat")
    core, x = at % 2, at // 2 % 2
    place = jnp.concatenate([jnp.stack([band, core, x]).astype(jnp.int32), owner_slot])
    chunks = STAY + STAY + COME + COME
    taken = take_rows(jnp.transpose(fields, (1, 0, 2)), place, chunks)
    n_stay, n_come = len(STAY), len(COME)
    keep, give = taken[:n_stay], taken[n_stay : 2 * n_stay]
    straight, cross = taken[2 * n_stay : 2 * n_stay + n_come], taken[2 * n_stay + n_come :]

    across_core = [(i, i ^ 1) for i in range(n_lon)]
    across_x = [(i, i ^ 2) for i in range(n_lon)]
    across_x_core = [(i, i ^ 3) for i in range(n_lon)]
    across_z = [(i, (i + (4 if i // 2 % 2 == 0 else -4)) % n_lon) for i in range(n_lon)]
    back_z = [(i, (i + (-4 if i // 2 % 2 == 0 else 4)) % n_lon) for i in range(n_lon)]
    across_y = [(i, i ^ 1) for i in range(2 * n_lon)]
    across_both = [(i, i ^ 3) for i in range(2 * n_lon)]

    lines = tap_lines(tap_weights, 3 * lon_dev)
    rows, slots = list_rows(place, lat_dev)
    scalars = rows, place, widths
    sizes = STAY + COME
    starts = [sum(sizes[:c]) for c in range(len(sizes))]
    done = {}

    def get(kind, i):
        if (kind, i) in done:
            return done[kind, i]

        def moved(operand, axes, pairs):
            first = [get(*g)[0] if g[0] in "ft" else get(*g) for g in WAITS.get((kind, i), ())]
            if first:
                operand = lax.optimization_barrier((operand, *first))[0]
            return lax.ppermute(operand, axes, pairs)

        if kind == "k":
            result = keep[i]
        elif kind == "l":
            result = (rows, lines)[i]
        elif kind == "c":
            result = moved(give[i], "lon", across_core)
        elif kind == "y":
            operand, pairs = ((straight, across_y), (cross, across_both))[i % 2]
            result = moved(operand[i // 2], ("lon", "lat"), pairs)
        elif kind == "x":
            result = moved(get(*PARTS[i]), "lon", across_x)
        elif kind == "z":
            result = moved(get("x", i), "lon", across_z)
        elif kind == "p":
            operand, pairs = ((keep[1], across_x), (give[1], across_x_core))[i]
            result = moved(operand, "lon", pairs)
        elif kind == "q":
            operand = get(*(("k", 0), ("c", 0), ("p", 0), ("p", 1))[i])
            result = moved(operand, "lon", back_z if i < 2 else across_z)
        elif kind == "t":
            here = [get("k", 0), get("c", 0)]
            beside = [get("p", 0), get("p", 1)]
            if i == 0:
                panels = here + beside + [get("q", 2), get("q", 3)]
            else:
                panels = beside + [get("q", 0), get("q", 1)] + here
            places = [[(p, row) for p in panels] for row in range(STAY[0])]
            result = filter_pair(scalars, lines, places, 0, lon_dev)
        elif kind == "b":
            operand, pairs = ((get("t", 0)[1], across_core), (get("t", 1)[0], across_x), (get("t", 1)[1], across_x_core))[i]
            result = moved(operand, "lon", pairs)
        elif kind == "f":
            places = []
            for row in FILTERS[i]:
                chunk, index = next((c, row - at) for c, at in enumerate(starts) if at <= row < at + sizes[c])
                if chunk < n_stay:
                    pair = ("k", chunk), ("c", chunk)
                else:
                    pair = ("y", 2 * (chunk - n_stay)), ("y", 2 * (chunk - n_stay) + 1)
                parts = [get(*p) for p in pair]
                parts += [get(axis, PARTS.index(p)) for axis in "xz" for p in pair]
                places.append([(p, index) for p in parts])
            base = FILTERS[i][0]
            if i < len(FILTERS) - 1:
                result = filter_pair(scalars, lines, places, base, lon_dev)
            else:
                early = filter_pair(scalars, lines, [p[:4] for p in places], base, lon_dev, "early")
                result = filter_pair(scalars, lines, [p[4:] for p in places], base, lon_dev, "late", early)
        else:
            result = moved(get("f", i)[1], "lon", across_core)
        done[kind, i] = result
        return result

    mine = [get("t", 0)[0], get("b", 1)] + [get("f", i)[0] for i in range(len(FILTERS))]
    theirs = [get("b", 0), get("b", 2)] + [get("o", i) for i in range(len(FILTERS))]
    out = put_rows(mine + theirs, slots, lon_dev, lat_dev)
    return jnp.transpose(out, (1, 0, 2))


def filter_kernel(reach, rows_ref, slots_ref, sector_ref, widths_ref, line_ref, *refs):
    ins, out_ref = refs[:-1], refs[-1]
    lon_dev, channels = out_ref.shape[1:]
    row = rows_ref[pl.program_id(0)]
    line = active_line(line_ref, row, widths_ref[row], (reach + 1) * lon_dev)
    total = ins[0][0].astype(jnp.float32)
    for group, ref in enumerate(ins):
        block = toeplitz(line, (sector_ref[group] + 1) * lon_dev, lon_dev, lon_dev)
        total += jnp.dot(block, ref[0], preferred_element_type=jnp.float32)[:lon_dev]
    out_ref[0] = total.astype(out_ref.dtype)


def filter_rows(rows, slots, sectors, widths, lines, arrays, reach):
    lat_dev, lon_dev, channels = arrays[0].shape
    row_spec = pl.BlockSpec((1, lon_dev, channels), lambda i, rows, slots, sectors, widths: (i, 0, 0))
    line_spec = pl.BlockSpec(lines.shape, lambda i, rows, slots, sectors, widths: (0, 0))
    out_spec = pl.BlockSpec((1, lon_dev, channels), lambda i, rows, slots, sectors, widths: (slots[i], 0, 0))
    return pl.pallas_call(
        functools.partial(filter_kernel, reach),
        out_shape=jax.ShapeDtypeStruct(arrays[0].shape, arrays[0].dtype),
        grid_spec=pltpu.PrefetchScalarGridSpec(
            num_scalar_prefetch=4,
            grid=(lat_dev,),
            in_specs=[line_spec] + [row_spec] * len(arrays),
            out_specs=out_spec,
        ),
        compiler_params=pltpu.CompilerParams(vmem_limit_bytes=VMEM_LIMIT),
        name="filter_rows",
    )(rows, slots, sectors, widths, lines, *arrays)


def any_mesh(fields, owner_slot, widths, tap_weights):
    lat_dev, lon_dev, channels = fields.shape
    n_lon = lax.axis_size("lon")
    n_lat = lax.axis_size("lat")
    reach = n_lon // 8
    band = lax.axis_index("lat")
    dest_band = owner_slot // lat_dev
    home_rows = band * lat_dev + jnp.arange(lat_dev, dtype=jnp.int32)
    ordering = jnp.argsort(dest_band[home_rows], stable=True)
    rows = jnp.argsort((dest_band != band).astype(jnp.int32), stable=True)[:lat_dev].astype(jnp.int32)
    slots = (owner_slot[rows] % lat_dev).astype(jnp.int32)
    outgoing = fields[ordering].reshape(n_lat, lat_dev // n_lat, lon_dev, channels)
    incoming = lax.all_to_all(outgoing, "lat", split_axis=0, concat_axis=0, tiled=True)
    own = incoming.reshape(lat_dev, lon_dev, channels)
    lines = tap_lines(tap_weights, (reach + 1) * lon_dev)
    arrays, order = [own], [reach]
    ahead = behind = own
    for step in range(1, reach + 1):
        ahead = shift_by(ahead, "lon", -1)
        behind = shift_by(behind, "lon", 1)
        arrays += [ahead, behind]
        order += [reach + step, reach - step]
    sectors = jnp.array(order, jnp.int32)
    return filter_rows(rows, slots, sectors, widths, lines, arrays, reach)


def solution(mesh):
    in_specs = (P("lat", "lon", None), P(), P(), P())
    out_specs = P("lat", "lon", None)
    chips = (mesh.shape["lon"], mesh.shape["lat"]) == (16, 2)

    def body(fields, owner_slot, widths, tap_weights):
        fits = chips and fields.shape[0] == 4 * sum(STAY)
        form = chip_aware if fits else any_mesh
        return form(fields, owner_slot, widths, tap_weights)

    return jax.shard_map(body, mesh=mesh, in_specs=in_specs, out_specs=out_specs, check_vma=False)
```
